32 devices in a mesh: real: 2 (over y), comp: 4 (over z), space: 4 (over x, core).
Axes of the slice: x: 2, y: 2, z: 4, core: 2. Of those that a mesh axis runs over, the one named last changes fastest.
Arguments:
- concentration: float32 [256, 32, 2048], P(('real', 'comp'), None, 'space'), parts along dimension 0, may hold values from -12 to 12
- face_rate: float32 [2, 64, 2048], P(None, 'real', 'space'), parts along dimension 1, may hold values from 0.02 to 0.15
- face_flag: int32 [2, 64, 2048], P(None, 'real', 'space'), parts along dimension 1, may hold values from 0 to 1
- retardation: float32 [16], replicated, may hold values from 1 to 3
- dispersion: float32 [16], replicated, may hold values from 0.01 to 0.08
- mixing: float32 [16, 16], replicated, may hold values from -0.08 to 2.5
- mixing_inverse: float32 [16, 16], replicated, may hold values from -0.05 to 0.5
- affinity: float32 [16], replicated, may hold values from 0.5 to 3
- mineral: float32 [16], replicated, may hold values from 0.3 to 1.5
- stiff_mask: int32 [8, 64, 2048], P(None, ('real', 'comp'), 'space'), parts along dimension 1, may hold values from 0 to 1, as said below
Outputs:
- concentration_out: float32 [256, 32, 2048], P(('real', 'comp'), None, 'space'), parts along dimension 0
The draws below stay inside these ranges and needn't reach their ends.
There are 2 independent parts, one for each index of `real`. The reference program is written for one: setup_inputs(seed, part) draws one part's arguments, and reference() takes and returns one part's arrays. A program takes and returns all parts, laid end to end along the dimension named above; an argument that names none is the same for every part. Nothing has to cross between parts.
Inputs may be any that keep to these rules, and one draw needn't show every extreme that they name: `stiff_mask`: in every block of cells made of all 8 layers, x rows k * 8 to (k + 1) * 8 - 1 and y columns l * 512 to (l + 1) * 512 - 1, at most 8192 cells are stiff, and some block has exactly 8192.
All inputs are finite; a program needn't handle non-finite values.
Results may differ from the reference program's by a relative error of at most 0.00011.
Values sent between devices are 32-bit elements; how exact they have to be, the bound alone decides.
No kernel may reach another device: no remote copies, remote signals or barrier semaphores. Data moves between devices by JAX's collectives and lax.ppermute only.
A program may use at most 64 MiB of HBM per device.

```python
import math
import jax
import jax.numpy as jnp
from jax import lax

NC = 16
NZ = 8
NY = 2048
XR = 8
STEPS = 2
NEWT = 4
STIFF = 4
NX = 32
NYD = 512
PLANES = 128
CELLS_DEV = 32768
CAP = 8192


def mixing_pair(key):
    folded = jax.random.fold_in(key, 17)
    key_off, key_diag = jax.random.split(folded)
    off_diagonal = jax.random.uniform(key_off, (NC, NC), jnp.float32, -0.08, 0.08) * (1.0 - jnp.eye(NC, dtype=jnp.float32))
    diagonal = jax.random.uniform(key_diag, (NC,), jnp.float32, 1.5, 2.5)
    return off_diagonal + jnp.diag(diagonal)


def draw_mixing(key, part):
    return mixing_pair(key)


def draw_mixing_inverse(key, part):
    return jnp.linalg.inv(mixing_pair(key) + 3.0 * jnp.eye(NC, dtype=jnp.float32))


def draw_stiff_mask(key, part):
    row_blocks = NX // XR
    column_blocks = NY // NYD
    block_count = row_blocks * column_blocks
    key_heavy, key_light, key_chosen, key_ranks = jax.random.split(key, 4)
    heavy_flag = jax.random.randint(key_heavy, (block_count,), 0, 4) == 0
    light_counts = jax.random.randint(key_light, (block_count,), CAP // 8, CAP // 3 + 1)
    counts = jnp.where(heavy_flag, CAP, light_counts)
    chosen = jax.random.randint(key_chosen, (), 0, block_count)
    counts = jnp.where(jnp.arange(block_count) == chosen, CAP, counts)
    block_keys = jax.random.split(key_ranks, block_count)
    ranking = jax.vmap(lambda subkey: jax.random.permutation(subkey, CELLS_DEV))(block_keys)
    marked = (ranking < counts[:, None]).astype(jnp.int32)
    marked = marked.reshape(row_blocks, column_blocks, NZ, XR, NYD).transpose(2, 0, 3, 1, 4)
    return marked.reshape(NZ, NX, NY)


def touch_ends(drawn, key, least, high):
    shape = drawn.shape
    index_at = [jax.random.randint(jax.random.fold_in(key, axis), (), 0, shape[axis]) for axis in range(len(shape))]
    drawn = drawn.at[tuple(index_at)].set(least)
    longest = shape.index(max(shape))
    index_at[longest] = (index_at[longest] + 1) % shape[longest]
    return drawn.at[tuple(index_at)].set(high)


def shard_levels(own_key, shape, shards, least, high):
    factor_of, own = 1.0, jax.random.fold_in(own_key, 6)
    for position, parts in shards:
        steps = jnp.exp(jax.random.uniform(jax.random.fold_in(own, position), (parts,), jnp.float32, least / len(shards), high / len(shards)))
        factor_of = factor_of * jnp.repeat(steps, shape[position] // parts).reshape([-1 if axis == position else 1 for axis in range(len(shape))])
    return factor_of


def noise(key, extent, deviation, reach, cuts=(), kind=jnp.bfloat16):
    drawn = deviation * jax.random.normal(key, extent, jnp.float32)
    if cuts:
        drawn = drawn * shard_levels(key, extent, cuts, -0.22, 0.18)
    return jnp.clip(drawn, -reach, reach).astype(kind)


def setup_inputs(seed: int = 0, part: int = 0) -> dict:
    seeds = jax.random.split(jax.random.key(seed), 11)
    part_keys = jax.random.split(jax.random.fold_in(seeds[10], part), 11)
    return {
        "concentration": noise(part_keys[0], (PLANES, NX, NY), 2.0, 12.0, ((0, 4), (2, 4)), jnp.float32),
        "face_rate": jnp.clip(jnp.exp(math.log(0.15) - 2.014903 * jax.random.uniform(part_keys[1], (2, NX, NY), jnp.float32) ** shard_levels(part_keys[1], (2, NX, NY), ((2, 4),), -0.2, 0.2)), 0.02, 0.15),
        "face_flag": touch_ends(jax.random.randint(part_keys[2], (2, NX, NY), 0, 2), jax.random.fold_in(part_keys[2], 1), 0, 1).astype(jnp.int32),
        "retardation": jnp.clip(jnp.exp(jax.random.uniform(seeds[3], (NC,), jnp.float32, math.log(1.0), math.log(3.0))), 1.0, 3.0),
        "dispersion": jnp.clip(jnp.exp(jax.random.uniform(seeds[4], (NC,), jnp.float32, math.log(0.01), math.log(0.08))), 0.01, 0.08),
        "mixing": draw_mixing(jax.random.fold_in(seeds[10], 71), part),
        "mixing_inverse": draw_mixing_inverse(jax.random.fold_in(seeds[10], 71), part),
        "affinity": jnp.clip(jnp.exp(jax.random.uniform(seeds[7], (NC,), jnp.float32, math.log(0.5), math.log(3.0))), 0.5, 3.0),
        "mineral": jnp.clip(jnp.exp(jax.random.uniform(seeds[8], (NC,), jnp.float32, math.log(0.3), math.log(1.5))), 0.3, 1.5),
        "stiff_mask": draw_stiff_mask(jax.random.fold_in(jax.random.fold_in(seeds[10], part), 71), part),
    }


highest = lax.Precision.HIGHEST

def shift_down(values, axis_index):
    size_along = values.shape[axis_index]
    zero_row = jnp.zeros_like(lax.slice_in_dim(values, 0, 1, axis=axis_index))
    kept = lax.slice_in_dim(values, 0, size_along - 1, axis=axis_index)
    return jnp.concatenate([zero_row, kept], axis=axis_index)

def shift_up(values, axis_index):
    size_along = values.shape[axis_index]
    zero_row = jnp.zeros_like(lax.slice_in_dim(values, 0, 1, axis=axis_index))
    kept = lax.slice_in_dim(values, 1, size_along, axis=axis_index)
    return jnp.concatenate([kept, zero_row], axis=axis_index)

def face_weights(face_rate, face_flag):
    flag_values = face_flag.astype(jnp.float32)
    weight_plus = face_rate * flag_values
    weight_minus = face_rate * (1.0 - flag_values)
    return (weight_plus, weight_minus)

def advance(values, lower_row, upper_row, lower_col, upper_col, coefficients, retard_planes, spread_planes):
    divergence = coefficients[0] * lower_row + coefficients[1] * upper_row + coefficients[2] * lower_col + coefficients[3] * upper_col - coefficients[4] * values
    laplace = lower_row + upper_row + lower_col + upper_col - 4.0 * values
    return values + (divergence + spread_planes * laplace) / retard_planes

def residual_of(species, target, mixing, affinity, mineral, stiff):
    total = jnp.dot(mixing.astype(jnp.float32), species.astype(jnp.float32), precision=highest, preferred_element_type=jnp.float32) + affinity[:, None] * jnp.tanh(species)
    if stiff:
        total = total + mineral[:, None] * jnp.tanh(2.0 * species)
    return total - target

def newton_steps(species, target, repeats, stiff, mixing, mixing_inverse, affinity, mineral):
    for iteration in range(repeats):
        update = residual_of(species, target, mixing, affinity, mineral, stiff)
        species = species - jnp.dot(mixing_inverse.astype(jnp.float32), update.astype(jnp.float32), precision=highest, preferred_element_type=jnp.float32)
    return species

def reference(concentration, face_rate, face_flag, retardation, dispersion, mixing, mixing_inverse, affinity, mineral, stiff_mask):
    weight_plus, weight_minus = face_weights(face_rate, face_flag)
    down_plus = shift_down(weight_plus[0], 0)
    down_minus = shift_down(weight_minus[0], 0)
    side_plus = shift_down(weight_plus[1], 1)
    side_minus = shift_down(weight_minus[1], 1)
    centre = down_minus + weight_plus[0] + side_minus + weight_plus[1]
    coefficients = jnp.stack([down_plus, weight_minus[0], side_plus, weight_minus[1], centre])
    flat_mask = stiff_mask.reshape(-1) > 0

    def one_component(packed):
        component_planes, retard_value, spread_value = packed
        return advance(component_planes, shift_down(component_planes, 1), shift_up(component_planes, 1), shift_down(component_planes, 2), shift_up(component_planes, 2), coefficients, retard_value, spread_value)
    values = concentration
    for step_index in range(STEPS):
        layered = values.reshape(NC, NZ, NX, NY)
        layered = lax.map(one_component, (layered, retardation, dispersion))
        target = layered.reshape(NC, NZ * NX * NY)
        species = jnp.zeros_like(target)
        species = newton_steps(species, target, NEWT, False, mixing, mixing_inverse, affinity, mineral)
        stiffer = newton_steps(species, target, STIFF, True, mixing, mixing_inverse, affinity, mineral)
        species = jnp.where(flat_mask[None, :], stiffer, species)
        values = species.reshape(PLANES, NX, NY)
    return values
```

```python
import functools

import jax
import jax.numpy as jnp
from jax import lax
from jax.experimental import pallas as pl
from jax.experimental.pallas import tpu as pltpu
from jax.sharding import PartitionSpec as P

NC = 16
NZ = 8
STEPS = 2
NEWT = 4
STIFF = 4


highest = lax.Precision.HIGHEST


def shifted(shard, axis, by):
    devices = lax.axis_size(axis)
    pairs = [(i, i + by) for i in range(devices) if 0 <= i + by < devices]
    return lax.ppermute(shard, axis, pairs)


def extended(block, sides, width):
    for axis, dim in sides:
        count = lax.axis_size(axis)
        forward = [(i, i + 1) for i in range(count - 1)]
        backward = [(target, source) for source, target in forward]
        low = lax.ppermute(
            lax.slice_in_dim(block, block.shape[dim] - width, None, axis=dim), axis, forward
        )
        high = lax.ppermute(lax.slice_in_dim(block, 0, width, axis=dim), axis, backward)
        block = jnp.concatenate([low, block, high], axis=dim)
    return block


def shift_down(values, axis_index):
    size_along = values.shape[axis_index]
    zero_row = jnp.zeros_like(lax.slice_in_dim(values, 0, 1, axis=axis_index))
    kept = lax.slice_in_dim(values, 0, size_along - 1, axis=axis_index)
    return jnp.concatenate([zero_row, kept], axis=axis_index)


def face_weights(face_rate, face_flag):
    flag_values = face_flag.astype(jnp.float32)
    weight_plus = face_rate * flag_values
    weight_minus = face_rate * (1.0 - flag_values)
    return (weight_plus, weight_minus)


def advance(
    values, lower_row, upper_row, lower_col, upper_col, coefficients, retard_planes, spread_planes
):
    divergence = (
        coefficients[0] * lower_row
        + coefficients[1] * upper_row
        + coefficients[2] * lower_col
        + coefficients[3] * upper_col
        - coefficients[4] * values
    )
    laplace = lower_row + upper_row + lower_col + upper_col - 4.0 * values
    return values + (divergence + spread_planes * laplace) / retard_planes


def residual_of(species, target, mixing, affinity, mineral, stiff):
    total = jnp.dot(
        mixing, species, precision=highest, preferred_element_type=jnp.float32
    ) + affinity[:, None] * jnp.tanh(species)
    if stiff:
        total = total + mineral[:, None] * jnp.tanh(2.0 * species)
    return total - target


def newton_steps(species, target, repeats, stiff, mixing, mixing_inverse, affinity, mineral):
    for iteration in range(repeats):
        update = residual_of(species, target, mixing, affinity, mineral, stiff)
        species = species - jnp.dot(
            mixing_inverse, update, precision=highest, preferred_element_type=jnp.float32
        )
    return species


def speciate(cell_block, stiff_mask, mixing, mixing_inverse, affinity, mineral):
    target = cell_block.reshape(NC, -1)
    flat_mask = stiff_mask.reshape(-1) > 0
    species = jnp.zeros_like(target)
    species = newton_steps(species, target, NEWT, False, mixing, mixing_inverse, affinity, mineral)
    stiffer = newton_steps(species, target, STIFF, True, mixing, mixing_inverse, affinity, mineral)
    species = jnp.where(flat_mask[None, :], stiffer, species)
    return species.reshape(cell_block.shape)


def by_rows(
    concentration,
    face_rate,
    face_flag,
    retardation,
    dispersion,
    mixing,
    mixing_inverse,
    affinity,
    mineral,
    stiff_mask,
):
    weight_plus, weight_minus = face_weights(face_rate, face_flag)
    rim_weights = jnp.stack([weight_plus[1, :, -1], weight_minus[1, :, -1]])
    left_rims = shifted(rim_weights, "space", 1)
    side_plus = jnp.concatenate([left_rims[0][:, None], weight_plus[1, :, :-1]], axis=1)
    side_minus = jnp.concatenate([left_rims[1][:, None], weight_minus[1, :, :-1]], axis=1)
    down_plus = shift_down(weight_plus[0], 0)
    down_minus = shift_down(weight_minus[0], 0)
    centre = down_minus + weight_plus[0] + side_minus + weight_plus[1]
    coefficients = jnp.stack([down_plus, weight_minus[0], side_plus, weight_minus[1], centre])
    retard_all = jnp.repeat(retardation, NZ)
    spread_all = jnp.repeat(dispersion, NZ)
    rows_held = stiff_mask.shape[1]
    row_start = lax.axis_index("comp") * rows_held
    cell_coefficients = lax.dynamic_slice_in_dim(coefficients, row_start, rows_held, 1)
    retard_planes = retard_all[:, None, None]
    spread_planes = spread_all[:, None, None]
    cell_block = lax.all_to_all(concentration, "comp", split_axis=1, concat_axis=0, tiled=True)
    for step_index in range(STEPS):
        padded = extended(cell_block, (("comp", 1), ("space", 2)), 1)
        cell_block = advance(
            cell_block,
            padded[:, :-2, 1:-1],
            padded[:, 2:, 1:-1],
            padded[:, 1:-1, :-2],
            padded[:, 1:-1, 2:],
            cell_coefficients,
            retard_planes,
            spread_planes,
        )
        cell_block = speciate(cell_block, stiff_mask, mixing, mixing_inverse, affinity, mineral)
    return lax.all_to_all(cell_block, "comp", split_axis=0, concat_axis=1, tiled=True)


TILE = 8
LANES = 128


def step_kernel(
    held,
    layer,
    with_rim,
    place_ref,
    scale_ref,
    *refs,
):
    pieces = len(held)
    value_refs, refs = refs[:pieces], refs[pieces:]
    (low_ref, high_ref, rate_ref, flag_ref, stiff_ref, ratio_ref, first_ref, both_ref), refs = (
        refs[:8],
        refs[8:],
    )
    out_refs, refs = refs[:pieces], refs[pieces:]
    if with_rim:
        rim_ref, refs = refs[0], refs[1:]
    offset_ref, species_ref, plain_ref, first_split, both_split = refs
    groups, stacked, cols = species_ref.shape
    rows = groups * TILE
    components = stacked // TILE
    row_at = lax.broadcasted_iota(jnp.int32, (rows, cols), 0)
    col_at = lax.broadcasted_iota(jnp.int32, (rows, cols), 1)

    def split(value):
        high = value.astype(jnp.bfloat16)
        return high, (value - high.astype(jnp.float32)).astype(jnp.bfloat16)

    for source, target in ((first_ref, first_split), (both_ref, both_split)):
        high, low = split(source[...])
        target[...] = jnp.concatenate([high, low, high], axis=1)

    def product(weights, parts):
        highs, lows = zip(*[split(part) for part in parts])
        operand = jnp.concatenate(highs + highs + lows, axis=0)
        return jnp.dot(weights[...], operand, preferred_element_type=jnp.float32)

    weight_plus, weight_minus = face_weights(rate_ref[...], flag_ref[...])
    low_side, high_side = low_ref[...], high_ref[...]

    def column(side, at):
        return jnp.broadcast_to(side[:, at : at + 1], (rows, cols))

    def from_lower_row(value):
        return jnp.where(row_at == 0, 0.0, pltpu.roll(value, 1, 0))

    def from_upper_row(value):
        return jnp.where(row_at == rows - 1, 0.0, pltpu.roll(value, rows - 1, 0))

    def from_lower_col(value, edge):
        return jnp.where(col_at == 0, edge, pltpu.roll(value, 1, 1))

    def from_upper_col(value, edge):
        return jnp.where(col_at == cols - 1, edge, pltpu.roll(value, cols - 1, 1))

    rim_at = 2 * components
    down_plus = from_lower_row(weight_plus[0])
    down_minus = from_lower_row(weight_minus[0])
    side_plus = from_lower_col(weight_plus[1], column(low_side, rim_at))
    side_minus = from_lower_col(weight_minus[1], column(low_side, rim_at + 1))
    centre = down_minus + weight_plus[0] + side_minus + weight_plus[1]
    at = 0
    for value_ref, count in zip(value_refs, held):
        for index in range(count):
            value = value_ref[index]
            spread, retard = scale_ref[0, at], scale_ref[1, at]
            change = (
                (down_plus + spread) * from_lower_row(value)
                + (weight_minus[0] + spread) * from_upper_row(value)
                + (side_plus + spread) * from_lower_col(value, column(low_side, components + at))
                + (weight_minus[1] + spread) * from_upper_col(value, column(high_side, at))
                - (centre + 4.0 * spread) * value
            )
            value = value + change * retard
            for group in range(groups):
                offset_ref[group, at * TILE : (at + 1) * TILE, :] = value[
                    group * TILE : (group + 1) * TILE
                ]
            at += 1

    for group in range(groups):
        offset = product(first_split, [offset_ref[group]])
        offset_ref[group] = offset
        species_ref[group] = offset

    def plain_step(_, carry):
        for group in range(groups):
            species = species_ref[group]
            species_ref[group] = offset_ref[group] + product(
                both_split, [species, jnp.tanh(species)]
            )
        return carry

    lax.fori_loop(0, NEWT - 1, plain_step, 0)
    plain_ref[...] = species_ref[...]
    ratio = jnp.concatenate([ratio_ref[...]] * (cols // LANES), axis=1)

    def stiff_step(_, carry):
        for group in range(groups):
            species = species_ref[group]
            reaction = jnp.tanh(species) + ratio * jnp.tanh(species + species)
            species_ref[group] = offset_ref[group] + product(both_split, [species, reaction])
        return carry

    lax.fori_loop(0, STIFF, stiff_step, 0)
    ranks, block = stiff_ref.shape[0], rows // stiff_ref.shape[0]
    for group in range(groups):
        rank = lax.rem(place_ref[0] + ranks - (group * TILE) // block, ranks)
        inside = (group * TILE) % block
        stiff = stiff_ref[rank, layer, inside : inside + TILE, :] > 0.0
        at = 0
        for out_ref, count in zip(out_refs, held):
            for index in range(count):
                spot = slice(at * TILE, (at + 1) * TILE)
                out_ref[index, group * TILE : (group + 1) * TILE, :] = jnp.where(
                    stiff, species_ref[group, spot, :], plain_ref[group, spot, :]
                )
                at += 1
    if with_rim:
        lane_at = lax.broadcasted_iota(jnp.int32, (rows, LANES), 1)
        edges = [out_ref[i] for out_ref, count in zip(out_refs, held) for i in range(count)]
        columns = [value[:, :1] for value in edges] + [value[:, cols - 1 :] for value in edges]
        columns += [weight_plus[1][:, cols - 1 :], weight_minus[1][:, cols - 1 :]]
        rim = jnp.zeros((rows, LANES), jnp.float32)
        for lane, edge in enumerate(columns):
            rim = jnp.where(lane_at == lane, jnp.broadcast_to(edge, (rows, LANES)), rim)
        rim_ref[...] = rim


def layer_step(values, low, high, shared, layer, with_rim):
    place, scales, face_rate, face_flag, stiff, ratio, first, both = shared
    held = [value.shape[0] for value in values]
    components = sum(held)
    rows, cols = values[0].shape[1:]
    groups = rows // TILE
    stacked = components * TILE
    whole = pl.BlockSpec(memory_space=pltpu.VMEM)
    scalar = pl.BlockSpec(memory_space=pltpu.SMEM)
    out_shape = [jax.ShapeDtypeStruct(value.shape, jnp.float32) for value in values]
    if with_rim:
        out_shape.append(jax.ShapeDtypeStruct((rows, LANES), jnp.float32))
    field = pltpu.VMEM((groups, stacked, cols), jnp.float32)
    cells = rows * cols
    operands = [place, scales, *values, low, high, face_rate, face_flag, stiff, ratio, first, both]
    results = pl.pallas_call(
        functools.partial(step_kernel, held, layer, with_rim),
        out_shape=out_shape,
        in_specs=[scalar, scalar] + [whole] * (len(operands) - 2),
        out_specs=[whole] * len(out_shape),
        scratch_shapes=[
            field,
            field,
            field,
            pltpu.VMEM((stacked, 3 * stacked), jnp.bfloat16),
            pltpu.VMEM((stacked, 6 * stacked), jnp.bfloat16),
        ],
        compiler_params=pltpu.CompilerParams(vmem_limit_bytes=24 * 1024 * 1024),
        cost_estimate=pl.CostEstimate(
            flops=2 * (NEWT + STIFF) * 6 * stacked * components * cells,
            bytes_accessed=8 * components * cells,
            transcendentals=(NEWT + 2 * STIFF) * components * cells,
        ),
        name="layer_step",
    )(*operands)
    return (results[:-1], results[-1]) if with_rim else (results, None)


def by_layers(
    concentration,
    face_rate,
    face_flag,
    retardation,
    dispersion,
    mixing,
    mixing_inverse,
    affinity,
    mineral,
    stiff_mask,
):
    ranks = lax.axis_size("comp")
    me = lax.axis_index("comp")
    planes, rows, cols = concentration.shape
    held = planes // NZ
    layers = NZ // ranks
    block = stiff_mask.shape[1]
    own = concentration.reshape(held, ranks, layers, rows, cols)

    def send(value, by):
        return lax.ppermute(value, "comp", [(i, (i + by) % ranks) for i in range(ranks)])

    arrived = []
    for layer in range(layers):
        values = []
        for q in range(ranks):
            piece = lax.dynamic_slice(
                own, (0, (me + q) % ranks, layer, 0, 0), (held, 1, 1, rows, cols)
            ).reshape(held, rows, cols)
            if layer > 0 and q > 0:
                piece, arrived[layer - 1][q] = lax.optimization_barrier(
                    (piece, arrived[layer - 1][q])
                )
            values.append(send(piece, q) if q else piece)
        arrived.append(values)

    rim_rate = face_rate[1, :, -1]
    rim_flag = face_flag[1, :, -1]
    rim = jnp.stack(face_weights(rim_rate, rim_flag))
    from_low = shifted(jnp.concatenate([concentration[:, :, -1], rim]), "space", 1)
    from_high = shifted(concentration[:, :, 0], "space", -1)
    sides = jnp.stack([from_high, from_low[:planes]]).reshape(2, held, ranks, layers, rows)
    sides = sides.transpose(2, 3, 0, 1, 4).reshape(ranks, layers, -1)
    edge_rows = -(-sides.shape[-1] // cols)
    sides = jnp.pad(sides, ((0, 0), (0, 0), (0, edge_rows * cols - sides.shape[-1])))
    sides = sides.reshape(ranks, layers, edge_rows, cols)
    marks = stiff_mask.astype(jnp.float32).reshape(ranks, layers, block, cols)
    small = jnp.concatenate([marks, sides], axis=2)
    small = [
        lax.dynamic_index_in_dim(small, (me + q) % ranks, 0, keepdims=False) for q in range(ranks)
    ]
    small = jnp.stack([send(piece, q) if q else piece for q, piece in enumerate(small)])
    sides = small[:, :, block:].reshape(ranks, layers, -1)[:, :, : 2 * held * rows]
    sides = sides.reshape(ranks, layers, 2, held, rows).transpose(1, 2, 0, 3, 4)
    sides = sides.reshape(layers, 2 * ranks * held, rows)
    rims = jnp.broadcast_to(from_low[planes:], (layers, 2, rows))
    sides = jnp.concatenate([sides, rims], axis=1)
    sides = jnp.pad(sides, ((0, 0), (0, LANES - sides.shape[1]), (0, 0))).transpose(0, 2, 1)

    order = ((me - jnp.arange(ranks)) % ranks)[:, None] * held + jnp.arange(held)
    order = order.reshape(-1)
    inverse = mixing_inverse[order][:, order]
    amounts = affinity[order]
    blend = jnp.eye(NC, dtype=jnp.float32) - jnp.dot(
        inverse, mixing[order][:, order], precision=highest
    )
    tile = jnp.eye(TILE, dtype=jnp.float32)
    first = jnp.kron(inverse, tile)
    both = jnp.concatenate([jnp.kron(blend, tile), jnp.kron(-inverse * amounts, tile)], axis=1)
    ratio = jnp.repeat(mineral[order] / amounts, TILE)
    ratio = jnp.broadcast_to(ratio[:, None], (NC * TILE, LANES))
    scales = jnp.stack([dispersion[order], 1.0 / retardation[order]])
    place = me.astype(jnp.int32).reshape(1)
    shared = (place, scales, face_rate, face_flag, small, ratio, first, both)

    result = jnp.zeros((held, NZ, rows, cols), jnp.float32)
    for layer in range(layers):
        values, low, high = arrived[layer], sides[layer], sides[layer]
        for step in range(STEPS):
            values, rims = layer_step(values, low, high, shared, layer, step < STEPS - 1)
            if step < STEPS - 1:
                low, high = shifted(rims, "space", 1), shifted(rims, "space", -1)
        for q in range(ranks):
            piece = send(values[q], -q) if q else values[q]
            result = lax.dynamic_update_slice(
                result, piece[:, None], (0, (me + q) % ranks * layers + layer, 0, 0)
            )
    return result.reshape(planes, rows, cols)


def shards(concentration, face_rate, face_flag, *parameters):
    ranks = lax.axis_size("comp")
    planes, rows, cols = concentration.shape
    whole = NZ % ranks == 0 and planes % NZ == 0 and 2 * NC + 2 <= LANES
    even = rows % (ranks * TILE) == 0 and cols % LANES == 0
    plan = by_layers if whole and even else by_rows
    return plan(concentration, face_rate, face_flag, *parameters)


def solution(mesh):
    in_specs = (
        P(("real", "comp"), None, "space"),
        P(None, "real", "space"),
        P(None, "real", "space"),
        P(),
        P(),
        P(),
        P(),
        P(),
        P(),
        P(None, ("real", "comp"), "space"),
    )
    out_specs = P(("real", "comp"), None, "space")
    return jax.shard_map(shards, mesh=mesh, in_specs=in_specs, out_specs=out_specs, check_vma=False)
```

```python
import functools

import jax
import jax.numpy as jnp
from jax import lax
from jax.experimental import pallas as pl
from jax.experimental.pallas import tpu as pltpu
from jax.sharding import PartitionSpec as P

NC = 16
NZ = 8
STEPS = 2
NEWT = 4
STIFF = 4


highest = lax.Precision.HIGHEST


def shifted(shard, axis, by):
    devices = lax.axis_size(axis)
    pairs = [(i, i + by) for i in range(devices) if 0 <= i + by < devices]
    return lax.ppermute(shard, axis, pairs)


def extended(block, sides, width):
    for axis, dim in sides:
        count = lax.axis_size(axis)
        forward = [(i, i + 1) for i in range(count - 1)]
        backward = [(target, source) for source, target in forward]
        low = lax.ppermute(
            lax.slice_in_dim(block, block.shape[dim] - width, None, axis=dim), axis, forward
        )
        high = lax.ppermute(lax.slice_in_dim(block, 0, width, axis=dim), axis, backward)
        block = jnp.concatenate([low, block, high], axis=dim)
    return block


def shift_down(values, axis_index):
    size_along = values.shape[axis_index]
    zero_row = jnp.zeros_like(lax.slice_in_dim(values, 0, 1, axis=axis_index))
    kept = lax.slice_in_dim(values, 0, size_along - 1, axis=axis_index)
    return jnp.concatenate([zero_row, kept], axis=axis_index)


def face_weights(face_rate, face_flag):
    flag_values = face_flag.astype(jnp.float32)
    weight_plus = face_rate * flag_values
    weight_minus = face_rate * (1.0 - flag_values)
    return (weight_plus, weight_minus)


def advance(
    values, lower_row, upper_row, lower_col, upper_col, coefficients, retard_planes, spread_planes
):
    divergence = (
        coefficients[0] * lower_row
        + coefficients[1] * upper_row
        + coefficients[2] * lower_col
        + coefficients[3] * upper_col
        - coefficients[4] * values
    )
    laplace = lower_row + upper_row + lower_col + upper_col - 4.0 * values
    return values + (divergence + spread_planes * laplace) / retard_planes


def residual_of(species, target, mixing, affinity, mineral, stiff):
    total = jnp.dot(
        mixing, species, precision=highest, preferred_element_type=jnp.float32
    ) + affinity[:, None] * jnp.tanh(species)
    if stiff:
        total = total + mineral[:, None] * jnp.tanh(2.0 * species)
    return total - target


def newton_steps(species, target, repeats, stiff, mixing, mixing_inverse, affinity, mineral):
    for iteration in range(repeats):
        update = residual_of(species, target, mixing, affinity, mineral, stiff)
        species = species - jnp.dot(
            mixing_inverse, update, precision=highest, preferred_element_type=jnp.float32
        )
    return species


def speciate(cell_block, stiff_mask, mixing, mixing_inverse, affinity, mineral):
    target = cell_block.reshape(NC, -1)
    flat_mask = stiff_mask.reshape(-1) > 0
    species = jnp.zeros_like(target)
    species = newton_steps(species, target, NEWT, False, mixing, mixing_inverse, affinity, mineral)
    stiffer = newton_steps(species, target, STIFF, True, mixing, mixing_inverse, affinity, mineral)
    species = jnp.where(flat_mask[None, :], stiffer, species)
    return species.reshape(cell_block.shape)


def by_rows(
    concentration,
    face_rate,
    face_flag,
    retardation,
    dispersion,
    mixing,
    mixing_inverse,
    affinity,
    mineral,
    stiff_mask,
):
    weight_plus, weight_minus = face_weights(face_rate, face_flag)
    rim_weights = jnp.stack([weight_plus[1, :, -1], weight_minus[1, :, -1]])
    left_rims = shifted(rim_weights, "space", 1)
    side_plus = jnp.concatenate([left_rims[0][:, None], weight_plus[1, :, :-1]], axis=1)
    side_minus = jnp.concatenate([left_rims[1][:, None], weight_minus[1, :, :-1]], axis=1)
    down_plus = shift_down(weight_plus[0], 0)
    down_minus = shift_down(weight_minus[0], 0)
    centre = down_minus + weight_plus[0] + side_minus + weight_plus[1]
    coefficients = jnp.stack([down_plus, weight_minus[0], side_plus, weight_minus[1], centre])
    retard_all = jnp.repeat(retardation, NZ)
    spread_all = jnp.repeat(dispersion, NZ)
    rows_held = stiff_mask.shape[1]
    row_start = lax.axis_index("comp") * rows_held
    cell_coefficients = lax.dynamic_slice_in_dim(coefficients, row_start, rows_held, 1)
    retard_planes = retard_all[:, None, None]
    spread_planes = spread_all[:, None, None]
    cell_block = lax.all_to_all(concentration, "comp", split_axis=1, concat_axis=0, tiled=True)
    for step_index in range(STEPS):
        padded = extended(cell_block, (("comp", 1), ("space", 2)), 1)
        cell_block = advance(
            cell_block,
            padded[:, :-2, 1:-1],
            padded[:, 2:, 1:-1],
            padded[:, 1:-1, :-2],
            padded[:, 1:-1, 2:],
            cell_coefficients,
            retard_planes,
            spread_planes,
        )
        cell_block = speciate(cell_block, stiff_mask, mixing, mixing_inverse, affinity, mineral)
    return lax.all_to_all(cell_block, "comp", split_axis=0, concat_axis=1, tiled=True)


TILE = 8
LANES = 128


def step_kernel(pieces, is_first, with_rim, place_ref, scale_ref, *refs):
    value_refs, refs = refs[:pieces], refs[pieces:]
    (low_ref, high_ref, rate_ref, flag_ref, ratio_ref, first_ref, both_ref), refs = (
        refs[:7],
        refs[7:],
    )
    if not is_first:
        stiff_ref, refs = refs[0], refs[1:]
    out_refs, refs = refs[:pieces], refs[pieces:]
    if with_rim:
        rim_ref, refs = refs[0], refs[1:]
    if is_first:
        stiff_ref, refs = refs[0], refs[1:]
    offset_ref, species_ref, plain_ref, first_split, both_split = refs
    groups, stacked, cols = species_ref.shape
    rows = groups * TILE
    components = stacked // TILE
    held = components // pieces
    row_at = lax.broadcasted_iota(jnp.int32, (rows, cols), 0)
    col_at = lax.broadcasted_iota(jnp.int32, (rows, cols), 1)

    def split(value):
        high = value.astype(jnp.bfloat16)
        return high, (value - high.astype(jnp.float32)).astype(jnp.bfloat16)

    for source, target in ((first_ref, first_split), (both_ref, both_split)):
        high, low = split(source[...])
        target[...] = jnp.concatenate([high, low, high], axis=1)

    def product(weights, parts):
        highs, lows = zip(*[split(part) for part in parts])
        operand = jnp.concatenate(highs + highs + lows, axis=0)
        return jnp.dot(weights[...], operand, preferred_element_type=jnp.float32)

    weight_plus, weight_minus = face_weights(rate_ref[...], flag_ref[...])
    low_side, high_side = low_ref[...], high_ref[...]

    def column(side, at):
        return jnp.broadcast_to(side[:, at : at + 1], (rows, cols))

    def from_lower_row(value):
        return jnp.where(row_at == 0, 0.0, pltpu.roll(value, 1, 0))

    def from_upper_row(value):
        return jnp.where(row_at == rows - 1, 0.0, pltpu.roll(value, rows - 1, 0))

    def from_lower_col(value, edge):
        return jnp.where(col_at == 0, edge, pltpu.roll(value, 1, 1))

    def from_upper_col(value, edge):
        return jnp.where(col_at == cols - 1, edge, pltpu.roll(value, cols - 1, 1))

    rim_at = 2 * components
    down_plus = from_lower_row(weight_plus[0])
    down_minus = from_lower_row(weight_minus[0])
    side_plus = from_lower_col(weight_plus[1], column(low_side, rim_at))
    side_minus = from_lower_col(weight_minus[1], column(low_side, rim_at + 1))
    centre = down_minus + weight_plus[0] + side_minus + weight_plus[1]
    at = 0
    for value_ref in value_refs:
        for index in range(held):
            value = value_ref[index * rows : (index + 1) * rows, :]
            spread, retard = scale_ref[0, at], scale_ref[1, at]
            change = (
                (down_plus + spread) * from_lower_row(value)
                + (weight_minus[0] + spread) * from_upper_row(value)
                + (side_plus + spread) * from_lower_col(value, column(low_side, components + at))
                + (weight_minus[1] + spread) * from_upper_col(value, column(high_side, at))
                - (centre + 4.0 * spread) * value
            )
            value = value + change * retard
            for group in range(groups):
                offset_ref[group, at * TILE : (at + 1) * TILE, :] = value[
                    group * TILE : (group + 1) * TILE
                ]
            at += 1

    for group in range(groups):
        offset = product(first_split, [offset_ref[group]])
        offset_ref[group] = offset
        species_ref[group] = offset

    def plain_step(_, carry):
        for group in range(groups):
            species = species_ref[group]
            species_ref[group] = offset_ref[group] + product(
                both_split, [species, jnp.tanh(species)]
            )
        return carry

    lax.fori_loop(0, NEWT - 1, plain_step, 0)
    plain_ref[...] = species_ref[...]
    ratio = jnp.concatenate([ratio_ref[...]] * (cols // LANES), axis=1)

    def stiff_step(_, carry):
        for group in range(groups):
            species = species_ref[group]
            reaction = jnp.tanh(species) + ratio * jnp.tanh(species + species)
            species_ref[group] = offset_ref[group] + product(both_split, [species, reaction])
        return carry

    lax.fori_loop(0, STIFF, stiff_step, 0)
    if is_first:
        block = rows // pieces
        for q, value_ref in enumerate(value_refs):
            rank = lax.rem(place_ref[0] + pieces - q, pieces)
            spot = pl.ds(pl.multiple_of(rank * block, TILE), block)
            stiff_ref[spot, :] = value_ref[held * rows :, :]
    for group in range(groups):
        spot = slice(group * TILE, (group + 1) * TILE)
        stiff = stiff_ref[spot, :] > 0.0
        for at in range(components):
            lane = slice(at * TILE, (at + 1) * TILE)
            start = at % held * rows + group * TILE
            out_refs[at // held][start : start + TILE, :] = jnp.where(
                stiff, species_ref[group, lane, :], plain_ref[group, lane, :]
            )
    if with_rim:
        lane_at = lax.broadcasted_iota(jnp.int32, (rows, LANES), 1)
        edges = [ref[i * rows : (i + 1) * rows, :] for ref in out_refs for i in range(held)]
        columns = [value[:, :1] for value in edges] + [value[:, cols - 1 :] for value in edges]
        columns += [weight_plus[1][:, cols - 1 :], weight_minus[1][:, cols - 1 :]]
        rim = jnp.zeros((rows, LANES), jnp.float32)
        for lane, edge in enumerate(columns):
            rim = jnp.where(lane_at == lane, jnp.broadcast_to(edge, (rows, LANES)), rim)
        rim_ref[...] = rim


def layer_step(values, stiff, low, high, shared, with_rim):
    place, scales, face_rate, face_flag, ratio, first, both = shared
    pieces = len(values)
    rows, cols = face_rate.shape[1:]
    groups = rows // TILE
    stacked = ratio.shape[0]
    components = stacked // TILE
    whole = pl.BlockSpec(memory_space=pltpu.VMEM)
    scalar = pl.BlockSpec(memory_space=pltpu.SMEM)
    plane = jax.ShapeDtypeStruct((components // pieces * rows, cols), jnp.float32)
    out_shape = [plane] * pieces
    if with_rim:
        out_shape.append(jax.ShapeDtypeStruct((rows, LANES), jnp.float32))
    if stiff is None:
        out_shape.append(jax.ShapeDtypeStruct((rows, cols), jnp.float32))
    field = pltpu.VMEM((groups, stacked, cols), jnp.float32)
    cells = rows * cols
    operands = [place, scales, *values, low, high, face_rate, face_flag, ratio, first, both]
    if stiff is not None:
        operands.append(stiff)
    results = pl.pallas_call(
        functools.partial(step_kernel, pieces, stiff is None, with_rim),
        out_shape=out_shape,
        in_specs=[scalar, scalar] + [whole] * (len(operands) - 2),
        out_specs=[whole] * len(out_shape),
        scratch_shapes=[
            field,
            field,
            field,
            pltpu.VMEM((stacked, 3 * stacked), jnp.bfloat16),
            pltpu.VMEM((stacked, 6 * stacked), jnp.bfloat16),
        ],
        compiler_params=pltpu.CompilerParams(vmem_limit_bytes=24 * 1024 * 1024),
        cost_estimate=pl.CostEstimate(
            flops=2 * (NEWT + STIFF) * 6 * stacked * components * cells,
            bytes_accessed=8 * components * cells,
            transcendentals=(NEWT + 2 * STIFF) * components * cells,
        ),
        name="layer_step",
    )(*operands)
    values, results = results[:pieces], results[pieces:]
    rims = results[0] if with_rim else None
    return values, (results[-1] if stiff is None else stiff), rims


def by_layers(
    concentration,
    face_rate,
    face_flag,
    retardation,
    dispersion,
    mixing,
    mixing_inverse,
    affinity,
    mineral,
    stiff_mask,
):
    ranks = lax.axis_size("comp")
    me = lax.axis_index("comp")
    planes, rows, cols = concentration.shape
    held = planes // NZ
    layers = NZ // ranks
    block = stiff_mask.shape[1]
    own = concentration.reshape(held, ranks, layers, rows, cols)
    marks = stiff_mask.astype(jnp.float32).reshape(ranks, layers, block, cols)

    def send(value, by):
        return lax.ppermute(value, "comp", [(i, (i + by) % ranks) for i in range(ranks)])

    messages, arrived = [], []
    for layer in range(layers):
        parts = []
        for q in range(ranks):
            target = (me + q) % ranks
            piece = lax.dynamic_slice(own, (0, target, layer, 0, 0), (held, 1, 1, rows, cols))
            mark = lax.dynamic_slice(marks, (target, layer, 0, 0), (1, 1, block, cols))
            part = jnp.concatenate([piece.reshape(-1, cols), mark.reshape(-1, cols)])
            if layer > 0 and q > 0:
                part, arrived[layer - 1][q] = lax.optimization_barrier(
                    (part, arrived[layer - 1][q])
                )
            parts.append(part)
        messages.append(parts)
        arrived.append([send(part, q) if q else part for q, part in enumerate(parts)])

    planes_after, messages[0] = lax.optimization_barrier((concentration, messages[0]))
    rim = jnp.stack(face_weights(face_rate[1, :, -1], face_flag[1, :, -1]))
    edges = jnp.concatenate([planes_after[:, :, 0], planes_after[:, :, -1], rim])
    edges = lax.all_gather(edges, ("comp", "space"))
    spaces = lax.axis_size("space")
    mine = lax.axis_index("space")
    edges = edges.reshape(ranks, spaces, 2 * planes + 2, rows)
    edges = jnp.pad(edges, ((0, 0), (1, 1), (0, 0), (0, 0)))
    below = lax.dynamic_index_in_dim(edges, mine, 1, keepdims=False)
    above = lax.dynamic_index_in_dim(edges, mine + 2, 1, keepdims=False)

    def sides_of(values):
        values = values.reshape(ranks, held, ranks, layers, rows)
        values = lax.dynamic_index_in_dim(values, me, 2, keepdims=False)
        return values[(me - jnp.arange(ranks)) % ranks].reshape(NC, layers, rows)

    sides = jnp.concatenate(
        [
            sides_of(above[:, :planes]),
            sides_of(below[:, planes : 2 * planes]),
            jnp.broadcast_to(below[0, 2 * planes :, None], (2, layers, rows)),
            jnp.zeros((LANES - 2 * NC - 2, layers, rows), jnp.float32),
        ]
    ).transpose(1, 2, 0)

    order = ((me - jnp.arange(ranks)) % ranks)[:, None] * held + jnp.arange(held)
    order = order.reshape(-1)
    inverse = mixing_inverse[order][:, order]
    amounts = affinity[order]
    blend = jnp.eye(NC, dtype=jnp.float32) - jnp.dot(
        inverse, mixing[order][:, order], precision=highest
    )
    tile = jnp.eye(TILE, dtype=jnp.float32)
    first = jnp.kron(inverse, tile)
    both = jnp.concatenate([jnp.kron(blend, tile), jnp.kron(-inverse * amounts, tile)], axis=1)
    ratio = jnp.repeat(mineral[order] / amounts, TILE)
    ratio = jnp.broadcast_to(ratio[:, None], (NC * TILE, LANES))
    scales = jnp.stack([dispersion[order], 1.0 / retardation[order]])
    place = me.astype(jnp.int32).reshape(1)
    shared = (place, scales, face_rate, face_flag, ratio, first, both)

    result = jnp.zeros((held, NZ, rows, cols), jnp.float32)
    for layer in range(layers):
        values, stiff, low, high = arrived[layer], None, sides[layer], sides[layer]
        for step in range(STEPS):
            values, stiff, rims = layer_step(values, stiff, low, high, shared, step < STEPS - 1)
            if step < STEPS - 1:
                low, high = shifted(rims, "space", 1), shifted(rims, "space", -1)
        for q in range(ranks):
            piece = send(values[q], -q) if q else values[q]
            result = lax.dynamic_update_slice(
                result, piece.reshape(held, 1, rows, cols), (0, (me + q) % ranks * layers + layer, 0, 0)
            )
    return result.reshape(planes, rows, cols)


def shards(concentration, face_rate, face_flag, *parameters):
    ranks = lax.axis_size("comp")
    planes, rows, cols = concentration.shape
    whole = NZ % ranks == 0 and planes % NZ == 0 and 2 * NC + 2 <= LANES
    even = rows % (ranks * TILE) == 0 and cols % LANES == 0
    plan = by_layers if whole and even else by_rows
    return plan(concentration, face_rate, face_flag, *parameters)


def solution(mesh):
    in_specs = (
        P(("real", "comp"), None, "space"),
        P(None, "real", "space"),
        P(None, "real", "space"),
        P(),
        P(),
        P(),
        P(),
        P(),
        P(),
        P(None, ("real", "comp"), "space"),
    )
    out_specs = P(("real", "comp"), None, "space")
    return jax.shard_map(shards, mesh=mesh, in_specs=in_specs, out_specs=out_specs, check_vma=False)
```

```python
import functools

import jax
import jax.numpy as jnp
from jax import lax
from jax.experimental import pallas as pl
from jax.experimental.pallas import tpu as pltpu
from jax.sharding import PartitionSpec as P

NC = 16
NZ = 8
STEPS = 2
NEWT = 4
STIFF = 4


highest = lax.Precision.HIGHEST


def shifted(shard, axis, by):
    devices = lax.axis_size(axis)
    pairs = [(i, i + by) for i in range(devices) if 0 <= i + by < devices]
    return lax.ppermute(shard, axis, pairs)


def extended(block, sides, width):
    for axis, dim in sides:
        count = lax.axis_size(axis)
        forward = [(i, i + 1) for i in range(count - 1)]
        backward = [(target, source) for source, target in forward]
        low = lax.ppermute(
            lax.slice_in_dim(block, block.shape[dim] - width, None, axis=dim), axis, forward
        )
        high = lax.ppermute(lax.slice_in_dim(block, 0, width, axis=dim), axis, backward)
        block = jnp.concatenate([low, block, high], axis=dim)
    return block


def shift_down(values, axis_index):
    size_along = values.shape[axis_index]
    zero_row = jnp.zeros_like(lax.slice_in_dim(values, 0, 1, axis=axis_index))
    kept = lax.slice_in_dim(values, 0, size_along - 1, axis=axis_index)
    return jnp.concatenate([zero_row, kept], axis=axis_index)


def face_weights(face_rate, face_flag):
    flag_values = face_flag.astype(jnp.float32)
    weight_plus = face_rate * flag_values
    weight_minus = face_rate * (1.0 - flag_values)
    return (weight_plus, weight_minus)


def advance(
    values, lower_row, upper_row, lower_col, upper_col, coefficients, retard_planes, spread_planes
):
    divergence = (
        coefficients[0] * lower_row
        + coefficients[1] * upper_row
        + coefficients[2] * lower_col
        + coefficients[3] * upper_col
        - coefficients[4] * values
    )
    laplace = lower_row + upper_row + lower_col + upper_col - 4.0 * values
    return values + (divergence + spread_planes * laplace) / retard_planes


def residual_of(species, target, mixing, affinity, mineral, stiff):
    total = jnp.dot(
        mixing, species, precision=highest, preferred_element_type=jnp.float32
    ) + affinity[:, None] * jnp.tanh(species)
    if stiff:
        total = total + mineral[:, None] * jnp.tanh(2.0 * species)
    return total - target


def newton_steps(species, target, repeats, stiff, mixing, mixing_inverse, affinity, mineral):
    for iteration in range(repeats):
        update = residual_of(species, target, mixing, affinity, mineral, stiff)
        species = species - jnp.dot(
            mixing_inverse, update, precision=highest, preferred_element_type=jnp.float32
        )
    return species


def speciate(cell_block, stiff_mask, mixing, mixing_inverse, affinity, mineral):
    target = cell_block.reshape(NC, -1)
    flat_mask = stiff_mask.reshape(-1) > 0
    species = jnp.zeros_like(target)
    species = newton_steps(species, target, NEWT, False, mixing, mixing_inverse, affinity, mineral)
    stiffer = newton_steps(species, target, STIFF, True, mixing, mixing_inverse, affinity, mineral)
    species = jnp.where(flat_mask[None, :], stiffer, species)
    return species.reshape(cell_block.shape)


def by_rows(
    concentration,
    face_rate,
    face_flag,
    retardation,
    dispersion,
    mixing,
    mixing_inverse,
    affinity,
    mineral,
    stiff_mask,
):
    weight_plus, weight_minus = face_weights(face_rate, face_flag)
    rim_weights = jnp.stack([weight_plus[1, :, -1], weight_minus[1, :, -1]])
    left_rims = shifted(rim_weights, "space", 1)
    side_plus = jnp.concatenate([left_rims[0][:, None], weight_plus[1, :, :-1]], axis=1)
    side_minus = jnp.concatenate([left_rims[1][:, None], weight_minus[1, :, :-1]], axis=1)
    down_plus = shift_down(weight_plus[0], 0)
    down_minus = shift_down(weight_minus[0], 0)
    centre = down_minus + weight_plus[0] + side_minus + weight_plus[1]
    coefficients = jnp.stack([down_plus, weight_minus[0], side_plus, weight_minus[1], centre])
    retard_all = jnp.repeat(retardation, NZ)
    spread_all = jnp.repeat(dispersion, NZ)
    rows_held = stiff_mask.shape[1]
    row_start = lax.axis_index("comp") * rows_held
    cell_coefficients = lax.dynamic_slice_in_dim(coefficients, row_start, rows_held, 1)
    retard_planes = retard_all[:, None, None]
    spread_planes = spread_all[:, None, None]
    cell_block = lax.all_to_all(concentration, "comp", split_axis=1, concat_axis=0, tiled=True)
    for step_index in range(STEPS):
        padded = extended(cell_block, (("comp", 1), ("space", 2)), 1)
        cell_block = advance(
            cell_block,
            padded[:, :-2, 1:-1],
            padded[:, 2:, 1:-1],
            padded[:, 1:-1, :-2],
            padded[:, 1:-1, 2:],
            cell_coefficients,
            retard_planes,
            spread_planes,
        )
        cell_block = speciate(cell_block, stiff_mask, mixing, mixing_inverse, affinity, mineral)
    return lax.all_to_all(cell_block, "comp", split_axis=0, concat_axis=1, tiled=True)


TILE = 8
LANES = 128
VMEM_LIMIT = 24 * 1024 * 1024


def whole_spec():
    return pl.BlockSpec(memory_space=pltpu.VMEM)


def any_spec():
    return pl.BlockSpec(memory_space=pl.ANY)


def split(value):
    high = value.astype(jnp.bfloat16)
    return high, (value - high.astype(jnp.float32)).astype(jnp.bfloat16)


def gather_columns(columns, rows):
    lane_at = lax.broadcasted_iota(jnp.int32, (rows, LANES), 1)
    gathered = jnp.zeros((rows, LANES), jnp.float32)
    for lane, column in enumerate(columns):
        gathered = jnp.where(lane_at == lane, jnp.broadcast_to(column, (rows, LANES)), gathered)
    return gathered


def pack_kernel(ranks, layer, with_edges, plane_ref, mask_ref, after_ref, *refs):
    if with_edges:
        (rate_ref, flag_ref), refs = refs[:2], refs[2:]
    out_refs, refs = refs[:ranks], refs[ranks:]
    if with_edges:
        (edge_ref,), refs = refs[:1], refs[1:]
    mark_ref, low_ref, high_ref, sems = refs
    planes, rows, cols = plane_ref.shape
    layers = mask_ref.shape[0] // ranks
    block = mask_ref.shape[1]
    held = planes // mask_ref.shape[0]
    me = lax.axis_index("comp")
    copies = []

    def start(source, target):
        copies.append(pltpu.make_async_copy(source, target, sems.at[len(copies)]))
        copies[-1].start()
        return copies[-1]

    if with_edges:
        low = start(plane_ref.at[:, :, pl.ds(0, LANES)], low_ref)
        high = start(plane_ref.at[:, :, pl.ds(cols - LANES, LANES)], high_ref)
    for q, out_ref in enumerate(out_refs):
        at = lax.rem(me + q, ranks) * layers + layer
        for index in range(held):
            start(
                plane_ref.at[index * mask_ref.shape[0] + at],
                out_ref.at[pl.ds(index * rows, rows)],
            )
    for q, out_ref in enumerate(out_refs):
        at = lax.rem(me + q, ranks) * layers + layer
        mark_ref[q] = mask_ref[at].astype(jnp.float32)
        start(mark_ref.at[q], out_ref.at[pl.ds(held * rows, block)])
    if with_edges:
        low.wait()
        high.wait()
        copies = copies[2:]
        last = pl.ds(cols - LANES, LANES)
        weight_plus, weight_minus = face_weights(rate_ref[1, :, last], flag_ref[1, :, last])
        columns = [low_ref[plane][:, :1] for plane in range(planes)]
        columns += [high_ref[plane][:, LANES - 1 :] for plane in range(planes)]
        columns += [weight_plus[:, LANES - 1 :], weight_minus[:, LANES - 1 :]]
        edge_ref[...] = gather_columns(columns, rows)
    for copy in copies:
        copy.wait()


def pack(concentration, stiff_mask, layer, ranks, after, faces):
    planes, rows, cols = concentration.shape
    held = planes // NZ
    block = stiff_mask.shape[1]
    message = jax.ShapeDtypeStruct((held * rows + block, cols), jnp.float32)
    out_shape, out_specs = [message] * ranks, [any_spec()] * ranks
    if faces:
        out_shape.append(jax.ShapeDtypeStruct((rows, LANES), jnp.float32))
        out_specs.append(whole_spec())
    results = pl.pallas_call(
        functools.partial(pack_kernel, ranks, layer, bool(faces)),
        out_shape=out_shape,
        in_specs=[any_spec(), whole_spec(), any_spec()] + [whole_spec()] * len(faces),
        out_specs=out_specs,
        scratch_shapes=[
            pltpu.VMEM((ranks, block, cols), jnp.float32),
            pltpu.VMEM((planes, rows, LANES), jnp.float32),
            pltpu.VMEM((planes, rows, LANES), jnp.float32),
            pltpu.SemaphoreType.DMA((ranks * (held + 1) + 2,)),
        ],
        compiler_params=pltpu.CompilerParams(vmem_limit_bytes=VMEM_LIMIT),
        cost_estimate=pl.CostEstimate(
            flops=0, bytes_accessed=8 * ranks * held * rows * cols, transcendentals=0
        ),
        name="pack",
    )(concentration, stiff_mask, after, *faces)
    return list(results[:ranks]), results[ranks:]


def spread_kernel(ranks, mixing_ref, inverse_ref, affinity_ref, mineral_ref, *refs):
    _, first_ref, both_ref, ratio_ref = refs
    components = mixing_ref.shape[0]
    stacked = components * TILE
    held = components // ranks
    me = lax.axis_index("comp")

    def dot(left, right):
        return jnp.dot(left, right, precision=highest, preferred_element_type=jnp.float32)

    def pick(shape, stacked_dim):
        at = lax.broadcasted_iota(jnp.int32, shape, stacked_dim) // TILE
        component = lax.rem(me + ranks - at // held, ranks) * held + lax.rem(at, held)
        held_at = lax.broadcasted_iota(jnp.int32, shape, 1 - stacked_dim)
        return jnp.where(component == held_at, 1.0, 0.0)

    rows = pick((stacked, components), 0)
    cols = pick((components, stacked), 1)
    inner = (stacked, stacked)
    same = lax.rem(lax.broadcasted_iota(jnp.int32, inner, 0), TILE) == lax.rem(
        lax.broadcasted_iota(jnp.int32, inner, 1), TILE
    )

    def spread(matrix):
        return jnp.where(same, dot(dot(rows, matrix), cols), 0.0)

    inverse = inverse_ref[...]
    square = (components, components)
    unit = jnp.where(
        lax.broadcasted_iota(jnp.int32, square, 0) == lax.broadcasted_iota(jnp.int32, square, 1),
        1.0,
        0.0,
    )
    blend = unit - dot(inverse, mixing_ref[...])
    high, low = split(spread(inverse))
    first_ref[...] = jnp.concatenate([high, low, high], axis=1)
    high, low = split(
        jnp.concatenate([spread(blend), spread(-inverse * affinity_ref[...])], axis=1)
    )
    both_ref[...] = jnp.concatenate([high, low, high], axis=1)
    ratio = jnp.sum(rows * (mineral_ref[...] / affinity_ref[...]), axis=1, keepdims=True)
    ratio_ref[...] = jnp.broadcast_to(ratio, (stacked, LANES))


def spread_parameters(ranks, mixing, mixing_inverse, affinity, mineral, after):
    components = mixing.shape[0]
    stacked = components * TILE
    return pl.pallas_call(
        functools.partial(spread_kernel, ranks),
        out_shape=[
            jax.ShapeDtypeStruct((stacked, 3 * stacked), jnp.bfloat16),
            jax.ShapeDtypeStruct((stacked, 6 * stacked), jnp.bfloat16),
            jax.ShapeDtypeStruct((stacked, LANES), jnp.float32),
        ],
        in_specs=[whole_spec()] * 4 + [any_spec()],
        out_specs=[whole_spec()] * 3,
        compiler_params=pltpu.CompilerParams(vmem_limit_bytes=VMEM_LIMIT),
        cost_estimate=pl.CostEstimate(
            flops=12 * stacked * stacked * components,
            bytes_accessed=32 * stacked * stacked,
            transcendentals=0,
        ),
        name="spread_parameters",
    )(mixing, mixing_inverse, affinity.reshape(1, -1), mineral.reshape(1, -1), after)


def step_kernel(pieces, is_first, with_rim, layer, layers, spread_ref, retard_ref, *refs):
    value_refs, refs = refs[:pieces], refs[pieces:]
    (low_ref, high_ref, rate_ref, flag_ref, ratio_ref, first_ref, both_ref), refs = (
        refs[:7],
        refs[7:],
    )
    if not is_first:
        stiff_ref, refs = refs[0], refs[1:]
    out_refs, refs = refs[:pieces], refs[pieces:]
    if with_rim:
        rim_ref, refs = refs[0], refs[1:]
    if is_first:
        stiff_ref, refs = refs[0], refs[1:]
    offset_ref, species_ref, plain_ref = refs
    groups, stacked, cols = species_ref.shape
    rows = groups * TILE
    components = stacked // TILE
    held = components // pieces
    me = lax.axis_index("comp")
    ranks = [lax.rem(me + pieces - q, pieces) for q in range(pieces)]
    row_at = lax.broadcasted_iota(jnp.int32, (rows, cols), 0)
    col_at = lax.broadcasted_iota(jnp.int32, (rows, cols), 1)

    def product(weights, parts):
        highs, lows = zip(*[split(part) for part in parts])
        operand = jnp.concatenate(highs + highs + lows, axis=0)
        return jnp.dot(weights[...], operand, preferred_element_type=jnp.float32)

    weight_plus, weight_minus = face_weights(rate_ref[...], flag_ref[...])

    def column(side, at):
        return jnp.broadcast_to(side[:, at : at + 1], (rows, cols))

    def from_lower_row(value):
        return jnp.where(row_at == 0, 0.0, pltpu.roll(value, 1, 0))

    def from_upper_row(value):
        return jnp.where(row_at == rows - 1, 0.0, pltpu.roll(value, rows - 1, 0))

    def from_lower_col(value, edge):
        return jnp.where(col_at == 0, edge, pltpu.roll(value, 1, 1))

    def from_upper_col(value, edge):
        return jnp.where(col_at == cols - 1, edge, pltpu.roll(value, cols - 1, 1))

    if is_first:
        planes = held * layers * pieces
        rim_side, rim_at = low_ref[0], 2 * planes
        turn = LANES - (me * layers + layer)
        sides = []
        for rank in ranks:
            side = pltpu.roll(low_ref[jnp.bitwise_xor(me, rank)], turn, 1)
            for index in range(held):
                at = index * layers * pieces
                sides.append((side, planes + at, side, at))
    else:
        rim_side, rim_at = low_ref[...], 2 * components
        low_side, high_side = low_ref[...], high_ref[...]
        sides = [(low_side, components + at, high_side, at) for at in range(components)]
    down_plus = from_lower_row(weight_plus[0])
    down_minus = from_lower_row(weight_minus[0])
    side_plus = from_lower_col(weight_plus[1], column(rim_side, rim_at))
    side_minus = from_lower_col(weight_minus[1], column(rim_side, rim_at + 1))
    centre = down_minus + weight_plus[0] + side_minus + weight_plus[1]
    for at, (low_side, low_at, high_side, high_at) in enumerate(sides):
        q, index = divmod(at, held)
        value = value_refs[q][index * rows : (index + 1) * rows, :]
        component = ranks[q] * held + index
        spread = spread_ref[component]
        retard = 1.0 / jnp.full((rows, cols), retard_ref[component], jnp.float32)
        change = (
            (down_plus + spread) * from_lower_row(value)
            + (weight_minus[0] + spread) * from_upper_row(value)
            + (side_plus + spread) * from_lower_col(value, column(low_side, low_at))
            + (weight_minus[1] + spread) * from_upper_col(value, column(high_side, high_at))
            - (centre + 4.0 * spread) * value
        )
        value = value + change * retard
        for group in range(groups):
            offset_ref[group, at * TILE : (at + 1) * TILE, :] = value[
                group * TILE : (group + 1) * TILE
            ]

    for group in range(groups):
        offset = product(first_ref, [offset_ref[group]])
        offset_ref[group] = offset
        species_ref[group] = offset

    def plain_step(_, carry):
        for group in range(groups):
            species = species_ref[group]
            species_ref[group] = offset_ref[group] + product(both_ref, [species, jnp.tanh(species)])
        return carry

    lax.fori_loop(0, NEWT - 1, plain_step, 0)
    plain_ref[...] = species_ref[...]
    ratio = jnp.concatenate([ratio_ref[...]] * (cols // LANES), axis=1)

    def stiff_step(_, carry):
        for group in range(groups):
            species = species_ref[group]
            reaction = jnp.tanh(species) + ratio * jnp.tanh(species + species)
            species_ref[group] = offset_ref[group] + product(both_ref, [species, reaction])
        return carry

    lax.fori_loop(0, STIFF, stiff_step, 0)
    if is_first:
        block = rows // pieces
        for rank, value_ref in zip(ranks, value_refs):
            spot = pl.ds(pl.multiple_of(rank * block, TILE), block)
            stiff_ref[spot, :] = value_ref[held * rows :, :]
    for group in range(groups):
        spot = slice(group * TILE, (group + 1) * TILE)
        stiff = stiff_ref[spot, :] > 0.0
        for at in range(components):
            lane = slice(at * TILE, (at + 1) * TILE)
            start = at % held * rows + group * TILE
            out_refs[at // held][start : start + TILE, :] = jnp.where(
                stiff, species_ref[group, lane, :], plain_ref[group, lane, :]
            )
    if with_rim:
        edges = [ref[i * rows : (i + 1) * rows, :] for ref in out_refs for i in range(held)]
        columns = [value[:, :1] for value in edges] + [value[:, cols - 1 :] for value in edges]
        columns += [weight_plus[1][:, cols - 1 :], weight_minus[1][:, cols - 1 :]]
        rim_ref[...] = gather_columns(columns, rows)


def layer_step(values, stiff, low, high, shared, layer, layers, with_rim):
    dispersion, retardation, face_rate, face_flag, ratio, first, both = shared
    pieces = len(values)
    rows, cols = face_rate.shape[1:]
    groups = rows // TILE
    stacked = ratio.shape[0]
    components = stacked // TILE
    scalar = pl.BlockSpec(memory_space=pltpu.SMEM)
    plane = jax.ShapeDtypeStruct((components // pieces * rows, cols), jnp.float32)
    out_shape = [plane] * pieces
    if with_rim:
        out_shape.append(jax.ShapeDtypeStruct((rows, LANES), jnp.float32))
    if stiff is None:
        out_shape.append(jax.ShapeDtypeStruct((rows, cols), jnp.float32))
    field = pltpu.VMEM((groups, stacked, cols), jnp.float32)
    cells = rows * cols
    operands = [dispersion, retardation, *values, low, high, face_rate, face_flag]
    operands += [ratio, first, both]
    if stiff is not None:
        operands.append(stiff)
    results = pl.pallas_call(
        functools.partial(step_kernel, pieces, stiff is None, with_rim, layer, layers),
        out_shape=out_shape,
        in_specs=[scalar, scalar] + [whole_spec()] * (len(operands) - 2),
        out_specs=[whole_spec()] * len(out_shape),
        scratch_shapes=[field, field, field],
        compiler_params=pltpu.CompilerParams(vmem_limit_bytes=VMEM_LIMIT),
        cost_estimate=pl.CostEstimate(
            flops=0, bytes_accessed=8 * components * cells, transcendentals=0
        ),
        name="layer_step",
    )(*operands)
    values, results = results[:pieces], results[pieces:]
    rims = results[0] if with_rim else None
    return values, (results[-1] if stiff is None else stiff), rims


def by_layers(
    concentration,
    face_rate,
    face_flag,
    retardation,
    dispersion,
    mixing,
    mixing_inverse,
    affinity,
    mineral,
    stiff_mask,
):
    ranks = lax.axis_size("comp")
    me = lax.axis_index("comp")
    planes, rows, cols = concentration.shape
    held = planes // NZ
    layers = NZ // ranks

    def send(value, by):
        return lax.ppermute(value, "comp", [(i, (i + by) % ranks) for i in range(ranks)])

    faces = (face_rate, face_flag)
    messages, (edges,) = pack(concentration, stiff_mask, 0, ranks, face_rate, faces)
    arrived = [[send(part, q) if q else part for q, part in enumerate(messages)]]

    from_low, from_high = shifted(edges, "space", 1), shifted(edges, "space", -1)
    lane_at = lax.broadcasted_iota(jnp.int32, edges.shape, 1)
    sides = jnp.where(lane_at < planes, from_high, from_low)[None]
    span = 1
    while span < ranks:
        other = lax.ppermute(sides, "comp", [(i, i ^ span) for i in range(ranks)])
        sides = jnp.concatenate([sides, other])
        span *= 2

    first, both, ratio = spread_parameters(
        ranks, mixing, mixing_inverse, affinity, mineral, edges
    )
    shared = (dispersion, retardation, face_rate, face_flag, ratio, first, both)

    for layer in range(1, layers):
        messages, _ = pack(concentration, stiff_mask, layer, ranks, sides, ())
        arrived.append([send(part, q) if q else part for q, part in enumerate(messages)])

    result = jnp.zeros((held, NZ, rows, cols), jnp.float32)
    for layer in range(layers):
        values, stiff, low, high = arrived[layer], None, sides, sides
        for step in range(STEPS):
            last = step == STEPS - 1
            values, stiff, rims = layer_step(
                values, stiff, low, high, shared, layer, layers, not last
            )
            if not last:
                low, high = shifted(rims, "space", 1), shifted(rims, "space", -1)
        for q in range(ranks):
            piece = send(values[q], -q) if q else values[q]
            result = lax.dynamic_update_slice(
                result,
                piece.reshape(held, 1, rows, cols),
                (0, (me + q) % ranks * layers + layer, 0, 0),
            )
    return result.reshape(planes, rows, cols)


def shards(concentration, face_rate, face_flag, *parameters):
    ranks = lax.axis_size("comp")
    planes, rows, cols = concentration.shape
    whole = NZ % ranks == 0 and planes % NZ == 0 and ranks & (ranks - 1) == 0
    narrow = 2 * max(NC, planes) + 2 <= LANES
    even = rows % (ranks * TILE) == 0 and cols % LANES == 0
    plan = by_layers if whole and narrow and even else by_rows
    return plan(concentration, face_rate, face_flag, *parameters)


def solution(mesh):
    in_specs = (
        P(("real", "comp"), None, "space"),
        P(None, "real", "space"),
        P(None, "real", "space"),
        P(),
        P(),
        P(),
        P(),
        P(),
        P(),
        P(None, ("real", "comp"), "space"),
    )
    out_specs = P(("real", "comp"), None, "space")
    return jax.shard_map(shards, mesh=mesh, in_specs=in_specs, out_specs=out_specs, check_vma=False)
```

```python
import functools

import jax
import jax.numpy as jnp
from jax import lax
from jax.experimental import pallas as pl
from jax.experimental.pallas import tpu as pltpu
from jax.sharding import PartitionSpec as P

NC = 16
NZ = 8
STEPS = 2
NEWT = 4
STIFF = 4


highest = lax.Precision.HIGHEST


def shifted(shard, axis, by):
    devices = lax.axis_size(axis)
    pairs = [(i, i + by) for i in range(devices) if 0 <= i + by < devices]
    return lax.ppermute(shard, axis, pairs)


def extended(block, sides, width):
    for axis, dim in sides:
        count = lax.axis_size(axis)
        forward = [(i, i + 1) for i in range(count - 1)]
        backward = [(target, source) for source, target in forward]
        low = lax.ppermute(
            lax.slice_in_dim(block, block.shape[dim] - width, None, axis=dim), axis, forward
        )
        high = lax.ppermute(lax.slice_in_dim(block, 0, width, axis=dim), axis, backward)
        block = jnp.concatenate([low, block, high], axis=dim)
    return block


def shift_down(values, axis_index):
    size_along = values.shape[axis_index]
    zero_row = jnp.zeros_like(lax.slice_in_dim(values, 0, 1, axis=axis_index))
    kept = lax.slice_in_dim(values, 0, size_along - 1, axis=axis_index)
    return jnp.concatenate([zero_row, kept], axis=axis_index)


def face_weights(face_rate, face_flag):
    flag_values = face_flag.astype(jnp.float32)
    weight_plus = face_rate * flag_values
    weight_minus = face_rate * (1.0 - flag_values)
    return (weight_plus, weight_minus)


def advance(
    values, lower_row, upper_row, lower_col, upper_col, coefficients, retard_planes, spread_planes
):
    divergence = (
        coefficients[0] * lower_row
        + coefficients[1] * upper_row
        + coefficients[2] * lower_col
        + coefficients[3] * upper_col
        - coefficients[4] * values
    )
    laplace = lower_row + upper_row + lower_col + upper_col - 4.0 * values
    return values + (divergence + spread_planes * laplace) / retard_planes


def residual_of(species, target, mixing, affinity, mineral, stiff):
    total = jnp.dot(
        mixing, species, precision=highest, preferred_element_type=jnp.float32
    ) + affinity[:, None] * jnp.tanh(species)
    if stiff:
        total = total + mineral[:, None] * jnp.tanh(2.0 * species)
    return total - target


def newton_steps(species, target, repeats, stiff, mixing, mixing_inverse, affinity, mineral):
    for iteration in range(repeats):
        update = residual_of(species, target, mixing, affinity, mineral, stiff)
        species = species - jnp.dot(
            mixing_inverse, update, precision=highest, preferred_element_type=jnp.float32
        )
    return species


def speciate(cell_block, stiff_mask, mixing, mixing_inverse, affinity, mineral):
    target = cell_block.reshape(NC, -1)
    flat_mask = stiff_mask.reshape(-1) > 0
    species = jnp.zeros_like(target)
    species = newton_steps(species, target, NEWT, False, mixing, mixing_inverse, affinity, mineral)
    stiffer = newton_steps(species, target, STIFF, True, mixing, mixing_inverse, affinity, mineral)
    species = jnp.where(flat_mask[None, :], stiffer, species)
    return species.reshape(cell_block.shape)


def by_rows(
    concentration,
    face_rate,
    face_flag,
    retardation,
    dispersion,
    mixing,
    mixing_inverse,
    affinity,
    mineral,
    stiff_mask,
):
    weight_plus, weight_minus = face_weights(face_rate, face_flag)
    rim_weights = jnp.stack([weight_plus[1, :, -1], weight_minus[1, :, -1]])
    left_rims = shifted(rim_weights, "space", 1)
    side_plus = jnp.concatenate([left_rims[0][:, None], weight_plus[1, :, :-1]], axis=1)
    side_minus = jnp.concatenate([left_rims[1][:, None], weight_minus[1, :, :-1]], axis=1)
    down_plus = shift_down(weight_plus[0], 0)
    down_minus = shift_down(weight_minus[0], 0)
    centre = down_minus + weight_plus[0] + side_minus + weight_plus[1]
    coefficients = jnp.stack([down_plus, weight_minus[0], side_plus, weight_minus[1], centre])
    retard_all = jnp.repeat(retardation, NZ)
    spread_all = jnp.repeat(dispersion, NZ)
    rows_held = stiff_mask.shape[1]
    row_start = lax.axis_index("comp") * rows_held
    cell_coefficients = lax.dynamic_slice_in_dim(coefficients, row_start, rows_held, 1)
    retard_planes = retard_all[:, None, None]
    spread_planes = spread_all[:, None, None]
    cell_block = lax.all_to_all(concentration, "comp", split_axis=1, concat_axis=0, tiled=True)
    for step_index in range(STEPS):
        padded = extended(cell_block, (("comp", 1), ("space", 2)), 1)
        cell_block = advance(
            cell_block,
            padded[:, :-2, 1:-1],
            padded[:, 2:, 1:-1],
            padded[:, 1:-1, :-2],
            padded[:, 1:-1, 2:],
            cell_coefficients,
            retard_planes,
            spread_planes,
        )
        cell_block = speciate(cell_block, stiff_mask, mixing, mixing_inverse, affinity, mineral)
    return lax.all_to_all(cell_block, "comp", split_axis=0, concat_axis=1, tiled=True)


TILE = 8
LANES = 128
VMEM_LIMIT = 24 * 1024 * 1024
MOST_VMEM = 60 * 1024 * 1024


def whole_spec():
    return pl.BlockSpec(memory_space=pltpu.VMEM)


def any_spec():
    return pl.BlockSpec(memory_space=pl.ANY)


def hbm_spec():
    return pl.BlockSpec(memory_space=pltpu.HBM)


def split(value):
    high = value.astype(jnp.bfloat16)
    return high, (value - high.astype(jnp.float32)).astype(jnp.bfloat16)


def gather_columns(columns, rows):
    lane_at = lax.broadcasted_iota(jnp.int32, (rows, LANES), 1)
    gathered = jnp.zeros((rows, LANES), jnp.float32)
    for lane, column in enumerate(columns):
        gathered = jnp.where(lane_at == lane, jnp.broadcast_to(column, (rows, LANES)), gathered)
    return gathered


def bands(rows, cols):
    return -(-rows * LANES // (TILE * cols)) * TILE


def band_spots(rows, cols):
    wide = cols // LANES
    return [
        (group, group // wide * TILE, group % wide * LANES) for group in range(rows // TILE)
    ]


def pack_kernel(layer, plane_ref, mask_ref, *refs):
    if layer:
        (low_ref, high_ref), refs = refs[:2], refs[2:]
    else:
        (rate_ref, flag_ref), refs = refs[:2], refs[2:]
    refs, scratch = refs[:-6], refs[-6:]
    mask_part, mark_ref, first_ref, last_ref, mask_sems, sems = scratch
    if layer:
        out_refs = refs
    else:
        out_refs, edge_ref = refs[:-1], refs[-1]
    ranks = len(out_refs)
    planes, rows, cols = plane_ref.shape
    levels, block, _ = mask_ref.shape
    held = planes // levels
    me = lax.axis_index("comp")
    copies, masks = [], []

    def start(source, target):
        copies.append(pltpu.make_async_copy(source, target, sems.at[len(copies)]))
        copies[-1].start()

    for q, out_ref in enumerate(out_refs):
        at = lax.rem(me + q, ranks) * (levels // ranks) + layer
        masks.append(pltpu.make_async_copy(mask_ref.at[at], mask_part.at[q], mask_sems.at[q]))
        masks[-1].start()
        for index in range(held):
            start(plane_ref.at[index * levels + at], out_ref.at[pl.ds(index * rows, rows)])
    if layer:
        lane_at = lax.broadcasted_iota(jnp.int32, (rows, LANES), 1)
        sides = jnp.where(lane_at < planes, high_ref[...], low_ref[...])
        for group, row, lane in band_spots(rows, cols):
            part = sides[group * TILE : (group + 1) * TILE]
            for q in range(ranks):
                mark_ref[q, block + row : block + row + TILE, lane : lane + LANES] = part
    else:
        start(plane_ref.at[:, :, pl.ds(0, LANES)], first_ref)
        start(plane_ref.at[:, :, pl.ds(cols - LANES, LANES)], last_ref)
    for q, out_ref in enumerate(out_refs):
        masks[q].wait()
        mark_ref[q, :block, :] = mask_part[q].astype(jnp.float32)
        count = mark_ref.shape[1]
        start(mark_ref.at[q], out_ref.at[pl.ds(held * rows, count)])
    for copy in copies:
        copy.wait()
    if not layer:
        end = slice(cols - LANES, cols)
        weight_plus, weight_minus = face_weights(rate_ref[1, :, end], flag_ref[1, :, end])
        columns = [first_ref[plane][:, :1] for plane in range(planes)]
        columns += [last_ref[plane][:, LANES - 1 :] for plane in range(planes)]
        columns += [weight_plus[:, LANES - 1 :], weight_minus[:, LANES - 1 :]]
        edge_ref[...] = gather_columns(columns, rows)


def pack(concentration, stiff_mask, layer, ranks, others):
    planes, rows, cols = concentration.shape
    held = planes // NZ
    block = stiff_mask.shape[1]
    extra = block + (bands(rows, cols) if layer else 0)
    message = jax.ShapeDtypeStruct((held * rows + extra, cols), jnp.float32)
    out_shape, out_specs = [message] * ranks, [any_spec()] * ranks
    if not layer:
        out_shape.append(jax.ShapeDtypeStruct((rows, LANES), jnp.float32))
        out_specs.append(whole_spec())
    results = pl.pallas_call(
        functools.partial(pack_kernel, layer),
        out_shape=out_shape,
        in_specs=[hbm_spec()] * 2 + [whole_spec()] * 2,
        out_specs=out_specs,
        scratch_shapes=[
            pltpu.VMEM((ranks, block, cols), jnp.int32),
            pltpu.VMEM((ranks, extra, cols), jnp.float32),
            pltpu.VMEM((planes, rows, LANES), jnp.float32),
            pltpu.VMEM((planes, rows, LANES), jnp.float32),
            pltpu.SemaphoreType.DMA((ranks,)),
            pltpu.SemaphoreType.DMA((ranks * (held + 1) + 2,)),
        ],
        compiler_params=pltpu.CompilerParams(vmem_limit_bytes=VMEM_LIMIT if layer else MOST_VMEM),
        cost_estimate=pl.CostEstimate(flops=0, bytes_accessed=0, transcendentals=0),
        name="pack",
    )(concentration, stiff_mask, *others)
    return list(results[:ranks]), results[ranks:]


def edges_kernel(held, *refs):
    half = (len(refs) - 4) // 2
    low_refs, high_refs, (rate_ref, flag_ref, _, out_ref) = refs[:half], refs[half:-4], refs[-4:]
    rows = rate_ref.shape[1]
    weight_plus, weight_minus = face_weights(rate_ref[1], flag_ref[1])
    spots = [slice(index * rows, (index + 1) * rows) for index in range(held)]
    columns = [ref[spot, :][:, :1] for ref in low_refs for spot in spots]
    columns += [ref[spot, :][:, LANES - 1 :] for ref in high_refs for spot in spots]
    columns += [weight_plus[:, LANES - 1 :], weight_minus[:, LANES - 1 :]]
    out_ref[...] = gather_columns(columns, rows)


def edges_of(values, face_rate, face_flag, after):
    rows, cols = face_rate.shape[1:]
    last = cols // LANES - 1
    size = values[0].shape[0]
    low = pl.BlockSpec((size, LANES), lambda i: (0, 0))
    high = pl.BlockSpec((size, LANES), lambda i: (0, last))
    face = pl.BlockSpec((2, rows, LANES), lambda i: (0, 0, last))
    return pl.pallas_call(
        functools.partial(edges_kernel, size // rows),
        grid=(1,),
        out_shape=jax.ShapeDtypeStruct((rows, LANES), jnp.float32),
        in_specs=[low] * len(values) + [high] * len(values) + [face, face, hbm_spec()],
        out_specs=pl.BlockSpec((rows, LANES), lambda i: (0, 0)),
        compiler_params=pltpu.CompilerParams(vmem_limit_bytes=VMEM_LIMIT),
        cost_estimate=pl.CostEstimate(flops=0, bytes_accessed=0, transcendentals=0),
        name="edges",
    )(*values, *values, face_rate, face_flag, after)


def spread_kernel(ranks, mixing_ref, inverse_ref, affinity_ref, mineral_ref, *refs):
    _, first_ref, both_ref, ratio_ref = refs
    components = mixing_ref.shape[0]
    stacked = components * TILE
    held = components // ranks
    me = lax.axis_index("comp")

    def dot(left, right):
        return jnp.dot(left, right, precision=highest, preferred_element_type=jnp.float32)

    def pick(shape, stacked_dim):
        at = lax.broadcasted_iota(jnp.int32, shape, stacked_dim) // TILE
        component = lax.rem(me + ranks - at // held, ranks) * held + lax.rem(at, held)
        held_at = lax.broadcasted_iota(jnp.int32, shape, 1 - stacked_dim)
        return jnp.where(component == held_at, 1.0, 0.0)

    rows = pick((stacked, components), 0)
    cols = pick((components, stacked), 1)
    inner = (stacked, stacked)
    same = lax.rem(lax.broadcasted_iota(jnp.int32, inner, 0), TILE) == lax.rem(
        lax.broadcasted_iota(jnp.int32, inner, 1), TILE
    )

    def spread(matrix):
        return jnp.where(same, dot(dot(rows, matrix), cols), 0.0)

    inverse = inverse_ref[...]
    square = (components, components)
    unit = jnp.where(
        lax.broadcasted_iota(jnp.int32, square, 0) == lax.broadcasted_iota(jnp.int32, square, 1),
        1.0,
        0.0,
    )
    blend = unit - dot(inverse, mixing_ref[...])
    high, low = split(spread(inverse))
    first_ref[...] = jnp.concatenate([high, low, high], axis=1)
    high, low = split(
        jnp.concatenate([spread(blend), spread(-inverse * affinity_ref[...])], axis=1)
    )
    both_ref[...] = jnp.concatenate([high, low, high], axis=1)
    ratio = jnp.sum(rows * (mineral_ref[...] / affinity_ref[...]), axis=1, keepdims=True)
    ratio_ref[...] = jnp.broadcast_to(ratio, (stacked, LANES))


def spread_parameters(ranks, mixing, mixing_inverse, affinity, mineral, after):
    components = mixing.shape[0]
    stacked = components * TILE
    return pl.pallas_call(
        functools.partial(spread_kernel, ranks),
        out_shape=[
            jax.ShapeDtypeStruct((stacked, 3 * stacked), jnp.bfloat16),
            jax.ShapeDtypeStruct((stacked, 6 * stacked), jnp.bfloat16),
            jax.ShapeDtypeStruct((stacked, LANES), jnp.float32),
        ],
        in_specs=[whole_spec()] * 4 + [any_spec()],
        out_specs=[whole_spec()] * 3,
        compiler_params=pltpu.CompilerParams(vmem_limit_bytes=VMEM_LIMIT),
        cost_estimate=pl.CostEstimate(flops=0, bytes_accessed=0, transcendentals=0),
        name="spread_parameters",
    )(mixing, mixing_inverse, affinity.reshape(1, -1), mineral.reshape(1, -1), after)


def step_kernel(pieces, layer, is_first, with_rim, spread_ref, retard_ref, *refs):
    value_refs, refs = refs[:pieces], refs[pieces:]
    (low_ref, high_ref, rate_ref, flag_ref, ratio_ref, first_ref, both_ref), refs = (
        refs[:7],
        refs[7:],
    )
    if not is_first:
        stiff_ref, refs = refs[0], refs[1:]
    out_refs, refs = refs[:pieces], refs[pieces:]
    if with_rim:
        rim_ref, refs = refs[0], refs[1:]
    if is_first:
        stiff_ref, refs = refs[0], refs[1:]
    offset_ref, species_ref, plain_ref = refs
    groups, stacked, cols = species_ref.shape
    rows = groups * TILE
    components = stacked // TILE
    held = components // pieces
    me = lax.axis_index("comp")
    ranks = [lax.rem(me + pieces - q, pieces) for q in range(pieces)]
    row_at = lax.broadcasted_iota(jnp.int32, (rows, cols), 0)
    col_at = lax.broadcasted_iota(jnp.int32, (rows, cols), 1)

    def product(weights, parts):
        highs, lows = zip(*[split(part) for part in parts])
        operand = jnp.concatenate(highs + highs + lows, axis=0)
        return jnp.dot(weights[...], operand, preferred_element_type=jnp.float32)

    weight_plus, weight_minus = face_weights(rate_ref[...], flag_ref[...])

    def column(side, at):
        return jnp.broadcast_to(side[:, at : at + 1], (rows, cols))

    def from_lower_row(value):
        return jnp.where(row_at == 0, 0.0, pltpu.roll(value, 1, 0))

    def from_upper_row(value):
        return jnp.where(row_at == rows - 1, 0.0, pltpu.roll(value, rows - 1, 0))

    def from_lower_col(value, edge):
        return jnp.where(col_at == 0, edge, pltpu.roll(value, 1, 1))

    def from_upper_col(value, edge):
        return jnp.where(col_at == cols - 1, edge, pltpu.roll(value, cols - 1, 1))

    block = rows // pieces
    low_side, high_side = low_ref[...], high_ref[...]
    rim_at = 2 * components
    sides = [(low_side, components + at, high_side, at) for at in range(components)]
    if is_first and layer:
        sides = []
        rim_at = 2 * held * NZ
        turn = LANES - (me * (NZ // pieces) + layer)
        for value_ref in value_refs:
            start = held * rows + block
            side = jnp.concatenate(
                [
                    value_ref[start + row : start + row + TILE, lane : lane + LANES]
                    for _, row, lane in band_spots(rows, cols)
                ]
            )
            if not sides:
                low_side = side
            side = pltpu.roll(side, turn, 1)
            for index in range(held):
                sides.append((side, (held + index) * NZ, side, index * NZ))
    down_plus = from_lower_row(weight_plus[0])
    down_minus = from_lower_row(weight_minus[0])
    side_plus = from_lower_col(weight_plus[1], column(low_side, rim_at))
    side_minus = from_lower_col(weight_minus[1], column(low_side, rim_at + 1))
    centre = down_minus + weight_plus[0] + side_minus + weight_plus[1]
    for at, (low_side, low_at, high_side, high_at) in enumerate(sides):
        q, index = divmod(at, held)
        value = value_refs[q][index * rows : (index + 1) * rows, :]
        component = ranks[q] * held + index
        spread = spread_ref[component]
        retard = 1.0 / jnp.full((rows, cols), retard_ref[component], jnp.float32)
        change = (
            (down_plus + spread) * from_lower_row(value)
            + (weight_minus[0] + spread) * from_upper_row(value)
            + (side_plus + spread) * from_lower_col(value, column(low_side, low_at))
            + (weight_minus[1] + spread) * from_upper_col(value, column(high_side, high_at))
            - (centre + 4.0 * spread) * value
        )
        value = value + change * retard
        for group in range(groups):
            offset_ref[group, at * TILE : (at + 1) * TILE, :] = value[
                group * TILE : (group + 1) * TILE
            ]

    for group in range(groups):
        offset = product(first_ref, [offset_ref[group]])
        offset_ref[group] = offset
        species_ref[group] = offset

    def plain_step(_, carry):
        for group in range(groups):
            species = species_ref[group]
            species_ref[group] = offset_ref[group] + product(both_ref, [species, jnp.tanh(species)])
        return carry

    lax.fori_loop(0, NEWT - 1, plain_step, 0)
    plain_ref[...] = species_ref[...]
    ratio = jnp.concatenate([ratio_ref[...]] * (cols // LANES), axis=1)

    def stiff_step(_, carry):
        for group in range(groups):
            species = species_ref[group]
            reaction = jnp.tanh(species) + ratio * jnp.tanh(species + species)
            species_ref[group] = offset_ref[group] + product(both_ref, [species, reaction])
        return carry

    lax.fori_loop(0, STIFF, stiff_step, 0)
    if is_first:
        for rank, value_ref in zip(ranks, value_refs):
            spot = pl.ds(pl.multiple_of(rank * block, TILE), block)
            stiff_ref[spot, :] = value_ref[held * rows : held * rows + block, :]
    for group in range(groups):
        spot = slice(group * TILE, (group + 1) * TILE)
        stiff = stiff_ref[spot, :] > 0.0
        for at in range(components):
            lane = slice(at * TILE, (at + 1) * TILE)
            start = at % held * rows + group * TILE
            out_refs[at // held][start : start + TILE, :] = jnp.where(
                stiff, species_ref[group, lane, :], plain_ref[group, lane, :]
            )
    if with_rim:
        edges = [ref[i * rows : (i + 1) * rows, :] for ref in out_refs for i in range(held)]
        columns = [value[:, :1] for value in edges] + [value[:, cols - 1 :] for value in edges]
        columns += [weight_plus[1][:, cols - 1 :], weight_minus[1][:, cols - 1 :]]
        rim_ref[...] = gather_columns(columns, rows)


def layer_step(values, stiff, low, high, shared, layer, with_rim):
    dispersion, retardation, face_rate, face_flag, ratio, first, both = shared
    pieces = len(values)
    rows, cols = face_rate.shape[1:]
    groups = rows // TILE
    stacked = ratio.shape[0]
    components = stacked // TILE
    scalar = pl.BlockSpec(memory_space=pltpu.SMEM)
    plane = jax.ShapeDtypeStruct((components // pieces * rows, cols), jnp.float32)
    out_shape = [plane] * pieces
    if with_rim:
        out_shape.append(jax.ShapeDtypeStruct((rows, LANES), jnp.float32))
    if stiff is None:
        out_shape.append(jax.ShapeDtypeStruct((rows, cols), jnp.float32))
    field = pltpu.VMEM((groups, stacked, cols), jnp.float32)
    cells = rows * cols
    operands = [dispersion, retardation, *values, low, high, face_rate, face_flag]
    operands += [ratio, first, both]
    if stiff is not None:
        operands.append(stiff)
    results = pl.pallas_call(
        functools.partial(step_kernel, pieces, layer, stiff is None, with_rim),
        out_shape=out_shape,
        in_specs=[scalar, scalar] + [whole_spec()] * (len(operands) - 2),
        out_specs=[whole_spec()] * len(out_shape),
        scratch_shapes=[field, field, field],
        compiler_params=pltpu.CompilerParams(vmem_limit_bytes=VMEM_LIMIT),
        cost_estimate=pl.CostEstimate(flops=0, bytes_accessed=0, transcendentals=0),
        name="layer_step",
    )(*operands)
    values, results = results[:pieces], results[pieces:]
    rims = results[0] if with_rim else None
    return values, (results[-1] if stiff is None else stiff), rims


def by_layers(
    concentration,
    face_rate,
    face_flag,
    retardation,
    dispersion,
    mixing,
    mixing_inverse,
    affinity,
    mineral,
    stiff_mask,
):
    ranks = lax.axis_size("comp")
    me = lax.axis_index("comp")
    planes, rows, cols = concentration.shape
    held = planes // NZ
    layers = NZ // ranks

    def send(value, by):
        return lax.ppermute(value, "comp", [(i, (i + by) % ranks) for i in range(ranks)])

    arrived, others = [], (face_rate, face_flag)
    for layer in range(layers):
        messages, edges = pack(concentration, stiff_mask, layer, ranks, others)
        arrived.append([send(part, q) if q else part for q, part in enumerate(messages)])
        if edges:
            others = (shifted(edges[0], "space", 1), shifted(edges[0], "space", -1))
        after = messages[0]

    first, both, ratio = spread_parameters(ranks, mixing, mixing_inverse, affinity, mineral, after)
    shared = (dispersion, retardation, face_rate, face_flag, ratio, first, both)

    result = jnp.zeros((held, NZ, rows, cols), jnp.float32)
    for layer in range(layers):
        values, stiff = arrived[layer], None
        rims = None if layer else edges_of(values, face_rate, face_flag, after)
        for step in range(STEPS):
            if rims is None:
                low, high = others
            else:
                low, high = shifted(rims, "space", 1), shifted(rims, "space", -1)
            values, stiff, rims = layer_step(
                values, stiff, low, high, shared, layer, step < STEPS - 1
            )
        for q in range(ranks):
            piece = send(values[q], -q) if q else values[q]
            result = lax.dynamic_update_slice(
                result,
                piece.reshape(held, 1, rows, cols),
                (0, (me + q) % ranks * layers + layer, 0, 0),
            )
    return result.reshape(planes, rows, cols)


def shards(concentration, face_rate, face_flag, *parameters):
    ranks = lax.axis_size("comp")
    planes, rows, cols = concentration.shape
    whole = NZ % ranks == 0 and planes % NZ == 0
    narrow = 2 * max(NC, planes) + 2 <= LANES
    even = rows % (ranks * TILE) == 0 and cols % LANES == 0
    plan = by_layers if whole and narrow and even else by_rows
    return plan(concentration, face_rate, face_flag, *parameters)


def solution(mesh):
    in_specs = (
        P(("real", "comp"), None, "space"),
        P(None, "real", "space"),
        P(None, "real", "space"),
        P(),
        P(),
        P(),
        P(),
        P(),
        P(),
        P(None, ("real", "comp"), "space"),
    )
    out_specs = P(("real", "comp"), None, "space")
    return jax.shard_map(shards, mesh=mesh, in_specs=in_specs, out_specs=out_specs, check_vma=False)
```

```python
import functools

import jax
import jax.numpy as jnp
from jax import lax
from jax.experimental import pallas as pl
from jax.experimental.pallas import tpu as pltpu
from jax.sharding import PartitionSpec as P

NC = 16
NZ = 8
STEPS = 2
NEWT = 4
STIFF = 4


highest = lax.Precision.HIGHEST


def shifted(shard, axis, by):
    devices = lax.axis_size(axis)
    pairs = [(i, i + by) for i in range(devices) if 0 <= i + by < devices]
    return lax.ppermute(shard, axis, pairs)


def extended(block, sides, width):
    for axis, dim in sides:
        count = lax.axis_size(axis)
        forward = [(i, i + 1) for i in range(count - 1)]
        backward = [(target, source) for source, target in forward]
        low = lax.ppermute(
            lax.slice_in_dim(block, block.shape[dim] - width, None, axis=dim), axis, forward
        )
        high = lax.ppermute(lax.slice_in_dim(block, 0, width, axis=dim), axis, backward)
        block = jnp.concatenate([low, block, high], axis=dim)
    return block


def shift_down(values, axis_index):
    size_along = values.shape[axis_index]
    zero_row = jnp.zeros_like(lax.slice_in_dim(values, 0, 1, axis=axis_index))
    kept = lax.slice_in_dim(values, 0, size_along - 1, axis=axis_index)
    return jnp.concatenate([zero_row, kept], axis=axis_index)


def face_weights(face_rate, face_flag):
    flag_values = face_flag.astype(jnp.float32)
    weight_plus = face_rate * flag_values
    weight_minus = face_rate * (1.0 - flag_values)
    return (weight_plus, weight_minus)


def advance(
    values, lower_row, upper_row, lower_col, upper_col, coefficients, retard_planes, spread_planes
):
    divergence = (
        coefficients[0] * lower_row
        + coefficients[1] * upper_row
        + coefficients[2] * lower_col
        + coefficients[3] * upper_col
        - coefficients[4] * values
    )
    laplace = lower_row + upper_row + lower_col + upper_col - 4.0 * values
    return values + (divergence + spread_planes * laplace) / retard_planes


def residual_of(species, target, mixing, affinity, mineral, stiff):
    total = jnp.dot(
        mixing, species, precision=highest, preferred_element_type=jnp.float32
    ) + affinity[:, None] * jnp.tanh(species)
    if stiff:
        total = total + mineral[:, None] * jnp.tanh(2.0 * species)
    return total - target


def newton_steps(species, target, repeats, stiff, mixing, mixing_inverse, affinity, mineral):
    for iteration in range(repeats):
        update = residual_of(species, target, mixing, affinity, mineral, stiff)
        species = species - jnp.dot(
            mixing_inverse, update, precision=highest, preferred_element_type=jnp.float32
        )
    return species


def speciate(cell_block, stiff_mask, mixing, mixing_inverse, affinity, mineral):
    target = cell_block.reshape(NC, -1)
    flat_mask = stiff_mask.reshape(-1) > 0
    species = jnp.zeros_like(target)
    species = newton_steps(species, target, NEWT, False, mixing, mixing_inverse, affinity, mineral)
    stiffer = newton_steps(species, target, STIFF, True, mixing, mixing_inverse, affinity, mineral)
    species = jnp.where(flat_mask[None, :], stiffer, species)
    return species.reshape(cell_block.shape)


def by_rows(
    concentration,
    face_rate,
    face_flag,
    retardation,
    dispersion,
    mixing,
    mixing_inverse,
    affinity,
    mineral,
    stiff_mask,
):
    weight_plus, weight_minus = face_weights(face_rate, face_flag)
    rim_weights = jnp.stack([weight_plus[1, :, -1], weight_minus[1, :, -1]])
    left_rims = shifted(rim_weights, "space", 1)
    side_plus = jnp.concatenate([left_rims[0][:, None], weight_plus[1, :, :-1]], axis=1)
    side_minus = jnp.concatenate([left_rims[1][:, None], weight_minus[1, :, :-1]], axis=1)
    down_plus = shift_down(weight_plus[0], 0)
    down_minus = shift_down(weight_minus[0], 0)
    centre = down_minus + weight_plus[0] + side_minus + weight_plus[1]
    coefficients = jnp.stack([down_plus, weight_minus[0], side_plus, weight_minus[1], centre])
    retard_all = jnp.repeat(retardation, NZ)
    spread_all = jnp.repeat(dispersion, NZ)
    rows_held = stiff_mask.shape[1]
    row_start = lax.axis_index("comp") * rows_held
    cell_coefficients = lax.dynamic_slice_in_dim(coefficients, row_start, rows_held, 1)
    retard_planes = retard_all[:, None, None]
    spread_planes = spread_all[:, None, None]
    cell_block = lax.all_to_all(concentration, "comp", split_axis=1, concat_axis=0, tiled=True)
    for step_index in range(STEPS):
        padded = extended(cell_block, (("comp", 1), ("space", 2)), 1)
        cell_block = advance(
            cell_block,
            padded[:, :-2, 1:-1],
            padded[:, 2:, 1:-1],
            padded[:, 1:-1, :-2],
            padded[:, 1:-1, 2:],
            cell_coefficients,
            retard_planes,
            spread_planes,
        )
        cell_block = speciate(cell_block, stiff_mask, mixing, mixing_inverse, affinity, mineral)
    return lax.all_to_all(cell_block, "comp", split_axis=0, concat_axis=1, tiled=True)


TILE = 8
LANES = 128
VMEM_LIMIT = 24 * 1024 * 1024
MOST_VMEM = 60 * 1024 * 1024


def whole_spec():
    return pl.BlockSpec(memory_space=pltpu.VMEM)


def any_spec():
    return pl.BlockSpec(memory_space=pl.ANY)


def hbm_spec():
    return pl.BlockSpec(memory_space=pltpu.HBM)


def split(value):
    high = value.astype(jnp.bfloat16)
    return high, (value - high.astype(jnp.float32)).astype(jnp.bfloat16)


def gather_columns(columns, rows):
    lane_at = lax.broadcasted_iota(jnp.int32, (rows, LANES), 1)
    gathered = jnp.zeros((rows, LANES), jnp.float32)
    for lane, column in enumerate(columns):
        gathered = jnp.where(lane_at == lane, jnp.broadcast_to(column, (rows, LANES)), gathered)
    return gathered


def bands(rows, cols):
    return -(-rows * LANES // (TILE * cols)) * TILE


def band_spots(rows, cols):
    wide = cols // LANES
    return [
        (group, group // wide * TILE, group % wide * LANES) for group in range(rows // TILE)
    ]


def pack_kernel(layer, plane_ref, mask_ref, *refs):
    if layer:
        (low_ref, high_ref), refs = refs[:2], refs[2:]
    else:
        (rate_ref, flag_ref), refs = refs[:2], refs[2:]
    refs, (mask_part, first_ref, last_ref, mask_sems, sems) = refs[:-5], refs[-5:]
    if layer:
        out_refs = refs
    else:
        out_refs, edge_ref = refs[:-1], refs[-1]
    ranks = len(out_refs)
    planes, rows, cols = plane_ref.shape
    levels, block, _ = mask_ref.shape
    held = planes // levels
    me = lax.axis_index("comp")
    copies, masks = [], []

    def start(source, target):
        copies.append(pltpu.make_async_copy(source, target, sems.at[len(copies)]))
        copies[-1].start()

    if not layer:
        start(plane_ref.at[:, :, pl.ds(0, LANES)], first_ref)
        start(plane_ref.at[:, :, pl.ds(cols - LANES, LANES)], last_ref)
    for q, out_ref in enumerate(out_refs):
        at = lax.rem(me + q, ranks) * (levels // ranks) + layer
        masks.append(pltpu.make_async_copy(mask_ref.at[at], mask_part.at[q], mask_sems.at[q]))
        masks[-1].start()
        for index in range(held):
            start(plane_ref.at[index * levels + at], out_ref.at[pl.ds(index * rows, rows)])
    if layer:
        lane_at = lax.broadcasted_iota(jnp.int32, (rows, LANES), 1)
        sides = jnp.where(lane_at < planes, high_ref[...], low_ref[...])
        for group, row, lane in band_spots(rows, cols):
            part = sides[group * TILE : (group + 1) * TILE]
            row += held * rows + block
            for out_ref in out_refs:
                out_ref[row : row + TILE, lane : lane + LANES] = part
    else:
        copies[0].wait()
        copies[1].wait()
        end = slice(cols - LANES, cols)
        weight_plus, weight_minus = face_weights(rate_ref[1, :, end], flag_ref[1, :, end])
        columns = [first_ref[plane][:, :1] for plane in range(planes)]
        columns += [last_ref[plane][:, LANES - 1 :] for plane in range(planes)]
        columns += [weight_plus[:, LANES - 1 :], weight_minus[:, LANES - 1 :]]
        edge_ref[...] = gather_columns(columns, rows)
    for q, out_ref in enumerate(out_refs):
        masks[q].wait()
        out_ref[held * rows : held * rows + block, :] = mask_part[q].astype(jnp.float32)
    for copy in copies[0 if layer else 2 :]:
        copy.wait()


def pack(concentration, stiff_mask, layer, ranks, others):
    planes, rows, cols = concentration.shape
    held = planes // NZ
    block = stiff_mask.shape[1]
    extra = block + (bands(rows, cols) if layer else 0)
    message = jax.ShapeDtypeStruct((held * rows + extra, cols), jnp.float32)
    out_shape = [message] * ranks
    if not layer:
        out_shape.append(jax.ShapeDtypeStruct((rows, LANES), jnp.float32))
    results = pl.pallas_call(
        functools.partial(pack_kernel, layer),
        out_shape=out_shape,
        in_specs=[hbm_spec()] * 2 + [whole_spec()] * 2,
        out_specs=[whole_spec()] * len(out_shape),
        scratch_shapes=[
            pltpu.VMEM((ranks, block, cols), jnp.int32),
            pltpu.VMEM((planes, rows, LANES), jnp.float32),
            pltpu.VMEM((planes, rows, LANES), jnp.float32),
            pltpu.SemaphoreType.DMA((ranks,)),
            pltpu.SemaphoreType.DMA((ranks * held + 2,)),
        ],
        compiler_params=pltpu.CompilerParams(vmem_limit_bytes=VMEM_LIMIT if layer else MOST_VMEM),
        cost_estimate=pl.CostEstimate(flops=0, bytes_accessed=0, transcendentals=0),
        name="pack",
    )(concentration, stiff_mask, *others)
    return list(results[:ranks]), results[ranks:]


def edges_kernel(held, *refs):
    half = (len(refs) - 4) // 2
    low_refs, high_refs, (rate_ref, flag_ref, _, out_ref) = refs[:half], refs[half:-4], refs[-4:]
    rows = rate_ref.shape[1]
    weight_plus, weight_minus = face_weights(rate_ref[1], flag_ref[1])
    spots = [slice(index * rows, (index + 1) * rows) for index in range(held)]
    columns = [ref[spot, :][:, :1] for ref in low_refs for spot in spots]
    columns += [ref[spot, :][:, LANES - 1 :] for ref in high_refs for spot in spots]
    columns += [weight_plus[:, LANES - 1 :], weight_minus[:, LANES - 1 :]]
    out_ref[...] = gather_columns(columns, rows)


def edges_of(values, face_rate, face_flag, after):
    rows, cols = face_rate.shape[1:]
    last = cols // LANES - 1
    size = values[0].shape[0]
    low = pl.BlockSpec((size, LANES), lambda i: (0, 0))
    high = pl.BlockSpec((size, LANES), lambda i: (0, last))
    face = pl.BlockSpec((2, rows, LANES), lambda i: (0, 0, last))
    return pl.pallas_call(
        functools.partial(edges_kernel, size // rows),
        grid=(1,),
        out_shape=jax.ShapeDtypeStruct((rows, LANES), jnp.float32),
        in_specs=[low] * len(values) + [high] * len(values) + [face, face, hbm_spec()],
        out_specs=pl.BlockSpec((rows, LANES), lambda i: (0, 0)),
        compiler_params=pltpu.CompilerParams(vmem_limit_bytes=VMEM_LIMIT),
        cost_estimate=pl.CostEstimate(flops=0, bytes_accessed=0, transcendentals=0),
        name="edges",
    )(*values, *values, face_rate, face_flag, after)


def spread_kernel(ranks, mixing_ref, inverse_ref, affinity_ref, mineral_ref, *refs):
    _, first_ref, both_ref, ratio_ref = refs
    components = mixing_ref.shape[0]
    stacked = components * TILE
    held = components // ranks
    me = lax.axis_index("comp")

    def dot(left, right):
        return jnp.dot(left, right, precision=highest, preferred_element_type=jnp.float32)

    def pick(shape, stacked_dim):
        at = lax.broadcasted_iota(jnp.int32, shape, stacked_dim) // TILE
        component = lax.rem(me + ranks - at // held, ranks) * held + lax.rem(at, held)
        held_at = lax.broadcasted_iota(jnp.int32, shape, 1 - stacked_dim)
        return jnp.where(component == held_at, 1.0, 0.0)

    rows = pick((stacked, components), 0)
    cols = pick((components, stacked), 1)
    inner = (stacked, stacked)
    same = lax.rem(lax.broadcasted_iota(jnp.int32, inner, 0), TILE) == lax.rem(
        lax.broadcasted_iota(jnp.int32, inner, 1), TILE
    )

    def spread(matrix):
        return jnp.where(same, dot(dot(rows, matrix), cols), 0.0)

    inverse = inverse_ref[...]
    square = (components, components)
    unit = jnp.where(
        lax.broadcasted_iota(jnp.int32, square, 0) == lax.broadcasted_iota(jnp.int32, square, 1),
        1.0,
        0.0,
    )
    blend = unit - dot(inverse, mixing_ref[...])
    high, low = split(spread(inverse))
    first_ref[...] = jnp.concatenate([high, low, high], axis=1)
    high, low = split(
        jnp.concatenate([spread(blend), spread(-inverse * affinity_ref[...])], axis=1)
    )
    both_ref[...] = jnp.concatenate([high, low, high], axis=1)
    ratio = jnp.sum(rows * (mineral_ref[...] / affinity_ref[...]), axis=1, keepdims=True)
    ratio_ref[...] = jnp.broadcast_to(ratio, (stacked, LANES))


def spread_parameters(ranks, mixing, mixing_inverse, affinity, mineral, after):
    components = mixing.shape[0]
    stacked = components * TILE
    return pl.pallas_call(
        functools.partial(spread_kernel, ranks),
        out_shape=[
            jax.ShapeDtypeStruct((stacked, 3 * stacked), jnp.bfloat16),
            jax.ShapeDtypeStruct((stacked, 6 * stacked), jnp.bfloat16),
            jax.ShapeDtypeStruct((stacked, LANES), jnp.float32),
        ],
        in_specs=[whole_spec()] * 4 + [any_spec()],
        out_specs=[whole_spec()] * 3,
        compiler_params=pltpu.CompilerParams(vmem_limit_bytes=VMEM_LIMIT),
        cost_estimate=pl.CostEstimate(flops=0, bytes_accessed=0, transcendentals=0),
        name="spread_parameters",
    )(mixing, mixing_inverse, affinity.reshape(1, -1), mineral.reshape(1, -1), after)


def step_kernel(pieces, layer, is_first, with_rim, spread_ref, retard_ref, *refs):
    value_refs, refs = refs[:pieces], refs[pieces:]
    (low_ref, high_ref, rate_ref, flag_ref, ratio_ref, first_ref, both_ref), refs = (
        refs[:7],
        refs[7:],
    )
    if not is_first:
        stiff_ref, refs = refs[0], refs[1:]
    out_refs, refs = refs[:pieces], refs[pieces:]
    if with_rim:
        rim_ref, refs = refs[0], refs[1:]
    if is_first:
        stiff_ref, refs = refs[0], refs[1:]
    offset_ref, species_ref, plain_ref = refs
    groups, stacked, cols = species_ref.shape
    rows = groups * TILE
    components = stacked // TILE
    held = components // pieces
    me = lax.axis_index("comp")
    ranks = [lax.rem(me + pieces - q, pieces) for q in range(pieces)]
    row_at = lax.broadcasted_iota(jnp.int32, (rows, cols), 0)
    col_at = lax.broadcasted_iota(jnp.int32, (rows, cols), 1)

    def product(weights, parts):
        highs, lows = zip(*[split(part) for part in parts])
        operand = jnp.concatenate(highs + highs + lows, axis=0)
        return jnp.dot(weights[...], operand, preferred_element_type=jnp.float32)

    weight_plus, weight_minus = face_weights(rate_ref[...], flag_ref[...])

    def column(side, at):
        return jnp.broadcast_to(side[:, at : at + 1], (rows, cols))

    def from_lower_row(value):
        return jnp.where(row_at == 0, 0.0, pltpu.roll(value, 1, 0))

    def from_upper_row(value):
        return jnp.where(row_at == rows - 1, 0.0, pltpu.roll(value, rows - 1, 0))

    def from_lower_col(value, edge):
        return jnp.where(col_at == 0, edge, pltpu.roll(value, 1, 1))

    def from_upper_col(value, edge):
        return jnp.where(col_at == cols - 1, edge, pltpu.roll(value, cols - 1, 1))

    block = rows // pieces
    low_side, high_side = low_ref[...], high_ref[...]
    rim_at = 2 * components
    sides = [(low_side, components + at, high_side, at) for at in range(components)]
    if is_first and layer:
        sides = []
        rim_at = 2 * held * NZ
        turn = LANES - (me * (NZ // pieces) + layer)
        for value_ref in value_refs:
            start = held * rows + block
            side = jnp.concatenate(
                [
                    value_ref[start + row : start + row + TILE, lane : lane + LANES]
                    for _, row, lane in band_spots(rows, cols)
                ]
            )
            if not sides:
                low_side = side
            side = pltpu.roll(side, turn, 1)
            for index in range(held):
                sides.append((side, (held + index) * NZ, side, index * NZ))
    down_plus = from_lower_row(weight_plus[0])
    down_minus = from_lower_row(weight_minus[0])
    side_plus = from_lower_col(weight_plus[1], column(low_side, rim_at))
    side_minus = from_lower_col(weight_minus[1], column(low_side, rim_at + 1))
    centre = down_minus + weight_plus[0] + side_minus + weight_plus[1]
    for at, (low_side, low_at, high_side, high_at) in enumerate(sides):
        q, index = divmod(at, held)
        value = value_refs[q][index * rows : (index + 1) * rows, :]
        component = ranks[q] * held + index
        spread = spread_ref[component]
        retard = 1.0 / jnp.full((rows, cols), retard_ref[component], jnp.float32)
        change = (
            (down_plus + spread) * from_lower_row(value)
            + (weight_minus[0] + spread) * from_upper_row(value)
            + (side_plus + spread) * from_lower_col(value, column(low_side, low_at))
            + (weight_minus[1] + spread) * from_upper_col(value, column(high_side, high_at))
            - (centre + 4.0 * spread) * value
        )
        value = value + change * retard
        for group in range(groups):
            offset_ref[group, at * TILE : (at + 1) * TILE, :] = value[
                group * TILE : (group + 1) * TILE
            ]

    for group in range(groups):
        offset = product(first_ref, [offset_ref[group]])
        offset_ref[group] = offset
        species_ref[group] = offset

    def plain_step(_, carry):
        for group in range(groups):
            species = species_ref[group]
            species_ref[group] = offset_ref[group] + product(both_ref, [species, jnp.tanh(species)])
        return carry

    lax.fori_loop(0, NEWT - 1, plain_step, 0)
    plain_ref[...] = species_ref[...]
    ratio = jnp.concatenate([ratio_ref[...]] * (cols // LANES), axis=1)

    def stiff_step(_, carry):
        for group in range(groups):
            species = species_ref[group]
            reaction = jnp.tanh(species) + ratio * jnp.tanh(species + species)
            species_ref[group] = offset_ref[group] + product(both_ref, [species, reaction])
        return carry

    lax.fori_loop(0, STIFF, stiff_step, 0)
    if is_first:
        for rank, value_ref in zip(ranks, value_refs):
            spot = pl.ds(pl.multiple_of(rank * block, TILE), block)
            stiff_ref[spot, :] = value_ref[held * rows : held * rows + block, :]
    for group in range(groups):
        spot = slice(group * TILE, (group + 1) * TILE)
        stiff = stiff_ref[spot, :] > 0.0
        for at in range(components):
            lane = slice(at * TILE, (at + 1) * TILE)
            start = at % held * rows + group * TILE
            out_refs[at // held][start : start + TILE, :] = jnp.where(
                stiff, species_ref[group, lane, :], plain_ref[group, lane, :]
            )
    if with_rim:
        edges = [ref[i * rows : (i + 1) * rows, :] for ref in out_refs for i in range(held)]
        columns = [value[:, :1] for value in edges] + [value[:, cols - 1 :] for value in edges]
        columns += [weight_plus[1][:, cols - 1 :], weight_minus[1][:, cols - 1 :]]
        rim_ref[...] = gather_columns(columns, rows)


def layer_step(values, stiff, low, high, shared, layer, with_rim):
    dispersion, retardation, face_rate, face_flag, ratio, first, both = shared
    pieces = len(values)
    rows, cols = face_rate.shape[1:]
    groups = rows // TILE
    stacked = ratio.shape[0]
    components = stacked // TILE
    scalar = pl.BlockSpec(memory_space=pltpu.SMEM)
    plane = jax.ShapeDtypeStruct((components // pieces * rows, cols), jnp.float32)
    out_shape = [plane] * pieces
    if with_rim:
        out_shape.append(jax.ShapeDtypeStruct((rows, LANES), jnp.float32))
    if stiff is None:
        out_shape.append(jax.ShapeDtypeStruct((rows, cols), jnp.float32))
    field = pltpu.VMEM((groups, stacked, cols), jnp.float32)
    cells = rows * cols
    operands = [dispersion, retardation, *values, low, high, face_rate, face_flag]
    operands += [ratio, first, both]
    if stiff is not None:
        operands.append(stiff)
    results = pl.pallas_call(
        functools.partial(step_kernel, pieces, layer, stiff is None, with_rim),
        out_shape=out_shape,
        in_specs=[scalar, scalar] + [whole_spec()] * (len(operands) - 2),
        out_specs=[whole_spec()] * len(out_shape),
        scratch_shapes=[field, field, field],
        compiler_params=pltpu.CompilerParams(vmem_limit_bytes=VMEM_LIMIT),
        cost_estimate=pl.CostEstimate(flops=0, bytes_accessed=0, transcendentals=0),
        name="layer_step",
    )(*operands)
    values, results = results[:pieces], results[pieces:]
    rims = results[0] if with_rim else None
    return values, (results[-1] if stiff is None else stiff), rims


def by_layers(
    concentration,
    face_rate,
    face_flag,
    retardation,
    dispersion,
    mixing,
    mixing_inverse,
    affinity,
    mineral,
    stiff_mask,
):
    ranks = lax.axis_size("comp")
    me = lax.axis_index("comp")
    planes, rows, cols = concentration.shape
    held = planes // NZ
    layers = NZ // ranks

    def send(value, by):
        return lax.ppermute(value, "comp", [(i, (i + by) % ranks) for i in range(ranks)])

    arrived, others = [], (face_rate, face_flag)
    for layer in range(layers):
        messages, edges = pack(concentration, stiff_mask, layer, ranks, others)
        for q in range(1, ranks if layer else 0):
            messages[q], arrived[-1][q] = lax.optimization_barrier((messages[q], arrived[-1][q]))
        arrived.append([send(part, q) if q else part for q, part in enumerate(messages)])
        if edges:
            others = (shifted(edges[0], "space", 1), shifted(edges[0], "space", -1))
        after = messages[0]

    first, both, ratio = spread_parameters(ranks, mixing, mixing_inverse, affinity, mineral, after)
    shared = (dispersion, retardation, face_rate, face_flag, ratio, first, both)

    result = jnp.zeros((held, NZ, rows, cols), jnp.float32)
    for layer in range(layers):
        values, stiff = arrived[layer], None
        rims = None if layer else edges_of(values, face_rate, face_flag, after)
        for step in range(STEPS):
            if rims is None:
                low, high = others
            else:
                low, high = shifted(rims, "space", 1), shifted(rims, "space", -1)
            values, stiff, rims = layer_step(
                values, stiff, low, high, shared, layer, step < STEPS - 1
            )
        for q in range(ranks):
            piece = send(values[q], -q) if q else values[q]
            result = lax.dynamic_update_slice(
                result,
                piece.reshape(held, 1, rows, cols),
                (0, (me + q) % ranks * layers + layer, 0, 0),
            )
    return result.reshape(planes, rows, cols)


def shards(concentration, face_rate, face_flag, *parameters):
    ranks = lax.axis_size("comp")
    planes, rows, cols = concentration.shape
    whole = NZ % ranks == 0 and planes % NZ == 0
    narrow = 2 * max(NC, planes) + 2 <= LANES
    even = rows % (ranks * TILE) == 0 and cols % LANES == 0
    plan = by_layers if whole and narrow and even else by_rows
    return plan(concentration, face_rate, face_flag, *parameters)


def solution(mesh):
    in_specs = (
        P(("real", "comp"), None, "space"),
        P(None, "real", "space"),
        P(None, "real", "space"),
        P(),
        P(),
        P(),
        P(),
        P(),
        P(),
        P(None, ("real", "comp"), "space"),
    )
    out_specs = P(("real", "comp"), None, "space")
    return jax.shard_map(shards, mesh=mesh, in_specs=in_specs, out_specs=out_specs, check_vma=False)
```

```python
import functools

import jax
import jax.numpy as jnp
from jax import lax
from jax.experimental import pallas as pl
from jax.experimental.pallas import tpu as pltpu
from jax.sharding import PartitionSpec as P

NC = 16
NZ = 8
STEPS = 2
NEWT = 4
STIFF = 4


highest = lax.Precision.HIGHEST


def shifted(shard, axis, by):
    devices = lax.axis_size(axis)
    pairs = [(i, i + by) for i in range(devices) if 0 <= i + by < devices]
    return lax.ppermute(shard, axis, pairs)


def extended(block, sides, width):
    for axis, dim in sides:
        count = lax.axis_size(axis)
        forward = [(i, i + 1) for i in range(count - 1)]
        backward = [(target, source) for source, target in forward]
        low = lax.ppermute(
            lax.slice_in_dim(block, block.shape[dim] - width, None, axis=dim), axis, forward
        )
        high = lax.ppermute(lax.slice_in_dim(block, 0, width, axis=dim), axis, backward)
        block = jnp.concatenate([low, block, high], axis=dim)
    return block


def shift_down(values, axis_index):
    size_along = values.shape[axis_index]
    zero_row = jnp.zeros_like(lax.slice_in_dim(values, 0, 1, axis=axis_index))
    kept = lax.slice_in_dim(values, 0, size_along - 1, axis=axis_index)
    return jnp.concatenate([zero_row, kept], axis=axis_index)


def face_weights(face_rate, face_flag):
    flag_values = face_flag.astype(jnp.float32)
    weight_plus = face_rate * flag_values
    weight_minus = face_rate * (1.0 - flag_values)
    return (weight_plus, weight_minus)


def advance(
    values, lower_row, upper_row, lower_col, upper_col, coefficients, retard_planes, spread_planes
):
    divergence = (
        coefficients[0] * lower_row
        + coefficients[1] * upper_row
        + coefficients[2] * lower_col
        + coefficients[3] * upper_col
        - coefficients[4] * values
    )
    laplace = lower_row + upper_row + lower_col + upper_col - 4.0 * values
    return values + (divergence + spread_planes * laplace) / retard_planes


def residual_of(species, target, mixing, affinity, mineral, stiff):
    total = jnp.dot(
        mixing, species, precision=highest, preferred_element_type=jnp.float32
    ) + affinity[:, None] * jnp.tanh(species)
    if stiff:
        total = total + mineral[:, None] * jnp.tanh(2.0 * species)
    return total - target


def newton_steps(species, target, repeats, stiff, mixing, mixing_inverse, affinity, mineral):
    for iteration in range(repeats):
        update = residual_of(species, target, mixing, affinity, mineral, stiff)
        species = species - jnp.dot(
            mixing_inverse, update, precision=highest, preferred_element_type=jnp.float32
        )
    return species


def speciate(cell_block, stiff_mask, mixing, mixing_inverse, affinity, mineral):
    target = cell_block.reshape(NC, -1)
    flat_mask = stiff_mask.reshape(-1) > 0
    species = jnp.zeros_like(target)
    species = newton_steps(species, target, NEWT, False, mixing, mixing_inverse, affinity, mineral)
    stiffer = newton_steps(species, target, STIFF, True, mixing, mixing_inverse, affinity, mineral)
    species = jnp.where(flat_mask[None, :], stiffer, species)
    return species.reshape(cell_block.shape)


def by_rows(
    concentration,
    face_rate,
    face_flag,
    retardation,
    dispersion,
    mixing,
    mixing_inverse,
    affinity,
    mineral,
    stiff_mask,
):
    weight_plus, weight_minus = face_weights(face_rate, face_flag)
    rim_weights = jnp.stack([weight_plus[1, :, -1], weight_minus[1, :, -1]])
    left_rims = shifted(rim_weights, "space", 1)
    side_plus = jnp.concatenate([left_rims[0][:, None], weight_plus[1, :, :-1]], axis=1)
    side_minus = jnp.concatenate([left_rims[1][:, None], weight_minus[1, :, :-1]], axis=1)
    down_plus = shift_down(weight_plus[0], 0)
    down_minus = shift_down(weight_minus[0], 0)
    centre = down_minus + weight_plus[0] + side_minus + weight_plus[1]
    coefficients = jnp.stack([down_plus, weight_minus[0], side_plus, weight_minus[1], centre])
    retard_all = jnp.repeat(retardation, NZ)
    spread_all = jnp.repeat(dispersion, NZ)
    rows_held = stiff_mask.shape[1]
    row_start = lax.axis_index("comp") * rows_held
    cell_coefficients = lax.dynamic_slice_in_dim(coefficients, row_start, rows_held, 1)
    retard_planes = retard_all[:, None, None]
    spread_planes = spread_all[:, None, None]
    cell_block = lax.all_to_all(concentration, "comp", split_axis=1, concat_axis=0, tiled=True)
    for step_index in range(STEPS):
        padded = extended(cell_block, (("comp", 1), ("space", 2)), 1)
        cell_block = advance(
            cell_block,
            padded[:, :-2, 1:-1],
            padded[:, 2:, 1:-1],
            padded[:, 1:-1, :-2],
            padded[:, 1:-1, 2:],
            cell_coefficients,
            retard_planes,
            spread_planes,
        )
        cell_block = speciate(cell_block, stiff_mask, mixing, mixing_inverse, affinity, mineral)
    return lax.all_to_all(cell_block, "comp", split_axis=0, concat_axis=1, tiled=True)


TILE = 8
LANES = 128
VMEM_LIMIT = 24 * 1024 * 1024
MOST_VMEM = 60 * 1024 * 1024


def whole_spec():
    return pl.BlockSpec(memory_space=pltpu.VMEM)


def any_spec():
    return pl.BlockSpec(memory_space=pl.ANY)


def hbm_spec():
    return pl.BlockSpec(memory_space=pltpu.HBM)


def split(value):
    high = value.astype(jnp.bfloat16)
    return high, (value - high.astype(jnp.float32)).astype(jnp.bfloat16)


def gather_columns(columns, rows):
    lane_at = lax.broadcasted_iota(jnp.int32, (rows, LANES), 1)
    gathered = jnp.zeros((rows, LANES), jnp.float32)
    for lane, column in enumerate(columns):
        gathered = jnp.where(lane_at == lane, jnp.broadcast_to(column, (rows, LANES)), gathered)
    return gathered


def bands(rows, cols):
    return -(-rows * LANES // (TILE * cols)) * TILE


def band_spots(rows, cols):
    wide = cols // LANES
    return [
        (group, group // wide * TILE, group % wide * LANES) for group in range(rows // TILE)
    ]


def pack_kernel(layer, plane_ref, mask_ref, *refs):
    if layer:
        (low_ref, high_ref), refs = refs[:2], refs[2:]
    else:
        (rate_ref, flag_ref), refs = refs[:2], refs[2:]
    refs, (mask_part, first_ref, last_ref, mask_sems, sems) = refs[:-5], refs[-5:]
    if layer:
        out_refs = refs
    else:
        out_refs, edge_ref = refs[:-1], refs[-1]
    ranks = len(out_refs)
    planes, rows, cols = plane_ref.shape
    levels, block, _ = mask_ref.shape
    held = planes // levels
    me = lax.axis_index("comp")
    copies, masks = [], []

    def start(source, target):
        copies.append(pltpu.make_async_copy(source, target, sems.at[len(copies)]))
        copies[-1].start()

    if not layer:
        start(plane_ref.at[:, :, pl.ds(0, LANES)], first_ref)
        start(plane_ref.at[:, :, pl.ds(cols - LANES, LANES)], last_ref)
    for q, out_ref in enumerate(out_refs):
        at = jnp.bitwise_xor(me, q) * (levels // ranks) + layer
        masks.append(pltpu.make_async_copy(mask_ref.at[at], mask_part.at[q], mask_sems.at[q]))
        masks[-1].start()
        for index in range(held):
            start(plane_ref.at[index * levels + at], out_ref.at[pl.ds(index * rows, rows)])
    if layer:
        lane_at = lax.broadcasted_iota(jnp.int32, (rows, LANES), 1)
        sides = jnp.where(lane_at < planes, high_ref[...], low_ref[...])
        for group, row, lane in band_spots(rows, cols):
            part = sides[group * TILE : (group + 1) * TILE]
            row += held * rows + block
            for out_ref in out_refs:
                out_ref[row : row + TILE, lane : lane + LANES] = part
    else:
        copies[0].wait()
        copies[1].wait()
        end = slice(cols - LANES, cols)
        weight_plus, weight_minus = face_weights(rate_ref[1, :, end], flag_ref[1, :, end])
        columns = [first_ref[plane][:, :1] for plane in range(planes)]
        columns += [last_ref[plane][:, LANES - 1 :] for plane in range(planes)]
        columns += [weight_plus[:, LANES - 1 :], weight_minus[:, LANES - 1 :]]
        edge_ref[...] = gather_columns(columns, rows)
    for q, out_ref in enumerate(out_refs):
        masks[q].wait()
        out_ref[held * rows : held * rows + block, :] = mask_part[q].astype(jnp.float32)
    for copy in copies[0 if layer else 2 :]:
        copy.wait()


def pack(concentration, stiff_mask, layer, ranks, others):
    planes, rows, cols = concentration.shape
    held = planes // NZ
    block = stiff_mask.shape[1]
    extra = block + (bands(rows, cols) if layer else 0)
    message = jax.ShapeDtypeStruct((held * rows + extra, cols), jnp.float32)
    out_shape = [message] * ranks
    if not layer:
        out_shape.append(jax.ShapeDtypeStruct((rows, LANES), jnp.float32))
    results = pl.pallas_call(
        functools.partial(pack_kernel, layer),
        out_shape=out_shape,
        in_specs=[hbm_spec()] * 2 + [whole_spec()] * 2,
        out_specs=[whole_spec()] * len(out_shape),
        scratch_shapes=[
            pltpu.VMEM((ranks, block, cols), jnp.int32),
            pltpu.VMEM((planes, rows, LANES), jnp.float32),
            pltpu.VMEM((planes, rows, LANES), jnp.float32),
            pltpu.SemaphoreType.DMA((ranks,)),
            pltpu.SemaphoreType.DMA((ranks * held + 2,)),
        ],
        compiler_params=pltpu.CompilerParams(vmem_limit_bytes=VMEM_LIMIT if layer else MOST_VMEM),
        cost_estimate=pl.CostEstimate(flops=0, bytes_accessed=0, transcendentals=0),
        name="pack",
    )(concentration, stiff_mask, *others)
    return list(results[:ranks]), results[ranks:]


def edges_kernel(held, *refs):
    half = (len(refs) - 4) // 2
    low_refs, high_refs, (rate_ref, flag_ref, _, out_ref) = refs[:half], refs[half:-4], refs[-4:]
    rows = rate_ref.shape[1]
    weight_plus, weight_minus = face_weights(rate_ref[1], flag_ref[1])
    spots = [slice(index * rows, (index + 1) * rows) for index in range(held)]
    columns = [ref[spot, :][:, :1] for ref in low_refs for spot in spots]
    columns += [ref[spot, :][:, LANES - 1 :] for ref in high_refs for spot in spots]
    columns += [weight_plus[:, LANES - 1 :], weight_minus[:, LANES - 1 :]]
    out_ref[...] = gather_columns(columns, rows)


def edges_of(values, face_rate, face_flag, after):
    rows, cols = face_rate.shape[1:]
    last = cols // LANES - 1
    size = values[0].shape[0]
    low = pl.BlockSpec((size, LANES), lambda i: (0, 0))
    high = pl.BlockSpec((size, LANES), lambda i: (0, last))
    face = pl.BlockSpec((2, rows, LANES), lambda i: (0, 0, last))
    return pl.pallas_call(
        functools.partial(edges_kernel, size // rows),
        grid=(1,),
        out_shape=jax.ShapeDtypeStruct((rows, LANES), jnp.float32),
        in_specs=[low] * len(values) + [high] * len(values) + [face, face, hbm_spec()],
        out_specs=pl.BlockSpec((rows, LANES), lambda i: (0, 0)),
        compiler_params=pltpu.CompilerParams(vmem_limit_bytes=VMEM_LIMIT),
        cost_estimate=pl.CostEstimate(flops=0, bytes_accessed=0, transcendentals=0),
        name="edges",
    )(*values, *values, face_rate, face_flag, after)


def spread_kernel(ranks, mixing_ref, inverse_ref, affinity_ref, mineral_ref, *refs):
    _, first_ref, both_ref, ratio_ref = refs
    components = mixing_ref.shape[0]
    stacked = components * TILE
    held = components // ranks
    me = lax.axis_index("comp")

    def dot(left, right):
        return jnp.dot(left, right, precision=highest, preferred_element_type=jnp.float32)

    def pick(shape, stacked_dim):
        at = lax.broadcasted_iota(jnp.int32, shape, stacked_dim) // TILE
        component = jnp.bitwise_xor(me, at // held) * held + lax.rem(at, held)
        held_at = lax.broadcasted_iota(jnp.int32, shape, 1 - stacked_dim)
        return jnp.where(component == held_at, 1.0, 0.0)

    rows = pick((stacked, components), 0)
    cols = pick((components, stacked), 1)
    inner = (stacked, stacked)
    same = lax.rem(lax.broadcasted_iota(jnp.int32, inner, 0), TILE) == lax.rem(
        lax.broadcasted_iota(jnp.int32, inner, 1), TILE
    )

    def spread(matrix):
        return jnp.where(same, dot(dot(rows, matrix), cols), 0.0)

    inverse = inverse_ref[...]
    square = (components, components)
    unit = jnp.where(
        lax.broadcasted_iota(jnp.int32, square, 0) == lax.broadcasted_iota(jnp.int32, square, 1),
        1.0,
        0.0,
    )
    blend = unit - dot(inverse, mixing_ref[...])
    high, low = split(spread(inverse))
    first_ref[...] = jnp.concatenate([high, low, high], axis=1)
    high, low = split(
        jnp.concatenate([spread(blend), spread(-inverse * affinity_ref[...])], axis=1)
    )
    both_ref[...] = jnp.concatenate([high, low, high], axis=1)
    ratio = jnp.sum(rows * (mineral_ref[...] / affinity_ref[...]), axis=1, keepdims=True)
    ratio_ref[...] = jnp.broadcast_to(ratio, (stacked, LANES))


def spread_parameters(ranks, mixing, mixing_inverse, affinity, mineral, after):
    components = mixing.shape[0]
    stacked = components * TILE
    return pl.pallas_call(
        functools.partial(spread_kernel, ranks),
        out_shape=[
            jax.ShapeDtypeStruct((stacked, 3 * stacked), jnp.bfloat16),
            jax.ShapeDtypeStruct((stacked, 6 * stacked), jnp.bfloat16),
            jax.ShapeDtypeStruct((stacked, LANES), jnp.float32),
        ],
        in_specs=[whole_spec()] * 4 + [any_spec()],
        out_specs=[whole_spec()] * 3,
        compiler_params=pltpu.CompilerParams(vmem_limit_bytes=VMEM_LIMIT),
        cost_estimate=pl.CostEstimate(flops=0, bytes_accessed=0, transcendentals=0),
        name="spread_parameters",
    )(mixing, mixing_inverse, affinity.reshape(1, -1), mineral.reshape(1, -1), after)


def step_kernel(pieces, layer, is_first, with_rim, spread_ref, retard_ref, *refs):
    value_refs, refs = refs[:pieces], refs[pieces:]
    (low_ref, high_ref, rate_ref, flag_ref, ratio_ref, first_ref, both_ref), refs = (
        refs[:7],
        refs[7:],
    )
    if not is_first:
        stiff_ref, refs = refs[0], refs[1:]
    out_refs, refs = refs[:pieces], refs[pieces:]
    if with_rim:
        rim_ref, refs = refs[0], refs[1:]
    if is_first:
        stiff_ref, refs = refs[0], refs[1:]
    offset_ref, species_ref, plain_ref = refs
    groups, stacked, cols = species_ref.shape
    rows = groups * TILE
    components = stacked // TILE
    held = components // pieces
    me = lax.axis_index("comp")
    ranks = [jnp.bitwise_xor(me, q) for q in range(pieces)]
    row_at = lax.broadcasted_iota(jnp.int32, (rows, cols), 0)
    col_at = lax.broadcasted_iota(jnp.int32, (rows, cols), 1)

    def product(weights, parts):
        highs, lows = zip(*[split(part) for part in parts])
        operand = jnp.concatenate(highs + highs + lows, axis=0)
        return jnp.dot(weights[...], operand, preferred_element_type=jnp.float32)

    weight_plus, weight_minus = face_weights(rate_ref[...], flag_ref[...])

    def column(side, at):
        return jnp.broadcast_to(side[:, at : at + 1], (rows, cols))

    def from_lower_row(value):
        return jnp.where(row_at == 0, 0.0, pltpu.roll(value, 1, 0))

    def from_upper_row(value):
        return jnp.where(row_at == rows - 1, 0.0, pltpu.roll(value, rows - 1, 0))

    def from_lower_col(value, edge):
        return jnp.where(col_at == 0, edge, pltpu.roll(value, 1, 1))

    def from_upper_col(value, edge):
        return jnp.where(col_at == cols - 1, edge, pltpu.roll(value, cols - 1, 1))

    block = rows // pieces
    low_side, high_side = low_ref[...], high_ref[...]
    rim_at = 2 * components
    sides = [(low_side, components + at, high_side, at) for at in range(components)]
    if is_first and layer:
        sides = []
        rim_at = 2 * held * NZ
        turn = LANES - (me * (NZ // pieces) + layer)
        for value_ref in value_refs:
            start = held * rows + block
            side = jnp.concatenate(
                [
                    value_ref[start + row : start + row + TILE, lane : lane + LANES]
                    for _, row, lane in band_spots(rows, cols)
                ]
            )
            if not sides:
                low_side = side
            side = pltpu.roll(side, turn, 1)
            for index in range(held):
                sides.append((side, (held + index) * NZ, side, index * NZ))
    down_plus = from_lower_row(weight_plus[0])
    down_minus = from_lower_row(weight_minus[0])
    side_plus = from_lower_col(weight_plus[1], column(low_side, rim_at))
    side_minus = from_lower_col(weight_minus[1], column(low_side, rim_at + 1))
    centre = down_minus + weight_plus[0] + side_minus + weight_plus[1]
    for at, (low_side, low_at, high_side, high_at) in enumerate(sides):
        q, index = divmod(at, held)
        value = value_refs[q][index * rows : (index + 1) * rows, :]
        component = ranks[q] * held + index
        spread = spread_ref[component]
        retard = 1.0 / jnp.full((rows, cols), retard_ref[component], jnp.float32)
        change = (
            (down_plus + spread) * from_lower_row(value)
            + (weight_minus[0] + spread) * from_upper_row(value)
            + (side_plus + spread) * from_lower_col(value, column(low_side, low_at))
            + (weight_minus[1] + spread) * from_upper_col(value, column(high_side, high_at))
            - (centre + 4.0 * spread) * value
        )
        value = value + change * retard
        for group in range(groups):
            offset_ref[group, at * TILE : (at + 1) * TILE, :] = value[
                group * TILE : (group + 1) * TILE
            ]

    for group in range(groups):
        offset = product(first_ref, [offset_ref[group]])
        offset_ref[group] = offset
        species_ref[group] = offset

    def plain_step(_, carry):
        for group in range(groups):
            species = species_ref[group]
            species_ref[group] = offset_ref[group] + product(both_ref, [species, jnp.tanh(species)])
        return carry

    lax.fori_loop(0, NEWT - 1, plain_step, 0)
    plain_ref[...] = species_ref[...]
    ratio = jnp.concatenate([ratio_ref[...]] * (cols // LANES), axis=1)

    def stiff_step(_, carry):
        for group in range(groups):
            species = species_ref[group]
            reaction = jnp.tanh(species) + ratio * jnp.tanh(species + species)
            species_ref[group] = offset_ref[group] + product(both_ref, [species, reaction])
        return carry

    lax.fori_loop(0, STIFF, stiff_step, 0)
    if is_first:
        for rank, value_ref in zip(ranks, value_refs):
            spot = pl.ds(pl.multiple_of(rank * block, TILE), block)
            stiff_ref[spot, :] = value_ref[held * rows : held * rows + block, :]
    for group in range(groups):
        spot = slice(group * TILE, (group + 1) * TILE)
        stiff = stiff_ref[spot, :] > 0.0
        for at in range(components):
            lane = slice(at * TILE, (at + 1) * TILE)
            start = at % held * rows + group * TILE
            out_refs[at // held][start : start + TILE, :] = jnp.where(
                stiff, species_ref[group, lane, :], plain_ref[group, lane, :]
            )
    if with_rim:
        edges = [ref[i * rows : (i + 1) * rows, :] for ref in out_refs for i in range(held)]
        columns = [value[:, :1] for value in edges] + [value[:, cols - 1 :] for value in edges]
        columns += [weight_plus[1][:, cols - 1 :], weight_minus[1][:, cols - 1 :]]
        rim_ref[...] = gather_columns(columns, rows)


def layer_step(values, stiff, low, high, shared, layer, with_rim):
    dispersion, retardation, face_rate, face_flag, ratio, first, both = shared
    pieces = len(values)
    rows, cols = face_rate.shape[1:]
    groups = rows // TILE
    stacked = ratio.shape[0]
    components = stacked // TILE
    scalar = pl.BlockSpec(memory_space=pltpu.SMEM)
    plane = jax.ShapeDtypeStruct((components // pieces * rows, cols), jnp.float32)
    out_shape = [plane] * pieces
    if with_rim:
        out_shape.append(jax.ShapeDtypeStruct((rows, LANES), jnp.float32))
    if stiff is None:
        out_shape.append(jax.ShapeDtypeStruct((rows, cols), jnp.float32))
    field = pltpu.VMEM((groups, stacked, cols), jnp.float32)
    cells = rows * cols
    operands = [dispersion, retardation, *values, low, high, face_rate, face_flag]
    operands += [ratio, first, both]
    if stiff is not None:
        operands.append(stiff)
    results = pl.pallas_call(
        functools.partial(step_kernel, pieces, layer, stiff is None, with_rim),
        out_shape=out_shape,
        in_specs=[scalar, scalar] + [whole_spec()] * (len(operands) - 2),
        out_specs=[whole_spec()] * len(out_shape),
        scratch_shapes=[field, field, field],
        compiler_params=pltpu.CompilerParams(vmem_limit_bytes=VMEM_LIMIT),
        cost_estimate=pl.CostEstimate(flops=0, bytes_accessed=0, transcendentals=0),
        name="layer_step",
    )(*operands)
    values, results = results[:pieces], results[pieces:]
    rims = results[0] if with_rim else None
    return values, (results[-1] if stiff is None else stiff), rims


def by_layers(
    concentration,
    face_rate,
    face_flag,
    retardation,
    dispersion,
    mixing,
    mixing_inverse,
    affinity,
    mineral,
    stiff_mask,
):
    ranks = lax.axis_size("comp")
    me = lax.axis_index("comp")
    planes, rows, cols = concentration.shape
    held = planes // NZ
    layers = NZ // ranks

    def send(value, by):
        return lax.ppermute(value, "comp", [(i, i ^ by) for i in range(ranks)]) if by else value

    arrived, others = [], (face_rate, face_flag)
    for layer in range(layers):
        messages, edges = pack(concentration, stiff_mask, layer, ranks, others)
        if layer:
            messages, arrived[-1] = lax.optimization_barrier((messages, arrived[-1]))
        arrived.append([send(part, q) for q, part in enumerate(messages)])
        if edges:
            others = (shifted(edges[0], "space", 1), shifted(edges[0], "space", -1))
        after = messages[0]

    first, both, ratio = spread_parameters(ranks, mixing, mixing_inverse, affinity, mineral, after)
    shared = (dispersion, retardation, face_rate, face_flag, ratio, first, both)

    result = jnp.zeros((held, NZ, rows, cols), jnp.float32)
    for layer in range(layers):
        values, stiff = arrived[layer], None
        rims = None if layer else edges_of(values, face_rate, face_flag, after)
        for step in range(STEPS):
            if rims is None:
                low, high = others
            else:
                low, high = shifted(rims, "space", 1), shifted(rims, "space", -1)
            values, stiff, rims = layer_step(
                values, stiff, low, high, shared, layer, step < STEPS - 1
            )
        for q in range(ranks):
            piece = send(values[q], q)
            result = lax.dynamic_update_slice(
                result,
                piece.reshape(held, 1, rows, cols),
                (0, (me ^ q) * layers + layer, 0, 0),
            )
    return result.reshape(planes, rows, cols)


def shards(concentration, face_rate, face_flag, *parameters):
    ranks = lax.axis_size("comp")
    planes, rows, cols = concentration.shape
    whole = NZ % ranks == 0 and planes % NZ == 0 and ranks & (ranks - 1) == 0
    narrow = 2 * max(NC, planes) + 2 <= LANES
    even = rows % (ranks * TILE) == 0 and cols % LANES == 0
    plan = by_layers if whole and narrow and even else by_rows
    return plan(concentration, face_rate, face_flag, *parameters)


def solution(mesh):
    in_specs = (
        P(("real", "comp"), None, "space"),
        P(None, "real", "space"),
        P(None, "real", "space"),
        P(),
        P(),
        P(),
        P(),
        P(),
        P(),
        P(None, ("real", "comp"), "space"),
    )
    out_specs = P(("real", "comp"), None, "space")
    return jax.shard_map(shards, mesh=mesh, in_specs=in_specs, out_specs=out_specs, check_vma=False)
```

```python
import functools

import jax
import jax.numpy as jnp
from jax import lax
from jax.experimental import pallas as pl
from jax.experimental.pallas import tpu as pltpu
from jax.sharding import PartitionSpec as P

NC = 16
NZ = 8
STEPS = 2
NEWT = 4
STIFF = 4


highest = lax.Precision.HIGHEST


def shifted(shard, axis, by):
    devices = lax.axis_size(axis)
    pairs = [(i, i + by) for i in range(devices) if 0 <= i + by < devices]
    return lax.ppermute(shard, axis, pairs)


def extended(block, sides, width):
    for axis, dim in sides:
        count = lax.axis_size(axis)
        forward = [(i, i + 1) for i in range(count - 1)]
        backward = [(target, source) for source, target in forward]
        low = lax.ppermute(
            lax.slice_in_dim(block, block.shape[dim] - width, None, axis=dim), axis, forward
        )
        high = lax.ppermute(lax.slice_in_dim(block, 0, width, axis=dim), axis, backward)
        block = jnp.concatenate([low, block, high], axis=dim)
    return block


def shift_down(values, axis_index):
    size_along = values.shape[axis_index]
    zero_row = jnp.zeros_like(lax.slice_in_dim(values, 0, 1, axis=axis_index))
    kept = lax.slice_in_dim(values, 0, size_along - 1, axis=axis_index)
    return jnp.concatenate([zero_row, kept], axis=axis_index)


def face_weights(face_rate, face_flag):
    flag_values = face_flag.astype(jnp.float32)
    weight_plus = face_rate * flag_values
    weight_minus = face_rate * (1.0 - flag_values)
    return (weight_plus, weight_minus)


def advance(
    values, lower_row, upper_row, lower_col, upper_col, coefficients, retard_planes, spread_planes
):
    divergence = (
        coefficients[0] * lower_row
        + coefficients[1] * upper_row
        + coefficients[2] * lower_col
        + coefficients[3] * upper_col
        - coefficients[4] * values
    )
    laplace = lower_row + upper_row + lower_col + upper_col - 4.0 * values
    return values + (divergence + spread_planes * laplace) / retard_planes


def residual_of(species, target, mixing, affinity, mineral, stiff):
    total = jnp.dot(
        mixing, species, precision=highest, preferred_element_type=jnp.float32
    ) + affinity[:, None] * jnp.tanh(species)
    if stiff:
        total = total + mineral[:, None] * jnp.tanh(2.0 * species)
    return total - target


def newton_steps(species, target, repeats, stiff, mixing, mixing_inverse, affinity, mineral):
    for iteration in range(repeats):
        update = residual_of(species, target, mixing, affinity, mineral, stiff)
        species = species - jnp.dot(
            mixing_inverse, update, precision=highest, preferred_element_type=jnp.float32
        )
    return species


def speciate(cell_block, stiff_mask, mixing, mixing_inverse, affinity, mineral):
    target = cell_block.reshape(NC, -1)
    flat_mask = stiff_mask.reshape(-1) > 0
    species = jnp.zeros_like(target)
    species = newton_steps(species, target, NEWT, False, mixing, mixing_inverse, affinity, mineral)
    stiffer = newton_steps(species, target, STIFF, True, mixing, mixing_inverse, affinity, mineral)
    species = jnp.where(flat_mask[None, :], stiffer, species)
    return species.reshape(cell_block.shape)


def by_rows(
    concentration,
    face_rate,
    face_flag,
    retardation,
    dispersion,
    mixing,
    mixing_inverse,
    affinity,
    mineral,
    stiff_mask,
):
    weight_plus, weight_minus = face_weights(face_rate, face_flag)
    rim_weights = jnp.stack([weight_plus[1, :, -1], weight_minus[1, :, -1]])
    left_rims = shifted(rim_weights, "space", 1)
    side_plus = jnp.concatenate([left_rims[0][:, None], weight_plus[1, :, :-1]], axis=1)
    side_minus = jnp.concatenate([left_rims[1][:, None], weight_minus[1, :, :-1]], axis=1)
    down_plus = shift_down(weight_plus[0], 0)
    down_minus = shift_down(weight_minus[0], 0)
    centre = down_minus + weight_plus[0] + side_minus + weight_plus[1]
    coefficients = jnp.stack([down_plus, weight_minus[0], side_plus, weight_minus[1], centre])
    retard_all = jnp.repeat(retardation, NZ)
    spread_all = jnp.repeat(dispersion, NZ)
    rows_held = stiff_mask.shape[1]
    row_start = lax.axis_index("comp") * rows_held
    cell_coefficients = lax.dynamic_slice_in_dim(coefficients, row_start, rows_held, 1)
    retard_planes = retard_all[:, None, None]
    spread_planes = spread_all[:, None, None]
    cell_block = lax.all_to_all(concentration, "comp", split_axis=1, concat_axis=0, tiled=True)
    for step_index in range(STEPS):
        padded = extended(cell_block, (("comp", 1), ("space", 2)), 1)
        cell_block = advance(
            cell_block,
            padded[:, :-2, 1:-1],
            padded[:, 2:, 1:-1],
            padded[:, 1:-1, :-2],
            padded[:, 1:-1, 2:],
            cell_coefficients,
            retard_planes,
            spread_planes,
        )
        cell_block = speciate(cell_block, stiff_mask, mixing, mixing_inverse, affinity, mineral)
    return lax.all_to_all(cell_block, "comp", split_axis=0, concat_axis=1, tiled=True)


TILE = 8
LANES = 128
VMEM_LIMIT = 24 * 1024 * 1024
MOST_VMEM = 60 * 1024 * 1024


def whole_spec():
    return pl.BlockSpec(memory_space=pltpu.VMEM)


def any_spec():
    return pl.BlockSpec(memory_space=pl.ANY)


def hbm_spec():
    return pl.BlockSpec(memory_space=pltpu.HBM)


def pair(q, ranks):
    return (ranks - q) % ranks


def split(value):
    high = value.astype(jnp.bfloat16)
    return high, (value - high.astype(jnp.float32)).astype(jnp.bfloat16)


def gather_columns(columns, rows):
    lane_at = lax.broadcasted_iota(jnp.int32, (rows, LANES), 1)
    gathered = jnp.zeros((rows, LANES), jnp.float32)
    for lane, column in enumerate(columns):
        gathered = jnp.where(lane_at == lane, jnp.broadcast_to(column, (rows, LANES)), gathered)
    return gathered


def pack_kernel(layer, plane_ref, mask_ref, *refs):
    if not layer:
        (rate_ref, flag_ref), refs = refs[:2], refs[2:]
    refs, (part_ref, mask_part, first_ref, last_ref, mask_sems, in_sems, out_sems) = (
        refs[:-7],
        refs[-7:],
    )
    out_refs = refs[: part_ref.shape[0]]
    ranks = len(out_refs)
    planes, rows, cols = plane_ref.shape
    levels, block, _ = mask_ref.shape
    held = planes // levels
    me = lax.axis_index("comp")
    copies = []
    order = [*range(1, ranks), 0]

    def start(source, target, sem):
        copies.append(pltpu.make_async_copy(source, target, sem))
        copies[-1].start()

    for q in order:
        at = jnp.bitwise_xor(me, pair(q, ranks)) * (levels // ranks) + layer
        for index in range(held):
            spot = pl.ds(index * rows, rows)
            start(plane_ref.at[index * levels + at], part_ref.at[q, spot], in_sems.at[len(copies)])
        start(mask_ref.at[at], mask_part.at[q], mask_sems.at[q])
    arrivals = list(copies)
    if not layer:
        start(plane_ref.at[:, :, pl.ds(0, LANES)], first_ref, in_sems.at[len(copies)])
        start(
            plane_ref.at[:, :, pl.ds(cols - LANES, LANES)], last_ref, in_sems.at[len(copies)]
        )
    edges = copies[len(arrivals) :]
    copies.clear()
    for position, q in enumerate(order):
        for copy in arrivals[position * (held + 1) : (position + 1) * (held + 1)]:
            copy.wait()
        part_ref[q, held * rows :, :] = mask_part[q].astype(jnp.float32)
        start(part_ref.at[q], out_refs[q], out_sems.at[q])
    for copy in edges:
        copy.wait()
    if not layer:
        end = slice(cols - LANES, cols)
        weight_plus, weight_minus = face_weights(rate_ref[1, :, end], flag_ref[1, :, end])
        columns = [first_ref[plane][:, :1] for plane in range(planes)]
        columns += [last_ref[plane][:, LANES - 1 :] for plane in range(planes)]
        columns += [weight_plus[:, LANES - 1 :], weight_minus[:, LANES - 1 :]]
        refs[ranks][...] = gather_columns(columns, rows)
    for copy in copies:
        copy.wait()


def pack(concentration, stiff_mask, layer, ranks, faces):
    planes, rows, cols = concentration.shape
    held = planes // NZ
    block = stiff_mask.shape[1]
    size = held * rows + block
    out_shape = [jax.ShapeDtypeStruct((size, cols), jnp.float32)] * ranks
    out_specs = [any_spec()] * ranks
    if not layer:
        out_shape.append(jax.ShapeDtypeStruct((rows, LANES), jnp.float32))
        out_specs.append(whole_spec())
    results = pl.pallas_call(
        functools.partial(pack_kernel, layer),
        out_shape=out_shape,
        in_specs=[hbm_spec()] * 2 + [whole_spec()] * len(faces),
        out_specs=out_specs,
        scratch_shapes=[
            pltpu.VMEM((ranks, size, cols), jnp.float32),
            pltpu.VMEM((ranks, block, cols), jnp.int32),
            pltpu.VMEM((planes, rows, LANES), jnp.float32),
            pltpu.VMEM((planes, rows, LANES), jnp.float32),
            pltpu.SemaphoreType.DMA((ranks,)),
            pltpu.SemaphoreType.DMA((ranks * (held + 1) + 2,)),
            pltpu.SemaphoreType.DMA((ranks,)),
        ],
        compiler_params=pltpu.CompilerParams(vmem_limit_bytes=VMEM_LIMIT if layer else MOST_VMEM),
        cost_estimate=pl.CostEstimate(flops=0, bytes_accessed=0, transcendentals=0),
        name="pack",
    )(concentration, stiff_mask, *faces)
    return list(results[:ranks]), results[ranks:]


def spread_kernel(ranks, mixing_ref, inverse_ref, affinity_ref, mineral_ref, *refs):
    _, first_ref, both_ref, ratio_ref = refs
    components = mixing_ref.shape[0]
    stacked = components * TILE
    held = components // ranks
    me = lax.axis_index("comp")

    def dot(left, right):
        return jnp.dot(left, right, precision=highest, preferred_element_type=jnp.float32)

    def pick(shape, stacked_dim):
        at = lax.broadcasted_iota(jnp.int32, shape, stacked_dim) // TILE
        component = jnp.bitwise_xor(me, pair(at // held, ranks)) * held + lax.rem(at, held)
        held_at = lax.broadcasted_iota(jnp.int32, shape, 1 - stacked_dim)
        return jnp.where(component == held_at, 1.0, 0.0)

    rows = pick((stacked, components), 0)
    cols = pick((components, stacked), 1)
    inner = (stacked, stacked)
    same = lax.rem(lax.broadcasted_iota(jnp.int32, inner, 0), TILE) == lax.rem(
        lax.broadcasted_iota(jnp.int32, inner, 1), TILE
    )

    def spread(matrix):
        return jnp.where(same, dot(dot(rows, matrix), cols), 0.0)

    inverse = inverse_ref[...]
    square = (components, components)
    unit = jnp.where(
        lax.broadcasted_iota(jnp.int32, square, 0) == lax.broadcasted_iota(jnp.int32, square, 1),
        1.0,
        0.0,
    )
    blend = unit - dot(inverse, mixing_ref[...])
    high, low = split(spread(inverse))
    first_ref[...] = jnp.concatenate([high, low, high], axis=1)
    high, low = split(
        jnp.concatenate([spread(blend), spread(-inverse * affinity_ref[...])], axis=1)
    )
    both_ref[...] = jnp.concatenate([high, low, high], axis=1)
    ratio = jnp.sum(rows * (mineral_ref[...] / affinity_ref[...]), axis=1, keepdims=True)
    ratio_ref[...] = jnp.broadcast_to(ratio, (stacked, LANES))


def spread_parameters(ranks, mixing, mixing_inverse, affinity, mineral, after):
    components = mixing.shape[0]
    stacked = components * TILE
    return pl.pallas_call(
        functools.partial(spread_kernel, ranks),
        out_shape=[
            jax.ShapeDtypeStruct((stacked, 3 * stacked), jnp.bfloat16),
            jax.ShapeDtypeStruct((stacked, 6 * stacked), jnp.bfloat16),
            jax.ShapeDtypeStruct((stacked, LANES), jnp.float32),
        ],
        in_specs=[whole_spec()] * 4 + [any_spec()],
        out_specs=[whole_spec()] * 3,
        compiler_params=pltpu.CompilerParams(vmem_limit_bytes=VMEM_LIMIT),
        cost_estimate=pl.CostEstimate(flops=0, bytes_accessed=0, transcendentals=0),
        name="spread_parameters",
    )(mixing, mixing_inverse, affinity.reshape(1, -1), mineral.reshape(1, -1), after)


def step_kernel(pieces, layer, is_first, with_rim, spread_ref, retard_ref, *refs):
    value_refs, refs = refs[:pieces], refs[pieces:]
    (low_ref, high_ref, rate_ref, flag_ref, ratio_ref, first_ref, both_ref), refs = (
        refs[:7],
        refs[7:],
    )
    if not is_first:
        stiff_ref, refs = refs[0], refs[1:]
    out_refs, refs = refs[:pieces], refs[pieces:]
    if with_rim:
        rim_ref, refs = refs[0], refs[1:]
    if is_first:
        stiff_ref, refs = refs[0], refs[1:]
    offset_ref, species_ref, plain_ref = refs
    groups, stacked, cols = species_ref.shape
    rows = groups * TILE
    components = stacked // TILE
    held = components // pieces
    me = lax.axis_index("comp")
    ranks = [jnp.bitwise_xor(me, pair(q, pieces)) for q in range(pieces)]
    row_at = lax.broadcasted_iota(jnp.int32, (rows, cols), 0)
    col_at = lax.broadcasted_iota(jnp.int32, (rows, cols), 1)

    def product(weights, parts):
        highs, lows = zip(*[split(part) for part in parts])
        operand = jnp.concatenate(highs + highs + lows, axis=0)
        return jnp.dot(weights[...], operand, preferred_element_type=jnp.float32)

    weight_plus, weight_minus = face_weights(rate_ref[...], flag_ref[...])

    def column(side, at):
        return jnp.broadcast_to(side[:, at : at + 1], (rows, cols))

    def from_lower_row(value):
        return jnp.where(row_at == 0, 0.0, pltpu.roll(value, 1, 0))

    def from_upper_row(value):
        return jnp.where(row_at == rows - 1, 0.0, pltpu.roll(value, rows - 1, 0))

    def from_lower_col(value, edge):
        return jnp.where(col_at == 0, edge, pltpu.roll(value, 1, 1))

    def from_upper_col(value, edge):
        return jnp.where(col_at == cols - 1, edge, pltpu.roll(value, cols - 1, 1))

    block = rows // pieces
    if is_first:
        sides = []
        low_side, rim_at = low_ref[0], 2 * held * NZ
        turn = LANES - (me * (NZ // pieces) + layer)
        for q in range(pieces):
            side = pltpu.roll(low_ref[pair(q, pieces)], turn, 1)
            for index in range(held):
                sides.append((side, (held + index) * NZ, side, index * NZ))
    else:
        low_side, high_side, rim_at = low_ref[...], high_ref[...], 2 * components
        sides = [(low_side, components + at, high_side, at) for at in range(components)]
    down_plus = from_lower_row(weight_plus[0])
    down_minus = from_lower_row(weight_minus[0])
    side_plus = from_lower_col(weight_plus[1], column(low_side, rim_at))
    side_minus = from_lower_col(weight_minus[1], column(low_side, rim_at + 1))
    centre = down_minus + weight_plus[0] + side_minus + weight_plus[1]
    for at, (low_side, low_at, high_side, high_at) in enumerate(sides):
        q, index = divmod(at, held)
        value = value_refs[q][index * rows : (index + 1) * rows, :]
        component = ranks[q] * held + index
        spread = spread_ref[component]
        retard = 1.0 / jnp.full((rows, LANES), retard_ref[component], jnp.float32)
        retard = jnp.concatenate([retard] * (cols // LANES), axis=1)
        change = (
            (down_plus + spread) * from_lower_row(value)
            + (weight_minus[0] + spread) * from_upper_row(value)
            + (side_plus + spread) * from_lower_col(value, column(low_side, low_at))
            + (weight_minus[1] + spread) * from_upper_col(value, column(high_side, high_at))
            - (centre + 4.0 * spread) * value
        )
        value = value + change * retard
        for group in range(groups):
            offset_ref[group, at * TILE : (at + 1) * TILE, :] = value[
                group * TILE : (group + 1) * TILE
            ]

    for group in range(groups):
        offset = product(first_ref, [offset_ref[group]])
        offset_ref[group] = offset
        species_ref[group] = offset

    def plain_step(_, carry):
        for group in range(groups):
            species = species_ref[group]
            species_ref[group] = offset_ref[group] + product(both_ref, [species, jnp.tanh(species)])
        return carry

    lax.fori_loop(0, NEWT - 1, plain_step, 0)
    plain_ref[...] = species_ref[...]
    ratio = jnp.concatenate([ratio_ref[...]] * (cols // LANES), axis=1)

    def stiff_step(_, carry):
        for group in range(groups):
            species = species_ref[group]
            reaction = jnp.tanh(species) + ratio * jnp.tanh(species + species)
            species_ref[group] = offset_ref[group] + product(both_ref, [species, reaction])
        return carry

    lax.fori_loop(0, STIFF, stiff_step, 0)
    if is_first:
        for rank, value_ref in zip(ranks, value_refs):
            spot = pl.ds(pl.multiple_of(rank * block, TILE), block)
            stiff_ref[spot, :] = value_ref[held * rows : held * rows + block, :]
    for group in range(groups):
        spot = slice(group * TILE, (group + 1) * TILE)
        stiff = stiff_ref[spot, :] > 0.0
        for at in range(components):
            lane = slice(at * TILE, (at + 1) * TILE)
            start = at % held * rows + group * TILE
            out_refs[at // held][start : start + TILE, :] = jnp.where(
                stiff, species_ref[group, lane, :], plain_ref[group, lane, :]
            )
    if with_rim:
        edges = [ref[i * rows : (i + 1) * rows, :] for ref in out_refs for i in range(held)]
        columns = [value[:, :1] for value in edges] + [value[:, cols - 1 :] for value in edges]
        columns += [weight_plus[1][:, cols - 1 :], weight_minus[1][:, cols - 1 :]]
        rim_ref[...] = gather_columns(columns, rows)


def layer_step(values, stiff, low, high, shared, layer, with_rim):
    dispersion, retardation, face_rate, face_flag, ratio, first, both = shared
    pieces = len(values)
    rows, cols = face_rate.shape[1:]
    groups = rows // TILE
    stacked = ratio.shape[0]
    components = stacked // TILE
    scalar = pl.BlockSpec(memory_space=pltpu.SMEM)
    plane = jax.ShapeDtypeStruct((components // pieces * rows, cols), jnp.float32)
    out_shape = [plane] * pieces
    if with_rim:
        out_shape.append(jax.ShapeDtypeStruct((rows, LANES), jnp.float32))
    if stiff is None:
        out_shape.append(jax.ShapeDtypeStruct((rows, cols), jnp.float32))
    field = pltpu.VMEM((groups, stacked, cols), jnp.float32)
    cells = rows * cols
    operands = [dispersion, retardation, *values, low, high, face_rate, face_flag]
    operands += [ratio, first, both]
    if stiff is not None:
        operands.append(stiff)
    results = pl.pallas_call(
        functools.partial(step_kernel, pieces, layer, stiff is None, with_rim),
        out_shape=out_shape,
        in_specs=[scalar, scalar] + [whole_spec()] * (len(operands) - 2),
        out_specs=[whole_spec()] * len(out_shape),
        scratch_shapes=[field, field, field],
        compiler_params=pltpu.CompilerParams(vmem_limit_bytes=VMEM_LIMIT),
        cost_estimate=pl.CostEstimate(flops=0, bytes_accessed=0, transcendentals=0),
        name="layer_step",
    )(*operands)
    values, results = results[:pieces], results[pieces:]
    rims = results[0] if with_rim else None
    return values, (results[-1] if stiff is None else stiff), rims


def by_layers(
    concentration,
    face_rate,
    face_flag,
    retardation,
    dispersion,
    mixing,
    mixing_inverse,
    affinity,
    mineral,
    stiff_mask,
):
    ranks = lax.axis_size("comp")
    me = lax.axis_index("comp")
    planes, rows, cols = concentration.shape
    held = planes // NZ
    layers = NZ // ranks

    def send(value, by):
        return lax.ppermute(value, "comp", [(i, i ^ by) for i in range(ranks)]) if by else value

    def send_all(parts):
        return [send(part, pair(q, ranks)) for q, part in enumerate(parts)]

    messages, (edges,) = pack(concentration, stiff_mask, 0, ranks, (face_rate, face_flag))
    arrived = [send_all(messages)]

    from_low, from_high = shifted(edges, "space", 1), shifted(edges, "space", -1)
    lane_at = lax.broadcasted_iota(jnp.int32, edges.shape, 1)
    sides = jnp.where(lane_at < planes, from_high, from_low)[None]
    span = 1
    while span < ranks:
        sides = jnp.concatenate([sides, send(sides, span)])
        span *= 2

    for layer in range(1, layers):
        messages, _ = pack(concentration, stiff_mask, layer, ranks, ())
        messages, sides = lax.optimization_barrier((messages, sides))
        arrived.append(send_all(messages))

    first, both, ratio = spread_parameters(ranks, mixing, mixing_inverse, affinity, mineral, edges)
    shared = (dispersion, retardation, face_rate, face_flag, ratio, first, both)

    result = jnp.zeros((held, NZ, rows, cols), jnp.float32)
    for layer in range(layers):
        values, stiff = arrived[layer], None
        low, high = sides, sides
        for step in range(STEPS):
            last = step == STEPS - 1
            values, stiff, rims = layer_step(values, stiff, low, high, shared, layer, not last)
            if not last:
                low, high = shifted(rims, "space", 1), shifted(rims, "space", -1)
        for q, piece in enumerate(send_all(values)):
            result = lax.dynamic_update_slice(
                result,
                piece.reshape(held, 1, rows, cols),
                (0, (me ^ pair(q, ranks)) * layers + layer, 0, 0),
            )
    return result.reshape(planes, rows, cols)


def shards(concentration, face_rate, face_flag, *parameters):
    ranks = lax.axis_size("comp")
    planes, rows, cols = concentration.shape
    whole = NZ % ranks == 0 and planes % NZ == 0 and ranks & (ranks - 1) == 0
    narrow = 2 * max(NC, planes) + 2 <= LANES
    even = rows % (ranks * TILE) == 0 and cols % LANES == 0
    plan = by_layers if whole and narrow and even else by_rows
    return plan(concentration, face_rate, face_flag, *parameters)


def solution(mesh):
    in_specs = (
        P(("real", "comp"), None, "space"),
        P(None, "real", "space"),
        P(None, "real", "space"),
        P(),
        P(),
        P(),
        P(),
        P(),
        P(),
        P(None, ("real", "comp"), "space"),
    )
    out_specs = P(("real", "comp"), None, "space")
    return jax.shard_map(shards, mesh=mesh, in_specs=in_specs, out_specs=out_specs, check_vma=False)
```

```python
import functools

import jax
import jax.numpy as jnp
from jax import lax
from jax.experimental import pallas as pl
from jax.experimental.pallas import tpu as pltpu
from jax.sharding import PartitionSpec as P

NC = 16
NZ = 8
STEPS = 2
NEWT = 4
STIFF = 4


highest = lax.Precision.HIGHEST


def shifted(shard, axis, by):
    devices = lax.axis_size(axis)
    pairs = [(i, i + by) for i in range(devices) if 0 <= i + by < devices]
    return lax.ppermute(shard, axis, pairs)


def extended(block, sides, width):
    for axis, dim in sides:
        count = lax.axis_size(axis)
        forward = [(i, i + 1) for i in range(count - 1)]
        backward = [(target, source) for source, target in forward]
        low = lax.ppermute(
            lax.slice_in_dim(block, block.shape[dim] - width, None, axis=dim), axis, forward
        )
        high = lax.ppermute(lax.slice_in_dim(block, 0, width, axis=dim), axis, backward)
        block = jnp.concatenate([low, block, high], axis=dim)
    return block


def shift_down(values, axis_index):
    size_along = values.shape[axis_index]
    zero_row = jnp.zeros_like(lax.slice_in_dim(values, 0, 1, axis=axis_index))
    kept = lax.slice_in_dim(values, 0, size_along - 1, axis=axis_index)
    return jnp.concatenate([zero_row, kept], axis=axis_index)


def face_weights(face_rate, face_flag):
    flag_values = face_flag.astype(jnp.float32)
    weight_plus = face_rate * flag_values
    weight_minus = face_rate * (1.0 - flag_values)
    return (weight_plus, weight_minus)


def advance(
    values, lower_row, upper_row, lower_col, upper_col, coefficients, retard_planes, spread_planes
):
    divergence = (
        coefficients[0] * lower_row
        + coefficients[1] * upper_row
        + coefficients[2] * lower_col
        + coefficients[3] * upper_col
        - coefficients[4] * values
    )
    laplace = lower_row + upper_row + lower_col + upper_col - 4.0 * values
    return values + (divergence + spread_planes * laplace) / retard_planes


def residual_of(species, target, mixing, affinity, mineral, stiff):
    total = jnp.dot(
        mixing, species, precision=highest, preferred_element_type=jnp.float32
    ) + affinity[:, None] * jnp.tanh(species)
    if stiff:
        total = total + mineral[:, None] * jnp.tanh(2.0 * species)
    return total - target


def newton_steps(species, target, repeats, stiff, mixing, mixing_inverse, affinity, mineral):
    for iteration in range(repeats):
        update = residual_of(species, target, mixing, affinity, mineral, stiff)
        species = species - jnp.dot(
            mixing_inverse, update, precision=highest, preferred_element_type=jnp.float32
        )
    return species


def speciate(cell_block, stiff_mask, mixing, mixing_inverse, affinity, mineral):
    target = cell_block.reshape(NC, -1)
    flat_mask = stiff_mask.reshape(-1) > 0
    species = jnp.zeros_like(target)
    species = newton_steps(species, target, NEWT, False, mixing, mixing_inverse, affinity, mineral)
    stiffer = newton_steps(species, target, STIFF, True, mixing, mixing_inverse, affinity, mineral)
    species = jnp.where(flat_mask[None, :], stiffer, species)
    return species.reshape(cell_block.shape)


def by_rows(
    concentration,
    face_rate,
    face_flag,
    retardation,
    dispersion,
    mixing,
    mixing_inverse,
    affinity,
    mineral,
    stiff_mask,
):
    weight_plus, weight_minus = face_weights(face_rate, face_flag)
    rim_weights = jnp.stack([weight_plus[1, :, -1], weight_minus[1, :, -1]])
    left_rims = shifted(rim_weights, "space", 1)
    side_plus = jnp.concatenate([left_rims[0][:, None], weight_plus[1, :, :-1]], axis=1)
    side_minus = jnp.concatenate([left_rims[1][:, None], weight_minus[1, :, :-1]], axis=1)
    down_plus = shift_down(weight_plus[0], 0)
    down_minus = shift_down(weight_minus[0], 0)
    centre = down_minus + weight_plus[0] + side_minus + weight_plus[1]
    coefficients = jnp.stack([down_plus, weight_minus[0], side_plus, weight_minus[1], centre])
    retard_all = jnp.repeat(retardation, NZ)
    spread_all = jnp.repeat(dispersion, NZ)
    rows_held = stiff_mask.shape[1]
    row_start = lax.axis_index("comp") * rows_held
    cell_coefficients = lax.dynamic_slice_in_dim(coefficients, row_start, rows_held, 1)
    retard_planes = retard_all[:, None, None]
    spread_planes = spread_all[:, None, None]
    cell_block = lax.all_to_all(concentration, "comp", split_axis=1, concat_axis=0, tiled=True)
    for step_index in range(STEPS):
        padded = extended(cell_block, (("comp", 1), ("space", 2)), 1)
        cell_block = advance(
            cell_block,
            padded[:, :-2, 1:-1],
            padded[:, 2:, 1:-1],
            padded[:, 1:-1, :-2],
            padded[:, 1:-1, 2:],
            cell_coefficients,
            retard_planes,
            spread_planes,
        )
        cell_block = speciate(cell_block, stiff_mask, mixing, mixing_inverse, affinity, mineral)
    return lax.all_to_all(cell_block, "comp", split_axis=0, concat_axis=1, tiled=True)


TILE = 8
LANES = 128
VMEM_LIMIT = 24 * 1024 * 1024
MOST_VMEM = 60 * 1024 * 1024


def whole_spec():
    return pl.BlockSpec(memory_space=pltpu.VMEM)


def any_spec():
    return pl.BlockSpec(memory_space=pl.ANY)


def hbm_spec():
    return pl.BlockSpec(memory_space=pltpu.HBM)


def pair(q, ranks):
    return (ranks - q) % ranks


def spans(ranks):
    return [ranks >> bit for bit in range(1, ranks.bit_length())]


def doubled(ranks):
    places = [0]
    for by in spans(ranks):
        places += [place ^ by for place in places]
    return places


def split(value):
    high = value.astype(jnp.bfloat16)
    return high, (value - high.astype(jnp.float32)).astype(jnp.bfloat16)


def gather_columns(columns, rows):
    lane_at = lax.broadcasted_iota(jnp.int32, (rows, LANES), 1)
    gathered = jnp.zeros((rows, LANES), jnp.float32)
    for lane, column in enumerate(columns):
        gathered = jnp.where(lane_at == lane, jnp.broadcast_to(column, (rows, LANES)), gathered)
    return gathered


def pack_kernel(layer, plane_ref, mask_ref, *refs):
    if not layer:
        (rate_ref, flag_ref), refs = refs[:2], refs[2:]
    refs, (part_ref, mask_part, first_ref, last_ref, mask_sems, in_sems, out_sems) = (
        refs[:-7],
        refs[-7:],
    )
    out_refs = refs[: part_ref.shape[0]]
    ranks = len(out_refs)
    planes, rows, cols = plane_ref.shape
    levels, block, _ = mask_ref.shape
    held = planes // levels
    me = lax.axis_index("comp")
    copies = []
    order = [*range(1, ranks), 0]

    def start(source, target, sem):
        copies.append(pltpu.make_async_copy(source, target, sem))
        copies[-1].start()

    for q in order:
        at = jnp.bitwise_xor(me, pair(q, ranks)) * (levels // ranks) + layer
        for index in range(held):
            spot = pl.ds(index * rows, rows)
            start(plane_ref.at[index * levels + at], part_ref.at[q, spot], in_sems.at[len(copies)])
        start(mask_ref.at[at], mask_part.at[q], mask_sems.at[q])
    arrivals = list(copies)
    if not layer:
        start(plane_ref.at[:, :, pl.ds(0, LANES)], first_ref, in_sems.at[len(copies)])
        start(
            plane_ref.at[:, :, pl.ds(cols - LANES, LANES)], last_ref, in_sems.at[len(copies)]
        )
    edges = copies[len(arrivals) :]
    copies.clear()
    for position, q in enumerate(order):
        for copy in arrivals[position * (held + 1) : (position + 1) * (held + 1)]:
            copy.wait()
        part_ref[q, held * rows :, :] = mask_part[q].astype(jnp.float32)
        start(part_ref.at[q], out_refs[q], out_sems.at[q])
    for copy in edges:
        copy.wait()
    if not layer:
        end = slice(cols - LANES, cols)
        weight_plus, weight_minus = face_weights(rate_ref[1, :, end], flag_ref[1, :, end])
        columns = [first_ref[plane][:, :1] for plane in range(planes)]
        columns += [last_ref[plane][:, LANES - 1 :] for plane in range(planes)]
        columns += [weight_plus[:, LANES - 1 :], weight_minus[:, LANES - 1 :]]
        refs[ranks][...] = gather_columns(columns, rows)
    for copy in copies:
        copy.wait()


def pack(concentration, stiff_mask, layer, ranks, faces):
    planes, rows, cols = concentration.shape
    held = planes // NZ
    block = stiff_mask.shape[1]
    size = held * rows + block
    out_shape = [jax.ShapeDtypeStruct((size, cols), jnp.float32)] * ranks
    out_specs = [any_spec()] * ranks
    if not layer:
        out_shape.append(jax.ShapeDtypeStruct((rows, LANES), jnp.float32))
        out_specs.append(whole_spec())
    results = pl.pallas_call(
        functools.partial(pack_kernel, layer),
        out_shape=out_shape,
        in_specs=[hbm_spec()] * 2 + [whole_spec()] * len(faces),
        out_specs=out_specs,
        scratch_shapes=[
            pltpu.VMEM((ranks, size, cols), jnp.float32),
            pltpu.VMEM((ranks, block, cols), jnp.int32),
            pltpu.VMEM((planes, rows, LANES), jnp.float32),
            pltpu.VMEM((planes, rows, LANES), jnp.float32),
            pltpu.SemaphoreType.DMA((ranks,)),
            pltpu.SemaphoreType.DMA((ranks * (held + 1) + 2,)),
            pltpu.SemaphoreType.DMA((ranks,)),
        ],
        compiler_params=pltpu.CompilerParams(vmem_limit_bytes=VMEM_LIMIT if layer else MOST_VMEM),
        cost_estimate=pl.CostEstimate(flops=0, bytes_accessed=0, transcendentals=0),
        name="pack",
    )(concentration, stiff_mask, *faces)
    return list(results[:ranks]), results[ranks:]


def spread_kernel(ranks, mixing_ref, inverse_ref, affinity_ref, mineral_ref, *refs):
    _, first_ref, both_ref, ratio_ref = refs
    components = mixing_ref.shape[0]
    stacked = components * TILE
    held = components // ranks
    me = lax.axis_index("comp")

    def dot(left, right):
        return jnp.dot(left, right, precision=highest, preferred_element_type=jnp.float32)

    def pick(shape, stacked_dim):
        at = lax.broadcasted_iota(jnp.int32, shape, stacked_dim) // TILE
        component = jnp.bitwise_xor(me, pair(at // held, ranks)) * held + lax.rem(at, held)
        held_at = lax.broadcasted_iota(jnp.int32, shape, 1 - stacked_dim)
        return jnp.where(component == held_at, 1.0, 0.0)

    rows = pick((stacked, components), 0)
    cols = pick((components, stacked), 1)
    inner = (stacked, stacked)
    same = lax.rem(lax.broadcasted_iota(jnp.int32, inner, 0), TILE) == lax.rem(
        lax.broadcasted_iota(jnp.int32, inner, 1), TILE
    )

    def spread(matrix):
        return jnp.where(same, dot(dot(rows, matrix), cols), 0.0)

    inverse = inverse_ref[...]
    square = (components, components)
    unit = jnp.where(
        lax.broadcasted_iota(jnp.int32, square, 0) == lax.broadcasted_iota(jnp.int32, square, 1),
        1.0,
        0.0,
    )
    blend = unit - dot(inverse, mixing_ref[...])
    high, low = split(spread(inverse))
    first_ref[...] = jnp.concatenate([high, low, high], axis=1)
    high, low = split(
        jnp.concatenate([spread(blend), spread(-inverse * affinity_ref[...])], axis=1)
    )
    both_ref[...] = jnp.concatenate([high, low, high], axis=1)
    ratio = jnp.sum(rows * (mineral_ref[...] / affinity_ref[...]), axis=1, keepdims=True)
    ratio_ref[...] = jnp.broadcast_to(ratio, (stacked, LANES))


def spread_parameters(ranks, mixing, mixing_inverse, affinity, mineral, after):
    components = mixing.shape[0]
    stacked = components * TILE
    return pl.pallas_call(
        functools.partial(spread_kernel, ranks),
        out_shape=[
            jax.ShapeDtypeStruct((stacked, 3 * stacked), jnp.bfloat16),
            jax.ShapeDtypeStruct((stacked, 6 * stacked), jnp.bfloat16),
            jax.ShapeDtypeStruct((stacked, LANES), jnp.float32),
        ],
        in_specs=[whole_spec()] * 4 + [any_spec()],
        out_specs=[whole_spec()] * 3,
        compiler_params=pltpu.CompilerParams(vmem_limit_bytes=VMEM_LIMIT),
        cost_estimate=pl.CostEstimate(flops=0, bytes_accessed=0, transcendentals=0),
        name="spread_parameters",
    )(mixing, mixing_inverse, affinity.reshape(1, -1), mineral.reshape(1, -1), after)


def step_kernel(pieces, layer, is_first, with_rim, spread_ref, retard_ref, *refs):
    value_refs, refs = refs[:pieces], refs[pieces:]
    (low_ref, high_ref, rate_ref, flag_ref, ratio_ref, first_ref, both_ref), refs = (
        refs[:7],
        refs[7:],
    )
    if not is_first:
        stiff_ref, refs = refs[0], refs[1:]
    out_refs, refs = refs[:pieces], refs[pieces:]
    if with_rim:
        rim_ref, refs = refs[0], refs[1:]
    if is_first:
        stiff_ref, refs = refs[0], refs[1:]
    offset_ref, species_ref, plain_ref = refs
    groups, stacked, cols = species_ref.shape
    rows = groups * TILE
    components = stacked // TILE
    held = components // pieces
    me = lax.axis_index("comp")
    ranks = [jnp.bitwise_xor(me, pair(q, pieces)) for q in range(pieces)]
    row_at = lax.broadcasted_iota(jnp.int32, (rows, cols), 0)
    col_at = lax.broadcasted_iota(jnp.int32, (rows, cols), 1)

    def product(weights, parts):
        highs, lows = zip(*[split(part) for part in parts])
        operand = jnp.concatenate(highs + highs + lows, axis=0)
        return jnp.dot(weights[...], operand, preferred_element_type=jnp.float32)

    weight_plus, weight_minus = face_weights(rate_ref[...], flag_ref[...])

    def column(side, at):
        return jnp.broadcast_to(side[:, at : at + 1], (rows, cols))

    def from_lower_row(value):
        return jnp.where(row_at == 0, 0.0, pltpu.roll(value, 1, 0))

    def from_upper_row(value):
        return jnp.where(row_at == rows - 1, 0.0, pltpu.roll(value, rows - 1, 0))

    def from_lower_col(value, edge):
        return jnp.where(col_at == 0, edge, pltpu.roll(value, 1, 1))

    def from_upper_col(value, edge):
        return jnp.where(col_at == cols - 1, edge, pltpu.roll(value, cols - 1, 1))

    block = rows // pieces
    if is_first:
        sides = []
        low_side, rim_at = low_ref[0], 2 * held * NZ
        turn = LANES - (me * (NZ // pieces) + layer)
        for q in range(pieces):
            side = pltpu.roll(low_ref[doubled(pieces).index(pair(q, pieces))], turn, 1)
            for index in range(held):
                sides.append((side, (held + index) * NZ, side, index * NZ))
    else:
        low_side, high_side, rim_at = low_ref[...], high_ref[...], 2 * components
        sides = [(low_side, components + at, high_side, at) for at in range(components)]
    down_plus = from_lower_row(weight_plus[0])
    down_minus = from_lower_row(weight_minus[0])
    side_plus = from_lower_col(weight_plus[1], column(low_side, rim_at))
    side_minus = from_lower_col(weight_minus[1], column(low_side, rim_at + 1))
    centre = down_minus + weight_plus[0] + side_minus + weight_plus[1]
    for at, (low_side, low_at, high_side, high_at) in enumerate(sides):
        q, index = divmod(at, held)
        value = value_refs[q][index * rows : (index + 1) * rows, :]
        component = ranks[q] * held + index
        spread = spread_ref[component]
        retard = 1.0 / jnp.full((rows, LANES), retard_ref[component], jnp.float32)
        retard = jnp.concatenate([retard] * (cols // LANES), axis=1)
        change = (
            (down_plus + spread) * from_lower_row(value)
            + (weight_minus[0] + spread) * from_upper_row(value)
            + (side_plus + spread) * from_lower_col(value, column(low_side, low_at))
            + (weight_minus[1] + spread) * from_upper_col(value, column(high_side, high_at))
            - (centre + 4.0 * spread) * value
        )
        value = value + change * retard
        for group in range(groups):
            offset_ref[group, at * TILE : (at + 1) * TILE, :] = value[
                group * TILE : (group + 1) * TILE
            ]

    for group in range(groups):
        offset = product(first_ref, [offset_ref[group]])
        offset_ref[group] = offset
        species_ref[group] = offset

    def plain_step(_, carry):
        for group in range(groups):
            species = species_ref[group]
            species_ref[group] = offset_ref[group] + product(both_ref, [species, jnp.tanh(species)])
        return carry

    lax.fori_loop(0, NEWT - 1, plain_step, 0)
    plain_ref[...] = species_ref[...]
    ratio = jnp.concatenate([ratio_ref[...]] * (cols // LANES), axis=1)

    def stiff_step(_, carry):
        for group in range(groups):
            species = species_ref[group]
            reaction = jnp.tanh(species) + ratio * jnp.tanh(species + species)
            species_ref[group] = offset_ref[group] + product(both_ref, [species, reaction])
        return carry

    lax.fori_loop(0, STIFF, stiff_step, 0)
    if is_first:
        for rank, value_ref in zip(ranks, value_refs):
            spot = pl.ds(pl.multiple_of(rank * block, TILE), block)
            stiff_ref[spot, :] = value_ref[held * rows : held * rows + block, :]
    for group in range(groups):
        spot = slice(group * TILE, (group + 1) * TILE)
        stiff = stiff_ref[spot, :] > 0.0
        for at in range(components):
            lane = slice(at * TILE, (at + 1) * TILE)
            start = at % held * rows + group * TILE
            out_refs[at // held][start : start + TILE, :] = jnp.where(
                stiff, species_ref[group, lane, :], plain_ref[group, lane, :]
            )
    if with_rim:
        edges = [ref[i * rows : (i + 1) * rows, :] for ref in out_refs for i in range(held)]
        columns = [value[:, :1] for value in edges] + [value[:, cols - 1 :] for value in edges]
        columns += [weight_plus[1][:, cols - 1 :], weight_minus[1][:, cols - 1 :]]
        rim_ref[...] = gather_columns(columns, rows)


def layer_step(values, stiff, low, high, shared, layer, with_rim):
    dispersion, retardation, face_rate, face_flag, ratio, first, both = shared
    pieces = len(values)
    rows, cols = face_rate.shape[1:]
    groups = rows // TILE
    stacked = ratio.shape[0]
    components = stacked // TILE
    scalar = pl.BlockSpec(memory_space=pltpu.SMEM)
    plane = jax.ShapeDtypeStruct((components // pieces * rows, cols), jnp.float32)
    out_shape = [plane] * pieces
    if with_rim:
        out_shape.append(jax.ShapeDtypeStruct((rows, LANES), jnp.float32))
    if stiff is None:
        out_shape.append(jax.ShapeDtypeStruct((rows, cols), jnp.float32))
    field = pltpu.VMEM((groups, stacked, cols), jnp.float32)
    cells = rows * cols
    operands = [dispersion, retardation, *values, low, high, face_rate, face_flag]
    operands += [ratio, first, both]
    if stiff is not None:
        operands.append(stiff)
    results = pl.pallas_call(
        functools.partial(step_kernel, pieces, layer, stiff is None, with_rim),
        out_shape=out_shape,
        in_specs=[scalar, scalar] + [whole_spec()] * (len(operands) - 2),
        out_specs=[whole_spec()] * len(out_shape),
        scratch_shapes=[field, field, field],
        compiler_params=pltpu.CompilerParams(vmem_limit_bytes=VMEM_LIMIT),
        cost_estimate=pl.CostEstimate(flops=0, bytes_accessed=0, transcendentals=0),
        name="layer_step",
    )(*operands)
    values, results = results[:pieces], results[pieces:]
    rims = results[0] if with_rim else None
    return values, (results[-1] if stiff is None else stiff), rims


def by_layers(
    concentration,
    face_rate,
    face_flag,
    retardation,
    dispersion,
    mixing,
    mixing_inverse,
    affinity,
    mineral,
    stiff_mask,
):
    ranks = lax.axis_size("comp")
    me = lax.axis_index("comp")
    planes, rows, cols = concentration.shape
    held = planes // NZ
    layers = NZ // ranks

    def send(value, by):
        return lax.ppermute(value, "comp", [(i, i ^ by) for i in range(ranks)]) if by else value

    def send_all(parts):
        return [send(part, pair(q, ranks)) for q, part in enumerate(parts)]

    messages, (edges,) = pack(concentration, stiff_mask, 0, ranks, (face_rate, face_flag))
    arrived = [send_all(messages)]

    from_low, from_high = shifted(edges, "space", 1), shifted(edges, "space", -1)
    lane_at = lax.broadcasted_iota(jnp.int32, edges.shape, 1)
    sides = jnp.where(lane_at < planes, from_high, from_low)[None]
    later = [pack(concentration, stiff_mask, layer, ranks, ())[0] for layer in range(1, layers)]
    sides, later = lax.optimization_barrier((sides, later))
    for by in spans(ranks):
        if by == 1:
            sides, arrived[0] = lax.optimization_barrier((sides, arrived[0]))
        sides = jnp.concatenate([sides, send(sides, by)])

    for messages in later:
        messages[:-1], arrived[-1] = lax.optimization_barrier((messages[:-1], arrived[-1]))
        messages[-1], sides = lax.optimization_barrier((messages[-1], sides))
        arrived.append(send_all(messages))

    first, both, ratio = spread_parameters(ranks, mixing, mixing_inverse, affinity, mineral, edges)
    shared = (dispersion, retardation, face_rate, face_flag, ratio, first, both)

    result = jnp.zeros((held, NZ, rows, cols), jnp.float32)
    for layer in range(layers):
        values, stiff = arrived[layer], None
        low, high = sides, sides
        for step in range(STEPS):
            last = step == STEPS - 1
            values, stiff, rims = layer_step(values, stiff, low, high, shared, layer, not last)
            if not last:
                low, high = shifted(rims, "space", 1), shifted(rims, "space", -1)
        for q, piece in enumerate(send_all(values)):
            result = lax.dynamic_update_slice(
                result,
                piece.reshape(held, 1, rows, cols),
                (0, (me ^ pair(q, ranks)) * layers + layer, 0, 0),
            )
    return result.reshape(planes, rows, cols)


def shards(concentration, face_rate, face_flag, *parameters):
    ranks = lax.axis_size("comp")
    planes, rows, cols = concentration.shape
    whole = NZ % ranks == 0 and planes % NZ == 0 and ranks & (ranks - 1) == 0
    narrow = 2 * max(NC, planes) + 2 <= LANES
    even = rows % (ranks * TILE) == 0 and cols % LANES == 0
    plan = by_layers if whole and narrow and even else by_rows
    return plan(concentration, face_rate, face_flag, *parameters)


def solution(mesh):
    in_specs = (
        P(("real", "comp"), None, "space"),
        P(None, "real", "space"),
        P(None, "real", "space"),
        P(),
        P(),
        P(),
        P(),
        P(),
        P(),
        P(None, ("real", "comp"), "space"),
    )
    out_specs = P(("real", "comp"), None, "space")
    return jax.shard_map(shards, mesh=mesh, in_specs=in_specs, out_specs=out_specs, check_vma=False)
```

```python
import functools

import jax
import jax.numpy as jnp
from jax import lax
from jax.experimental import pallas as pl
from jax.experimental.pallas import tpu as pltpu
from jax.sharding import PartitionSpec as P

NC = 16
NZ = 8
STEPS = 2
NEWT = 4
STIFF = 4


highest = lax.Precision.HIGHEST


def shifted(shard, axis, by):
    devices = lax.axis_size(axis)
    pairs = [(i, i + by) for i in range(devices) if 0 <= i + by < devices]
    return lax.ppermute(shard, axis, pairs)


def extended(block, sides, width):
    for axis, dim in sides:
        count = lax.axis_size(axis)
        forward = [(i, i + 1) for i in range(count - 1)]
        backward = [(target, source) for source, target in forward]
        low = lax.ppermute(
            lax.slice_in_dim(block, block.shape[dim] - width, None, axis=dim), axis, forward
        )
        high = lax.ppermute(lax.slice_in_dim(block, 0, width, axis=dim), axis, backward)
        block = jnp.concatenate([low, block, high], axis=dim)
    return block


def shift_down(values, axis_index):
    size_along = values.shape[axis_index]
    zero_row = jnp.zeros_like(lax.slice_in_dim(values, 0, 1, axis=axis_index))
    kept = lax.slice_in_dim(values, 0, size_along - 1, axis=axis_index)
    return jnp.concatenate([zero_row, kept], axis=axis_index)


def face_weights(face_rate, face_flag):
    flag_values = face_flag.astype(jnp.float32)
    weight_plus = face_rate * flag_values
    weight_minus = face_rate * (1.0 - flag_values)
    return (weight_plus, weight_minus)


def advance(
    values, lower_row, upper_row, lower_col, upper_col, coefficients, retard_planes, spread_planes
):
    divergence = (
        coefficients[0] * lower_row
        + coefficients[1] * upper_row
        + coefficients[2] * lower_col
        + coefficients[3] * upper_col
        - coefficients[4] * values
    )
    laplace = lower_row + upper_row + lower_col + upper_col - 4.0 * values
    return values + (divergence + spread_planes * laplace) / retard_planes


def residual_of(species, target, mixing, affinity, mineral, stiff):
    total = jnp.dot(
        mixing, species, precision=highest, preferred_element_type=jnp.float32
    ) + affinity[:, None] * jnp.tanh(species)
    if stiff:
        total = total + mineral[:, None] * jnp.tanh(2.0 * species)
    return total - target


def newton_steps(species, target, repeats, stiff, mixing, mixing_inverse, affinity, mineral):
    for iteration in range(repeats):
        update = residual_of(species, target, mixing, affinity, mineral, stiff)
        species = species - jnp.dot(
            mixing_inverse, update, precision=highest, preferred_element_type=jnp.float32
        )
    return species


def speciate(cell_block, stiff_mask, mixing, mixing_inverse, affinity, mineral):
    target = cell_block.reshape(NC, -1)
    flat_mask = stiff_mask.reshape(-1) > 0
    species = jnp.zeros_like(target)
    species = newton_steps(species, target, NEWT, False, mixing, mixing_inverse, affinity, mineral)
    stiffer = newton_steps(species, target, STIFF, True, mixing, mixing_inverse, affinity, mineral)
    species = jnp.where(flat_mask[None, :], stiffer, species)
    return species.reshape(cell_block.shape)


def by_rows(
    concentration,
    face_rate,
    face_flag,
    retardation,
    dispersion,
    mixing,
    mixing_inverse,
    affinity,
    mineral,
    stiff_mask,
):
    weight_plus, weight_minus = face_weights(face_rate, face_flag)
    rim_weights = jnp.stack([weight_plus[1, :, -1], weight_minus[1, :, -1]])
    left_rims = shifted(rim_weights, "space", 1)
    side_plus = jnp.concatenate([left_rims[0][:, None], weight_plus[1, :, :-1]], axis=1)
    side_minus = jnp.concatenate([left_rims[1][:, None], weight_minus[1, :, :-1]], axis=1)
    down_plus = shift_down(weight_plus[0], 0)
    down_minus = shift_down(weight_minus[0], 0)
    centre = down_minus + weight_plus[0] + side_minus + weight_plus[1]
    coefficients = jnp.stack([down_plus, weight_minus[0], side_plus, weight_minus[1], centre])
    retard_all = jnp.repeat(retardation, NZ)
    spread_all = jnp.repeat(dispersion, NZ)
    rows_held = stiff_mask.shape[1]
    row_start = lax.axis_index("comp") * rows_held
    cell_coefficients = lax.dynamic_slice_in_dim(coefficients, row_start, rows_held, 1)
    retard_planes = retard_all[:, None, None]
    spread_planes = spread_all[:, None, None]
    cell_block = lax.all_to_all(concentration, "comp", split_axis=1, concat_axis=0, tiled=True)
    for step_index in range(STEPS):
        padded = extended(cell_block, (("comp", 1), ("space", 2)), 1)
        cell_block = advance(
            cell_block,
            padded[:, :-2, 1:-1],
            padded[:, 2:, 1:-1],
            padded[:, 1:-1, :-2],
            padded[:, 1:-1, 2:],
            cell_coefficients,
            retard_planes,
            spread_planes,
        )
        cell_block = speciate(cell_block, stiff_mask, mixing, mixing_inverse, affinity, mineral)
    return lax.all_to_all(cell_block, "comp", split_axis=0, concat_axis=1, tiled=True)


TILE = 8
LANES = 128
VMEM_LIMIT = 24 * 1024 * 1024
MOST_VMEM = 60 * 1024 * 1024


def whole_spec():
    return pl.BlockSpec(memory_space=pltpu.VMEM)


def any_spec():
    return pl.BlockSpec(memory_space=pl.ANY)


def hbm_spec():
    return pl.BlockSpec(memory_space=pltpu.HBM)


def pair(q, ranks):
    return (ranks - q) % ranks


def split(value):
    high = value.astype(jnp.bfloat16)
    return high, (value - high.astype(jnp.float32)).astype(jnp.bfloat16)


def gather_columns(columns, rows):
    lane_at = lax.broadcasted_iota(jnp.int32, (rows, LANES), 1)
    gathered = jnp.zeros((rows, LANES), jnp.float32)
    for lane, column in enumerate(columns):
        gathered = jnp.where(lane_at == lane, jnp.broadcast_to(column, (rows, LANES)), gathered)
    return gathered


def pack_kernel(layer, plane_ref, mask_ref, *refs):
    if not layer:
        (rate_ref, flag_ref), refs = refs[:2], refs[2:]
    refs, (part_ref, mask_part, first_ref, last_ref, mask_sems, in_sems, out_sems) = (
        refs[:-7],
        refs[-7:],
    )
    out_refs = refs[: part_ref.shape[0]]
    ranks = len(out_refs)
    planes, rows, cols = plane_ref.shape
    levels, block, _ = mask_ref.shape
    held = planes // levels
    me = lax.axis_index("comp")
    copies = []
    order = [*range(1, ranks), 0]

    def start(source, target, sem):
        copies.append(pltpu.make_async_copy(source, target, sem))
        copies[-1].start()

    for q in order:
        at = jnp.bitwise_xor(me, pair(q, ranks)) * (levels // ranks) + layer
        for index in range(held):
            spot = pl.ds(index * rows, rows)
            start(plane_ref.at[index * levels + at], part_ref.at[q, spot], in_sems.at[len(copies)])
        start(mask_ref.at[at], mask_part.at[q], mask_sems.at[q])
    arrivals = list(copies)
    if not layer:
        start(plane_ref.at[:, :, pl.ds(0, LANES)], first_ref, in_sems.at[len(copies)])
        start(
            plane_ref.at[:, :, pl.ds(cols - LANES, LANES)], last_ref, in_sems.at[len(copies)]
        )
    edges = copies[len(arrivals) :]
    copies.clear()
    for position, q in enumerate(order):
        for copy in arrivals[position * (held + 1) : (position + 1) * (held + 1)]:
            copy.wait()
        part_ref[q, held * rows :, :] = mask_part[q].astype(jnp.float32)
        start(part_ref.at[q], out_refs[q], out_sems.at[q])
    for copy in edges:
        copy.wait()
    if not layer:
        end = slice(cols - LANES, cols)
        weight_plus, weight_minus = face_weights(rate_ref[1, :, end], flag_ref[1, :, end])
        columns = [first_ref[plane][:, :1] for plane in range(planes)]
        columns += [last_ref[plane][:, LANES - 1 :] for plane in range(planes)]
        columns += [weight_plus[:, LANES - 1 :], weight_minus[:, LANES - 1 :]]
        refs[ranks][...] = gather_columns(columns, rows)
    for copy in copies:
        copy.wait()


def pack(concentration, stiff_mask, layer, ranks, faces):
    planes, rows, cols = concentration.shape
    held = planes // NZ
    block = stiff_mask.shape[1]
    size = held * rows + block
    out_shape = [jax.ShapeDtypeStruct((size, cols), jnp.float32)] * ranks
    out_specs = [any_spec()] * ranks
    if not layer:
        out_shape.append(jax.ShapeDtypeStruct((rows, LANES), jnp.float32))
        out_specs.append(whole_spec())
    results = pl.pallas_call(
        functools.partial(pack_kernel, layer),
        out_shape=out_shape,
        in_specs=[hbm_spec()] * 2 + [whole_spec()] * len(faces),
        out_specs=out_specs,
        scratch_shapes=[
            pltpu.VMEM((ranks, size, cols), jnp.float32),
            pltpu.VMEM((ranks, block, cols), jnp.int32),
            pltpu.VMEM((planes, rows, LANES), jnp.float32),
            pltpu.VMEM((planes, rows, LANES), jnp.float32),
            pltpu.SemaphoreType.DMA((ranks,)),
            pltpu.SemaphoreType.DMA((ranks * (held + 1) + 2,)),
            pltpu.SemaphoreType.DMA((ranks,)),
        ],
        compiler_params=pltpu.CompilerParams(vmem_limit_bytes=VMEM_LIMIT if layer else MOST_VMEM),
        cost_estimate=pl.CostEstimate(flops=0, bytes_accessed=0, transcendentals=0),
        name="pack",
    )(concentration, stiff_mask, *faces)
    return list(results[:ranks]), results[ranks:]


def spread_kernel(ranks, mixing_ref, inverse_ref, affinity_ref, mineral_ref, *refs):
    _, first_ref, both_ref, ratio_ref = refs
    components = mixing_ref.shape[0]
    stacked = components * TILE
    held = components // ranks
    me = lax.axis_index("comp")

    def dot(left, right):
        return jnp.dot(left, right, precision=highest, preferred_element_type=jnp.float32)

    def pick(shape, stacked_dim):
        at = lax.broadcasted_iota(jnp.int32, shape, stacked_dim) // TILE
        component = jnp.bitwise_xor(me, pair(at // held, ranks)) * held + lax.rem(at, held)
        held_at = lax.broadcasted_iota(jnp.int32, shape, 1 - stacked_dim)
        return jnp.where(component == held_at, 1.0, 0.0)

    rows = pick((stacked, components), 0)
    cols = pick((components, stacked), 1)
    inner = (stacked, stacked)
    same = lax.rem(lax.broadcasted_iota(jnp.int32, inner, 0), TILE) == lax.rem(
        lax.broadcasted_iota(jnp.int32, inner, 1), TILE
    )

    def spread(matrix):
        return jnp.where(same, dot(dot(rows, matrix), cols), 0.0)

    inverse = inverse_ref[...]
    square = (components, components)
    unit = jnp.where(
        lax.broadcasted_iota(jnp.int32, square, 0) == lax.broadcasted_iota(jnp.int32, square, 1),
        1.0,
        0.0,
    )
    blend = unit - dot(inverse, mixing_ref[...])
    high, low = split(spread(inverse))
    first_ref[...] = jnp.concatenate([high, low, high], axis=1)
    high, low = split(
        jnp.concatenate([spread(blend), spread(-inverse * affinity_ref[...])], axis=1)
    )
    both_ref[...] = jnp.concatenate([high, low, high], axis=1)
    ratio = jnp.sum(rows * (mineral_ref[...] / affinity_ref[...]), axis=1, keepdims=True)
    ratio_ref[...] = jnp.broadcast_to(ratio, (stacked, LANES))


def spread_parameters(ranks, mixing, mixing_inverse, affinity, mineral, after):
    components = mixing.shape[0]
    stacked = components * TILE
    return pl.pallas_call(
        functools.partial(spread_kernel, ranks),
        out_shape=[
            jax.ShapeDtypeStruct((stacked, 3 * stacked), jnp.bfloat16),
            jax.ShapeDtypeStruct((stacked, 6 * stacked), jnp.bfloat16),
            jax.ShapeDtypeStruct((stacked, LANES), jnp.float32),
        ],
        in_specs=[whole_spec()] * 4 + [any_spec()],
        out_specs=[whole_spec()] * 3,
        compiler_params=pltpu.CompilerParams(vmem_limit_bytes=VMEM_LIMIT),
        cost_estimate=pl.CostEstimate(flops=0, bytes_accessed=0, transcendentals=0),
        name="spread_parameters",
    )(mixing, mixing_inverse, affinity.reshape(1, -1), mineral.reshape(1, -1), after)


def step_kernel(pieces, layer, is_first, with_rim, spread_ref, retard_ref, *refs):
    value_refs, refs = refs[:pieces], refs[pieces:]
    (low_ref, high_ref, rate_ref, flag_ref, ratio_ref, first_ref, both_ref), refs = (
        refs[:7],
        refs[7:],
    )
    if not is_first:
        stiff_ref, refs = refs[0], refs[1:]
    out_refs, refs = refs[:pieces], refs[pieces:]
    if with_rim:
        rim_ref, refs = refs[0], refs[1:]
    if is_first:
        stiff_ref, refs = refs[0], refs[1:]
    offset_ref, species_ref, plain_ref = refs
    groups, stacked, cols = species_ref.shape
    rows = groups * TILE
    components = stacked // TILE
    held = components // pieces
    me = lax.axis_index("comp")
    ranks = [jnp.bitwise_xor(me, pair(q, pieces)) for q in range(pieces)]
    row_at = lax.broadcasted_iota(jnp.int32, (rows, cols), 0)
    col_at = lax.broadcasted_iota(jnp.int32, (rows, cols), 1)

    def product(weights, parts):
        highs, lows = zip(*[split(part) for part in parts])
        operand = jnp.concatenate(highs + highs + lows, axis=0)
        return jnp.dot(weights[...], operand, preferred_element_type=jnp.float32)

    weight_plus, weight_minus = face_weights(rate_ref[...], flag_ref[...])

    def column(side, at):
        return jnp.broadcast_to(side[:, at : at + 1], (rows, cols))

    def from_lower_row(value):
        return jnp.where(row_at == 0, 0.0, pltpu.roll(value, 1, 0))

    def from_upper_row(value):
        return jnp.where(row_at == rows - 1, 0.0, pltpu.roll(value, rows - 1, 0))

    def from_lower_col(value, edge):
        return jnp.where(col_at == 0, edge, pltpu.roll(value, 1, 1))

    def from_upper_col(value, edge):
        return jnp.where(col_at == cols - 1, edge, pltpu.roll(value, cols - 1, 1))

    block = rows // pieces
    if is_first:
        sides = []
        low_side, rim_at = low_ref[0], 2 * held * NZ
        turn = LANES - (me * (NZ // pieces) + layer)
        for q in range(pieces):
            side = pltpu.roll(low_ref[pair(q, pieces)], turn, 1)
            for index in range(held):
                sides.append((side, (held + index) * NZ, side, index * NZ))
    else:
        low_side, high_side, rim_at = low_ref[...], high_ref[...], 2 * components
        sides = [(low_side, components + at, high_side, at) for at in range(components)]
    down_plus = from_lower_row(weight_plus[0])
    down_minus = from_lower_row(weight_minus[0])
    side_plus = from_lower_col(weight_plus[1], column(low_side, rim_at))
    side_minus = from_lower_col(weight_minus[1], column(low_side, rim_at + 1))
    centre = down_minus + weight_plus[0] + side_minus + weight_plus[1]
    for at, (low_side, low_at, high_side, high_at) in enumerate(sides):
        q, index = divmod(at, held)
        value = value_refs[q][index * rows : (index + 1) * rows, :]
        component = ranks[q] * held + index
        spread = spread_ref[component]
        retard = 1.0 / jnp.full((rows, LANES), retard_ref[component], jnp.float32)
        retard = jnp.concatenate([retard] * (cols // LANES), axis=1)
        change = (
            (down_plus + spread) * from_lower_row(value)
            + (weight_minus[0] + spread) * from_upper_row(value)
            + (side_plus + spread) * from_lower_col(value, column(low_side, low_at))
            + (weight_minus[1] + spread) * from_upper_col(value, column(high_side, high_at))
            - (centre + 4.0 * spread) * value
        )
        value = value + change * retard
        for group in range(groups):
            offset_ref[group, at * TILE : (at + 1) * TILE, :] = value[
                group * TILE : (group + 1) * TILE
            ]

    for group in range(groups):
        offset = product(first_ref, [offset_ref[group]])
        offset_ref[group] = offset
        species_ref[group] = offset

    def plain_step(_, carry):
        for group in range(groups):
            species = species_ref[group]
            species_ref[group] = offset_ref[group] + product(both_ref, [species, jnp.tanh(species)])
        return carry

    lax.fori_loop(0, NEWT - 1, plain_step, 0, unroll=True)
    plain_ref[...] = species_ref[...]
    ratio = jnp.concatenate([ratio_ref[...]] * (cols // LANES), axis=1)

    def stiff_step(_, carry):
        for group in range(groups):
            species = species_ref[group]
            reaction = jnp.tanh(species) + ratio * jnp.tanh(species + species)
            species_ref[group] = offset_ref[group] + product(both_ref, [species, reaction])
        return carry

    lax.fori_loop(0, STIFF, stiff_step, 0, unroll=True)
    if is_first:
        for rank, value_ref in zip(ranks, value_refs):
            spot = pl.ds(pl.multiple_of(rank * block, TILE), block)
            stiff_ref[spot, :] = value_ref[held * rows : held * rows + block, :]
    for group in range(groups):
        spot = slice(group * TILE, (group + 1) * TILE)
        stiff = stiff_ref[spot, :] > 0.0
        for at in range(components):
            lane = slice(at * TILE, (at + 1) * TILE)
            start = at % held * rows + group * TILE
            out_refs[at // held][start : start + TILE, :] = jnp.where(
                stiff, species_ref[group, lane, :], plain_ref[group, lane, :]
            )
    if with_rim:
        edges = [ref[i * rows : (i + 1) * rows, :] for ref in out_refs for i in range(held)]
        columns = [value[:, :1] for value in edges] + [value[:, cols - 1 :] for value in edges]
        columns += [weight_plus[1][:, cols - 1 :], weight_minus[1][:, cols - 1 :]]
        rim_ref[...] = gather_columns(columns, rows)


def layer_step(values, stiff, low, high, shared, layer, with_rim):
    dispersion, retardation, face_rate, face_flag, ratio, first, both = shared
    pieces = len(values)
    rows, cols = face_rate.shape[1:]
    groups = rows // TILE
    stacked = ratio.shape[0]
    components = stacked // TILE
    scalar = pl.BlockSpec(memory_space=pltpu.SMEM)
    plane = jax.ShapeDtypeStruct((components // pieces * rows, cols), jnp.float32)
    out_shape = [plane] * pieces
    if with_rim:
        out_shape.append(jax.ShapeDtypeStruct((rows, LANES), jnp.float32))
    if stiff is None:
        out_shape.append(jax.ShapeDtypeStruct((rows, cols), jnp.float32))
    field = pltpu.VMEM((groups, stacked, cols), jnp.float32)
    cells = rows * cols
    operands = [dispersion, retardation, *values, low, high, face_rate, face_flag]
    operands += [ratio, first, both]
    if stiff is not None:
        operands.append(stiff)
    results = pl.pallas_call(
        functools.partial(step_kernel, pieces, layer, stiff is None, with_rim),
        out_shape=out_shape,
        in_specs=[scalar, scalar] + [whole_spec()] * (len(operands) - 2),
        out_specs=[whole_spec()] * len(out_shape),
        scratch_shapes=[field, field, field],
        compiler_params=pltpu.CompilerParams(vmem_limit_bytes=VMEM_LIMIT),
        cost_estimate=pl.CostEstimate(flops=0, bytes_accessed=0, transcendentals=0),
        name="layer_step",
    )(*operands)
    values, results = results[:pieces], results[pieces:]
    rims = results[0] if with_rim else None
    return values, (results[-1] if stiff is None else stiff), rims


def by_layers(
    concentration,
    face_rate,
    face_flag,
    retardation,
    dispersion,
    mixing,
    mixing_inverse,
    affinity,
    mineral,
    stiff_mask,
):
    ranks = lax.axis_size("comp")
    me = lax.axis_index("comp")
    planes, rows, cols = concentration.shape
    held = planes // NZ
    layers = NZ // ranks

    def send(value, by):
        return lax.ppermute(value, "comp", [(i, i ^ by) for i in range(ranks)]) if by else value

    def send_all(parts):
        return [send(part, pair(q, ranks)) for q, part in enumerate(parts)]

    messages, (edges,) = pack(concentration, stiff_mask, 0, ranks, (face_rate, face_flag))
    arrived = [send_all(messages)]

    from_low, from_high = shifted(edges, "space", 1), shifted(edges, "space", -1)
    lane_at = lax.broadcasted_iota(jnp.int32, edges.shape, 1)
    sides = jnp.where(lane_at < planes, from_high, from_low)[None]
    span = 1
    while span < ranks:
        sides = jnp.concatenate([sides, send(sides, span)])
        span *= 2

    for layer in range(1, layers):
        messages, _ = pack(concentration, stiff_mask, layer, ranks, ())
        messages, sides = lax.optimization_barrier((messages, sides))
        arrived.append(send_all(messages))

    first, both, ratio = spread_parameters(ranks, mixing, mixing_inverse, affinity, mineral, edges)
    shared = (dispersion, retardation, face_rate, face_flag, ratio, first, both)

    result = jnp.zeros((held, NZ, rows, cols), jnp.float32)
    for layer in range(layers):
        values, stiff = arrived[layer], None
        low, high = sides, sides
        for step in range(STEPS):
            last = step == STEPS - 1
            values, stiff, rims = layer_step(values, stiff, low, high, shared, layer, not last)
            if not last:
                low, high = shifted(rims, "space", 1), shifted(rims, "space", -1)
        for q, piece in enumerate(send_all(values)):
            result = lax.dynamic_update_slice(
                result,
                piece.reshape(held, 1, rows, cols),
                (0, (me ^ pair(q, ranks)) * layers + layer, 0, 0),
            )
    return result.reshape(planes, rows, cols)


def shards(concentration, face_rate, face_flag, *parameters):
    ranks = lax.axis_size("comp")
    planes, rows, cols = concentration.shape
    whole = NZ % ranks == 0 and planes % NZ == 0 and ranks & (ranks - 1) == 0
    narrow = 2 * max(NC, planes) + 2 <= LANES
    even = rows % (ranks * TILE) == 0 and cols % LANES == 0
    plan = by_layers if whole and narrow and even else by_rows
    return plan(concentration, face_rate, face_flag, *parameters)


def solution(mesh):
    in_specs = (
        P(("real", "comp"), None, "space"),
        P(None, "real", "space"),
        P(None, "real", "space"),
        P(),
        P(),
        P(),
        P(),
        P(),
        P(),
        P(None, ("real", "comp"), "space"),
    )
    out_specs = P(("real", "comp"), None, "space")
    return jax.shard_map(shards, mesh=mesh, in_specs=in_specs, out_specs=out_specs, check_vma=False)
```

```python
import functools

import jax
import jax.numpy as jnp
from jax import lax
from jax.experimental import pallas as pl
from jax.experimental.pallas import tpu as pltpu
from jax.sharding import PartitionSpec as P

NC = 16
NZ = 8
STEPS = 2
NEWT = 4
STIFF = 4


highest = lax.Precision.HIGHEST


def shifted(shard, axis, by):
    devices = lax.axis_size(axis)
    pairs = [(i, i + by) for i in range(devices) if 0 <= i + by < devices]
    return lax.ppermute(shard, axis, pairs)


def extended(block, sides, width):
    for axis, dim in sides:
        count = lax.axis_size(axis)
        forward = [(i, i + 1) for i in range(count - 1)]
        backward = [(target, source) for source, target in forward]
        low = lax.ppermute(
            lax.slice_in_dim(block, block.shape[dim] - width, None, axis=dim), axis, forward
        )
        high = lax.ppermute(lax.slice_in_dim(block, 0, width, axis=dim), axis, backward)
        block = jnp.concatenate([low, block, high], axis=dim)
    return block


def shift_down(values, axis_index):
    size_along = values.shape[axis_index]
    zero_row = jnp.zeros_like(lax.slice_in_dim(values, 0, 1, axis=axis_index))
    kept = lax.slice_in_dim(values, 0, size_along - 1, axis=axis_index)
    return jnp.concatenate([zero_row, kept], axis=axis_index)


def face_weights(face_rate, face_flag):
    flag_values = face_flag.astype(jnp.float32)
    weight_plus = face_rate * flag_values
    weight_minus = face_rate * (1.0 - flag_values)
    return (weight_plus, weight_minus)


def advance(
    values, lower_row, upper_row, lower_col, upper_col, coefficients, retard_planes, spread_planes
):
    divergence = (
        coefficients[0] * lower_row
        + coefficients[1] * upper_row
        + coefficients[2] * lower_col
        + coefficients[3] * upper_col
        - coefficients[4] * values
    )
    laplace = lower_row + upper_row + lower_col + upper_col - 4.0 * values
    return values + (divergence + spread_planes * laplace) / retard_planes


def residual_of(species, target, mixing, affinity, mineral, stiff):
    total = jnp.dot(
        mixing, species, precision=highest, preferred_element_type=jnp.float32
    ) + affinity[:, None] * jnp.tanh(species)
    if stiff:
        total = total + mineral[:, None] * jnp.tanh(2.0 * species)
    return total - target


def newton_steps(species, target, repeats, stiff, mixing, mixing_inverse, affinity, mineral):
    for iteration in range(repeats):
        update = residual_of(species, target, mixing, affinity, mineral, stiff)
        species = species - jnp.dot(
            mixing_inverse, update, precision=highest, preferred_element_type=jnp.float32
        )
    return species


def speciate(cell_block, stiff_mask, mixing, mixing_inverse, affinity, mineral):
    target = cell_block.reshape(NC, -1)
    flat_mask = stiff_mask.reshape(-1) > 0
    species = jnp.zeros_like(target)
    species = newton_steps(species, target, NEWT, False, mixing, mixing_inverse, affinity, mineral)
    stiffer = newton_steps(species, target, STIFF, True, mixing, mixing_inverse, affinity, mineral)
    species = jnp.where(flat_mask[None, :], stiffer, species)
    return species.reshape(cell_block.shape)


def by_rows(
    concentration,
    face_rate,
    face_flag,
    retardation,
    dispersion,
    mixing,
    mixing_inverse,
    affinity,
    mineral,
    stiff_mask,
):
    weight_plus, weight_minus = face_weights(face_rate, face_flag)
    rim_weights = jnp.stack([weight_plus[1, :, -1], weight_minus[1, :, -1]])
    left_rims = shifted(rim_weights, "space", 1)
    side_plus = jnp.concatenate([left_rims[0][:, None], weight_plus[1, :, :-1]], axis=1)
    side_minus = jnp.concatenate([left_rims[1][:, None], weight_minus[1, :, :-1]], axis=1)
    down_plus = shift_down(weight_plus[0], 0)
    down_minus = shift_down(weight_minus[0], 0)
    centre = down_minus + weight_plus[0] + side_minus + weight_plus[1]
    coefficients = jnp.stack([down_plus, weight_minus[0], side_plus, weight_minus[1], centre])
    retard_all = jnp.repeat(retardation, NZ)
    spread_all = jnp.repeat(dispersion, NZ)
    rows_held = stiff_mask.shape[1]
    row_start = lax.axis_index("comp") * rows_held
    cell_coefficients = lax.dynamic_slice_in_dim(coefficients, row_start, rows_held, 1)
    retard_planes = retard_all[:, None, None]
    spread_planes = spread_all[:, None, None]
    cell_block = lax.all_to_all(concentration, "comp", split_axis=1, concat_axis=0, tiled=True)
    for step_index in range(STEPS):
        padded = extended(cell_block, (("comp", 1), ("space", 2)), 1)
        cell_block = advance(
            cell_block,
            padded[:, :-2, 1:-1],
            padded[:, 2:, 1:-1],
            padded[:, 1:-1, :-2],
            padded[:, 1:-1, 2:],
            cell_coefficients,
            retard_planes,
            spread_planes,
        )
        cell_block = speciate(cell_block, stiff_mask, mixing, mixing_inverse, affinity, mineral)
    return lax.all_to_all(cell_block, "comp", split_axis=0, concat_axis=1, tiled=True)


TILE = 8
LANES = 128
VMEM_LIMIT = 24 * 1024 * 1024
MOST_VMEM = 60 * 1024 * 1024


def whole_spec():
    return pl.BlockSpec(memory_space=pltpu.VMEM)


def any_spec():
    return pl.BlockSpec(memory_space=pl.ANY)


def hbm_spec():
    return pl.BlockSpec(memory_space=pltpu.HBM)


def pair(q, ranks):
    return (ranks - q) % ranks


def split(value):
    high = value.astype(jnp.bfloat16)
    return high, (value - high.astype(jnp.float32)).astype(jnp.bfloat16)


def gather_columns(columns, rows):
    lane_at = lax.broadcasted_iota(jnp.int32, (rows, LANES), 1)
    gathered = jnp.zeros((rows, LANES), jnp.float32)
    for lane, column in enumerate(columns):
        gathered = jnp.where(lane_at == lane, jnp.broadcast_to(column, (rows, LANES)), gathered)
    return gathered


def bands(rows, cols):
    return -(-rows * LANES // (TILE * cols)) * TILE


def band_spots(rows, cols):
    wide = cols // LANES
    return [
        (group, group // wide * TILE, group % wide * LANES) for group in range(rows // TILE)
    ]


def pack_kernel(layer, plane_ref, mask_ref, *refs):
    if layer:
        (low_ref, high_ref), refs = refs[:2], refs[2:]
    out_refs, (part_ref, mask_part, mask_sems, in_sems, out_sems) = refs[:-5], refs[-5:]
    ranks = len(out_refs)
    planes, rows, cols = plane_ref.shape
    levels, block, _ = mask_ref.shape
    held = planes // levels
    me = lax.axis_index("comp")
    copies = []
    order = [*range(1, ranks), 0]

    def start(source, target, sem):
        copies.append(pltpu.make_async_copy(source, target, sem))
        copies[-1].start()

    for q in order:
        at = jnp.bitwise_xor(me, pair(q, ranks)) * (levels // ranks) + layer
        for index in range(held):
            spot = pl.ds(index * rows, rows)
            start(plane_ref.at[index * levels + at], part_ref.at[q, spot], in_sems.at[len(copies)])
        start(mask_ref.at[at], mask_part.at[q], mask_sems.at[q])
    arrivals = list(copies)
    copies.clear()
    if layer:
        lane_at = lax.broadcasted_iota(jnp.int32, (rows, LANES), 1)
        sides = jnp.where(lane_at < planes, high_ref[...], low_ref[...])
        for group, row, lane in band_spots(rows, cols):
            row += held * rows + block
            for q in order:
                part_ref[q, row : row + TILE, lane : lane + LANES] = sides[
                    group * TILE : (group + 1) * TILE
                ]
    for position, q in enumerate(order):
        for copy in arrivals[position * (held + 1) : (position + 1) * (held + 1)]:
            copy.wait()
        part_ref[q, held * rows : held * rows + block, :] = mask_part[q].astype(jnp.float32)
        start(part_ref.at[q], out_refs[q], out_sems.at[q])
    for copy in copies:
        copy.wait()


def pack(concentration, stiff_mask, layer, ranks, sides):
    planes, rows, cols = concentration.shape
    held = planes // NZ
    block = stiff_mask.shape[1]
    size = held * rows + block + (bands(rows, cols) if layer else 0)
    results = pl.pallas_call(
        functools.partial(pack_kernel, layer),
        out_shape=[jax.ShapeDtypeStruct((size, cols), jnp.float32)] * ranks,
        in_specs=[hbm_spec()] * 2 + [whole_spec()] * len(sides),
        out_specs=[any_spec()] * ranks,
        scratch_shapes=[
            pltpu.VMEM((ranks, size, cols), jnp.float32),
            pltpu.VMEM((ranks, block, cols), jnp.int32),
            pltpu.SemaphoreType.DMA((ranks,)),
            pltpu.SemaphoreType.DMA((ranks * (held + 1),)),
            pltpu.SemaphoreType.DMA((ranks,)),
        ],
        compiler_params=pltpu.CompilerParams(vmem_limit_bytes=VMEM_LIMIT if layer else MOST_VMEM),
        cost_estimate=pl.CostEstimate(flops=0, bytes_accessed=0, transcendentals=0),
        name="pack",
    )(concentration, stiff_mask, *sides)
    return list(results)


def plane_edges_kernel(first_ref, last_ref, rate_ref, flag_ref, *refs):
    planes, rows, _ = first_ref.shape
    weight_plus, weight_minus = face_weights(rate_ref[1], flag_ref[1])
    columns = [first_ref[plane][:, :1] for plane in range(planes)]
    columns += [last_ref[plane][:, LANES - 1 :] for plane in range(planes)]
    columns += [weight_plus[:, LANES - 1 :], weight_minus[:, LANES - 1 :]]
    refs[-1][...] = gather_columns(columns, rows)


def plane_edges(concentration, face_rate, face_flag, after):
    planes, rows, cols = concentration.shape
    last = cols // LANES - 1
    face = pl.BlockSpec((2, rows, LANES), lambda i: (0, 0, last))
    return pl.pallas_call(
        plane_edges_kernel,
        grid=(1,),
        out_shape=jax.ShapeDtypeStruct((rows, LANES), jnp.float32),
        in_specs=[
            pl.BlockSpec((planes, rows, LANES), lambda i: (0, 0, 0)),
            pl.BlockSpec((planes, rows, LANES), lambda i: (0, 0, last)),
            face,
            face,
        ]
        + [any_spec()] * len(after),
        out_specs=pl.BlockSpec((rows, LANES), lambda i: (0, 0)),
        compiler_params=pltpu.CompilerParams(vmem_limit_bytes=VMEM_LIMIT),
        cost_estimate=pl.CostEstimate(flops=0, bytes_accessed=0, transcendentals=0),
        name="plane_edges",
    )(concentration, concentration, face_rate, face_flag, *after)


def edges_kernel(held, *refs):
    half = (len(refs) - 4) // 2
    low_refs, high_refs, (rate_ref, flag_ref, _, out_ref) = refs[:half], refs[half:-4], refs[-4:]
    rows = rate_ref.shape[1]
    weight_plus, weight_minus = face_weights(rate_ref[1], flag_ref[1])
    spots = [slice(index * rows, (index + 1) * rows) for index in range(held)]
    columns = [ref[spot, :][:, :1] for ref in low_refs for spot in spots]
    columns += [ref[spot, :][:, LANES - 1 :] for ref in high_refs for spot in spots]
    columns += [weight_plus[:, LANES - 1 :], weight_minus[:, LANES - 1 :]]
    out_ref[...] = gather_columns(columns, rows)


def edges_of(values, face_rate, face_flag, after):
    rows, cols = face_rate.shape[1:]
    last = cols // LANES - 1
    size = values[0].shape[0]
    low = pl.BlockSpec((size, LANES), lambda i: (0, 0))
    high = pl.BlockSpec((size, LANES), lambda i: (0, last))
    face = pl.BlockSpec((2, rows, LANES), lambda i: (0, 0, last))
    return pl.pallas_call(
        functools.partial(edges_kernel, size // rows),
        grid=(1,),
        out_shape=jax.ShapeDtypeStruct((rows, LANES), jnp.float32),
        in_specs=[low] * len(values) + [high] * len(values) + [face, face, hbm_spec()],
        out_specs=pl.BlockSpec((rows, LANES), lambda i: (0, 0)),
        compiler_params=pltpu.CompilerParams(vmem_limit_bytes=VMEM_LIMIT),
        cost_estimate=pl.CostEstimate(flops=0, bytes_accessed=0, transcendentals=0),
        name="edges",
    )(*values, *values, face_rate, face_flag, after)


def spread_kernel(ranks, mixing_ref, inverse_ref, affinity_ref, mineral_ref, *refs):
    _, first_ref, both_ref, ratio_ref = refs
    components = mixing_ref.shape[0]
    stacked = components * TILE
    held = components // ranks
    me = lax.axis_index("comp")

    def dot(left, right):
        return jnp.dot(left, right, precision=highest, preferred_element_type=jnp.float32)

    def pick(shape, stacked_dim):
        at = lax.broadcasted_iota(jnp.int32, shape, stacked_dim) // TILE
        component = jnp.bitwise_xor(me, pair(at // held, ranks)) * held + lax.rem(at, held)
        held_at = lax.broadcasted_iota(jnp.int32, shape, 1 - stacked_dim)
        return jnp.where(component == held_at, 1.0, 0.0)

    rows = pick((stacked, components), 0)
    cols = pick((components, stacked), 1)
    inner = (stacked, stacked)
    same = lax.rem(lax.broadcasted_iota(jnp.int32, inner, 0), TILE) == lax.rem(
        lax.broadcasted_iota(jnp.int32, inner, 1), TILE
    )

    def spread(matrix):
        return jnp.where(same, dot(dot(rows, matrix), cols), 0.0)

    inverse = inverse_ref[...]
    square = (components, components)
    unit = jnp.where(
        lax.broadcasted_iota(jnp.int32, square, 0) == lax.broadcasted_iota(jnp.int32, square, 1),
        1.0,
        0.0,
    )
    blend = unit - dot(inverse, mixing_ref[...])
    high, low = split(spread(inverse))
    first_ref[...] = jnp.concatenate([high, low, high], axis=1)
    high, low = split(
        jnp.concatenate([spread(blend), spread(-inverse * affinity_ref[...])], axis=1)
    )
    both_ref[...] = jnp.concatenate([high, low, high], axis=1)
    ratio = jnp.sum(rows * (mineral_ref[...] / affinity_ref[...]), axis=1, keepdims=True)
    ratio_ref[...] = jnp.broadcast_to(ratio, (stacked, LANES))


def spread_parameters(ranks, mixing, mixing_inverse, affinity, mineral, after):
    components = mixing.shape[0]
    stacked = components * TILE
    return pl.pallas_call(
        functools.partial(spread_kernel, ranks),
        out_shape=[
            jax.ShapeDtypeStruct((stacked, 3 * stacked), jnp.bfloat16),
            jax.ShapeDtypeStruct((stacked, 6 * stacked), jnp.bfloat16),
            jax.ShapeDtypeStruct((stacked, LANES), jnp.float32),
        ],
        in_specs=[whole_spec()] * 4 + [any_spec()],
        out_specs=[whole_spec()] * 3,
        compiler_params=pltpu.CompilerParams(vmem_limit_bytes=VMEM_LIMIT),
        cost_estimate=pl.CostEstimate(flops=0, bytes_accessed=0, transcendentals=0),
        name="spread_parameters",
    )(mixing, mixing_inverse, affinity.reshape(1, -1), mineral.reshape(1, -1), after)


def step_kernel(pieces, layer, is_first, with_rim, spread_ref, retard_ref, *refs):
    value_refs, refs = refs[:pieces], refs[pieces:]
    (low_ref, high_ref, rate_ref, flag_ref, ratio_ref, first_ref, both_ref), refs = (
        refs[:7],
        refs[7:],
    )
    if not is_first:
        stiff_ref, refs = refs[0], refs[1:]
    out_refs, refs = refs[:pieces], refs[pieces:]
    if with_rim:
        rim_ref, refs = refs[0], refs[1:]
    if is_first:
        stiff_ref, refs = refs[0], refs[1:]
    offset_ref, species_ref, plain_ref = refs
    groups, stacked, cols = species_ref.shape
    rows = groups * TILE
    components = stacked // TILE
    held = components // pieces
    me = lax.axis_index("comp")
    ranks = [jnp.bitwise_xor(me, pair(q, pieces)) for q in range(pieces)]
    row_at = lax.broadcasted_iota(jnp.int32, (rows, cols), 0)
    col_at = lax.broadcasted_iota(jnp.int32, (rows, cols), 1)

    def product(weights, parts):
        highs, lows = zip(*[split(part) for part in parts])
        operand = jnp.concatenate(highs + highs + lows, axis=0)
        return jnp.dot(weights[...], operand, preferred_element_type=jnp.float32)

    weight_plus, weight_minus = face_weights(rate_ref[...], flag_ref[...])

    def column(side, at):
        return jnp.broadcast_to(side[:, at : at + 1], (rows, cols))

    def from_lower_row(value):
        return jnp.where(row_at == 0, 0.0, pltpu.roll(value, 1, 0))

    def from_upper_row(value):
        return jnp.where(row_at == rows - 1, 0.0, pltpu.roll(value, rows - 1, 0))

    def from_lower_col(value, edge):
        return jnp.where(col_at == 0, edge, pltpu.roll(value, 1, 1))

    def from_upper_col(value, edge):
        return jnp.where(col_at == cols - 1, edge, pltpu.roll(value, cols - 1, 1))

    block = rows // pieces
    if is_first and layer:
        sides, rim_at = [], 2 * held * NZ
        turn = LANES - (me * (NZ // pieces) + layer)
        for value_ref in value_refs:
            start = held * rows + block
            side = jnp.concatenate(
                [
                    value_ref[start + row : start + row + TILE, lane : lane + LANES]
                    for _, row, lane in band_spots(rows, cols)
                ]
            )
            if not sides:
                low_side = side
            side = pltpu.roll(side, turn, 1)
            for index in range(held):
                sides.append((side, (held + index) * NZ, side, index * NZ))
    else:
        low_side, high_side, rim_at = low_ref[...], high_ref[...], 2 * components
        sides = [(low_side, components + at, high_side, at) for at in range(components)]
    down_plus = from_lower_row(weight_plus[0])
    down_minus = from_lower_row(weight_minus[0])
    side_plus = from_lower_col(weight_plus[1], column(low_side, rim_at))
    side_minus = from_lower_col(weight_minus[1], column(low_side, rim_at + 1))
    centre = down_minus + weight_plus[0] + side_minus + weight_plus[1]
    for at, (low_side, low_at, high_side, high_at) in enumerate(sides):
        q, index = divmod(at, held)
        value = value_refs[q][index * rows : (index + 1) * rows, :]
        component = ranks[q] * held + index
        spread = spread_ref[component]
        retard = 1.0 / jnp.full((rows, LANES), retard_ref[component], jnp.float32)
        retard = jnp.concatenate([retard] * (cols // LANES), axis=1)
        change = (
            (down_plus + spread) * from_lower_row(value)
            + (weight_minus[0] + spread) * from_upper_row(value)
            + (side_plus + spread) * from_lower_col(value, column(low_side, low_at))
            + (weight_minus[1] + spread) * from_upper_col(value, column(high_side, high_at))
            - (centre + 4.0 * spread) * value
        )
        value = value + change * retard
        for group in range(groups):
            offset_ref[group, at * TILE : (at + 1) * TILE, :] = value[
                group * TILE : (group + 1) * TILE
            ]

    for group in range(groups):
        offset = product(first_ref, [offset_ref[group]])
        offset_ref[group] = offset
        species_ref[group] = offset

    def plain_step(_, carry):
        for group in range(groups):
            species = species_ref[group]
            species_ref[group] = offset_ref[group] + product(both_ref, [species, jnp.tanh(species)])
        return carry

    lax.fori_loop(0, NEWT - 1, plain_step, 0, unroll=True)
    plain_ref[...] = species_ref[...]
    ratio = jnp.concatenate([ratio_ref[...]] * (cols // LANES), axis=1)

    def stiff_step(_, carry):
        for group in range(groups):
            species = species_ref[group]
            reaction = jnp.tanh(species) + ratio * jnp.tanh(species + species)
            species_ref[group] = offset_ref[group] + product(both_ref, [species, reaction])
        return carry

    lax.fori_loop(0, STIFF, stiff_step, 0, unroll=True)
    if is_first:
        for rank, value_ref in zip(ranks, value_refs):
            spot = pl.ds(pl.multiple_of(rank * block, TILE), block)
            stiff_ref[spot, :] = value_ref[held * rows : held * rows + block, :]
    for group in range(groups):
        spot = slice(group * TILE, (group + 1) * TILE)
        stiff = stiff_ref[spot, :] > 0.0
        for at in range(components):
            lane = slice(at * TILE, (at + 1) * TILE)
            start = at % held * rows + group * TILE
            out_refs[at // held][start : start + TILE, :] = jnp.where(
                stiff, species_ref[group, lane, :], plain_ref[group, lane, :]
            )
    if with_rim:
        edges = [ref[i * rows : (i + 1) * rows, :] for ref in out_refs for i in range(held)]
        columns = [value[:, :1] for value in edges] + [value[:, cols - 1 :] for value in edges]
        columns += [weight_plus[1][:, cols - 1 :], weight_minus[1][:, cols - 1 :]]
        rim_ref[...] = gather_columns(columns, rows)


def layer_step(values, stiff, low, high, shared, layer, with_rim):
    dispersion, retardation, face_rate, face_flag, ratio, first, both = shared
    pieces = len(values)
    rows, cols = face_rate.shape[1:]
    groups = rows // TILE
    stacked = ratio.shape[0]
    components = stacked // TILE
    scalar = pl.BlockSpec(memory_space=pltpu.SMEM)
    plane = jax.ShapeDtypeStruct((components // pieces * rows, cols), jnp.float32)
    out_shape = [plane] * pieces
    if with_rim:
        out_shape.append(jax.ShapeDtypeStruct((rows, LANES), jnp.float32))
    if stiff is None:
        out_shape.append(jax.ShapeDtypeStruct((rows, cols), jnp.float32))
    field = pltpu.VMEM((groups, stacked, cols), jnp.float32)
    cells = rows * cols
    operands = [dispersion, retardation, *values, low, high, face_rate, face_flag]
    operands += [ratio, first, both]
    if stiff is not None:
        operands.append(stiff)
    results = pl.pallas_call(
        functools.partial(step_kernel, pieces, layer, stiff is None, with_rim),
        out_shape=out_shape,
        in_specs=[scalar, scalar] + [whole_spec()] * (len(operands) - 2),
        out_specs=[whole_spec()] * len(out_shape),
        scratch_shapes=[field, field, field],
        compiler_params=pltpu.CompilerParams(vmem_limit_bytes=VMEM_LIMIT),
        cost_estimate=pl.CostEstimate(flops=0, bytes_accessed=0, transcendentals=0),
        name="layer_step",
    )(*operands)
    values, results = results[:pieces], results[pieces:]
    rims = results[0] if with_rim else None
    return values, (results[-1] if stiff is None else stiff), rims


def by_layers(
    concentration,
    face_rate,
    face_flag,
    retardation,
    dispersion,
    mixing,
    mixing_inverse,
    affinity,
    mineral,
    stiff_mask,
):
    ranks = lax.axis_size("comp")
    me = lax.axis_index("comp")
    planes, rows, cols = concentration.shape
    held = planes // NZ
    layers = NZ // ranks

    def send(value, by):
        return lax.ppermute(value, "comp", [(i, i ^ by) for i in range(ranks)]) if by else value

    def send_all(parts):
        return [send(part, pair(q, ranks)) for q, part in enumerate(parts)]

    messages = pack(concentration, stiff_mask, 0, ranks, ())
    arrived = [send_all(messages)]
    if layers > 1:
        edges = plane_edges(concentration, face_rate, face_flag, messages[:1])
        sides = (shifted(edges, "space", 1), shifted(edges, "space", -1))
    for layer in range(1, layers):
        messages = pack(concentration, stiff_mask, layer, ranks, sides)
        messages, arrived[-1] = lax.optimization_barrier((messages, arrived[-1]))
        arrived.append(send_all(messages))

    first, both, ratio = spread_parameters(ranks, mixing, mixing_inverse, affinity, mineral, messages[0]
    )
    shared = (dispersion, retardation, face_rate, face_flag, ratio, first, both)

    result = jnp.zeros((held, NZ, rows, cols), jnp.float32)
    for layer in range(layers):
        values, stiff = arrived[layer], None
        rims = None if layer else edges_of(values, face_rate, face_flag, messages[0])
        for step in range(STEPS):
            if rims is None:
                low, high = sides
            else:
                low, high = shifted(rims, "space", 1), shifted(rims, "space", -1)
            values, stiff, rims = layer_step(
                values, stiff, low, high, shared, layer, step < STEPS - 1
            )
        for q, piece in enumerate(send_all(values)):
            result = lax.dynamic_update_slice(
                result,
                piece.reshape(held, 1, rows, cols),
                (0, (me ^ pair(q, ranks)) * layers + layer, 0, 0),
            )
    return result.reshape(planes, rows, cols)


def shards(concentration, face_rate, face_flag, *parameters):
    ranks = lax.axis_size("comp")
    planes, rows, cols = concentration.shape
    whole = NZ % ranks == 0 and planes % NZ == 0 and ranks & (ranks - 1) == 0
    narrow = 2 * max(NC, planes) + 2 <= LANES
    even = rows % (ranks * TILE) == 0 and cols % LANES == 0
    plan = by_layers if whole and narrow and even else by_rows
    return plan(concentration, face_rate, face_flag, *parameters)


def solution(mesh):
    in_specs = (
        P(("real", "comp"), None, "space"),
        P(None, "real", "space"),
        P(None, "real", "space"),
        P(),
        P(),
        P(),
        P(),
        P(),
        P(),
        P(None, ("real", "comp"), "space"),
    )
    out_specs = P(("real", "comp"), None, "space")
    return jax.shard_map(shards, mesh=mesh, in_specs=in_specs, out_specs=out_specs, check_vma=False)
```

```python
import functools

import jax
import jax.numpy as jnp
from jax import lax
from jax.experimental import pallas as pl
from jax.experimental.pallas import tpu as pltpu
from jax.sharding import PartitionSpec as P

NC = 16
NZ = 8
STEPS = 2
NEWT = 4
STIFF = 4


highest = lax.Precision.HIGHEST


def shifted(shard, axis, by):
    devices = lax.axis_size(axis)
    pairs = [(i, i + by) for i in range(devices) if 0 <= i + by < devices]
    return lax.ppermute(shard, axis, pairs)


def extended(block, sides, width):
    for axis, dim in sides:
        count = lax.axis_size(axis)
        forward = [(i, i + 1) for i in range(count - 1)]
        backward = [(target, source) for source, target in forward]
        low = lax.ppermute(
            lax.slice_in_dim(block, block.shape[dim] - width, None, axis=dim), axis, forward
        )
        high = lax.ppermute(lax.slice_in_dim(block, 0, width, axis=dim), axis, backward)
        block = jnp.concatenate([low, block, high], axis=dim)
    return block


def shift_down(values, axis_index):
    size_along = values.shape[axis_index]
    zero_row = jnp.zeros_like(lax.slice_in_dim(values, 0, 1, axis=axis_index))
    kept = lax.slice_in_dim(values, 0, size_along - 1, axis=axis_index)
    return jnp.concatenate([zero_row, kept], axis=axis_index)


def face_weights(face_rate, face_flag):
    flag_values = face_flag.astype(jnp.float32)
    weight_plus = face_rate * flag_values
    weight_minus = face_rate * (1.0 - flag_values)
    return (weight_plus, weight_minus)


def advance(
    values, lower_row, upper_row, lower_col, upper_col, coefficients, retard_planes, spread_planes
):
    divergence = (
        coefficients[0] * lower_row
        + coefficients[1] * upper_row
        + coefficients[2] * lower_col
        + coefficients[3] * upper_col
        - coefficients[4] * values
    )
    laplace = lower_row + upper_row + lower_col + upper_col - 4.0 * values
    return values + (divergence + spread_planes * laplace) / retard_planes


def residual_of(species, target, mixing, affinity, mineral, stiff):
    total = jnp.dot(
        mixing, species, precision=highest, preferred_element_type=jnp.float32
    ) + affinity[:, None] * jnp.tanh(species)
    if stiff:
        total = total + mineral[:, None] * jnp.tanh(2.0 * species)
    return total - target


def newton_steps(species, target, repeats, stiff, mixing, mixing_inverse, affinity, mineral):
    for iteration in range(repeats):
        update = residual_of(species, target, mixing, affinity, mineral, stiff)
        species = species - jnp.dot(
            mixing_inverse, update, precision=highest, preferred_element_type=jnp.float32
        )
    return species


def speciate(cell_block, stiff_mask, mixing, mixing_inverse, affinity, mineral):
    target = cell_block.reshape(NC, -1)
    flat_mask = stiff_mask.reshape(-1) > 0
    species = jnp.zeros_like(target)
    species = newton_steps(species, target, NEWT, False, mixing, mixing_inverse, affinity, mineral)
    stiffer = newton_steps(species, target, STIFF, True, mixing, mixing_inverse, affinity, mineral)
    species = jnp.where(flat_mask[None, :], stiffer, species)
    return species.reshape(cell_block.shape)


def by_rows(
    concentration,
    face_rate,
    face_flag,
    retardation,
    dispersion,
    mixing,
    mixing_inverse,
    affinity,
    mineral,
    stiff_mask,
):
    weight_plus, weight_minus = face_weights(face_rate, face_flag)
    rim_weights = jnp.stack([weight_plus[1, :, -1], weight_minus[1, :, -1]])
    left_rims = shifted(rim_weights, "space", 1)
    side_plus = jnp.concatenate([left_rims[0][:, None], weight_plus[1, :, :-1]], axis=1)
    side_minus = jnp.concatenate([left_rims[1][:, None], weight_minus[1, :, :-1]], axis=1)
    down_plus = shift_down(weight_plus[0], 0)
    down_minus = shift_down(weight_minus[0], 0)
    centre = down_minus + weight_plus[0] + side_minus + weight_plus[1]
    coefficients = jnp.stack([down_plus, weight_minus[0], side_plus, weight_minus[1], centre])
    retard_all = jnp.repeat(retardation, NZ)
    spread_all = jnp.repeat(dispersion, NZ)
    rows_held = stiff_mask.shape[1]
    row_start = lax.axis_index("comp") * rows_held
    cell_coefficients = lax.dynamic_slice_in_dim(coefficients, row_start, rows_held, 1)
    retard_planes = retard_all[:, None, None]
    spread_planes = spread_all[:, None, None]
    cell_block = lax.all_to_all(concentration, "comp", split_axis=1, concat_axis=0, tiled=True)
    for step_index in range(STEPS):
        padded = extended(cell_block, (("comp", 1), ("space", 2)), 1)
        cell_block = advance(
            cell_block,
            padded[:, :-2, 1:-1],
            padded[:, 2:, 1:-1],
            padded[:, 1:-1, :-2],
            padded[:, 1:-1, 2:],
            cell_coefficients,
            retard_planes,
            spread_planes,
        )
        cell_block = speciate(cell_block, stiff_mask, mixing, mixing_inverse, affinity, mineral)
    return lax.all_to_all(cell_block, "comp", split_axis=0, concat_axis=1, tiled=True)


TILE = 8
LANES = 128
VMEM_LIMIT = 24 * 1024 * 1024
MOST_VMEM = 60 * 1024 * 1024


def whole_spec():
    return pl.BlockSpec(memory_space=pltpu.VMEM)


def any_spec():
    return pl.BlockSpec(memory_space=pl.ANY)


def hbm_spec():
    return pl.BlockSpec(memory_space=pltpu.HBM)


def pair(q, ranks):
    return (ranks - q) % ranks


def paired(value, first):
    low = range(first, lax.axis_size("space") - 1, 2)
    return lax.ppermute(value, "space", [(i, i + 1) for i in low] + [(i + 1, i) for i in low])


def by_side(even_ref, odd_ref):
    upward = lax.rem(lax.axis_index("space"), 2) == 0
    even, odd = even_ref[...], odd_ref[...]
    return jnp.where(upward, odd, even), jnp.where(upward, even, odd)


def split(value):
    high = value.astype(jnp.bfloat16)
    return high, (value - high.astype(jnp.float32)).astype(jnp.bfloat16)


def gather_columns(columns, rows):
    lane_at = lax.broadcasted_iota(jnp.int32, (rows, LANES), 1)
    gathered = jnp.zeros((rows, LANES), jnp.float32)
    for lane, column in enumerate(columns):
        gathered = jnp.where(lane_at == lane, jnp.broadcast_to(column, (rows, LANES)), gathered)
    return gathered


def bands(rows, cols):
    return -(-rows * LANES // (TILE * cols)) * TILE


def band_spots(rows, cols):
    wide = cols // LANES
    return [
        (group, group // wide * TILE, group % wide * LANES) for group in range(rows // TILE)
    ]


def pack_kernel(layer, plane_ref, mask_ref, *refs):
    if layer:
        (low_ref, high_ref), refs = refs[:2], refs[2:]
    out_refs, (part_ref, mask_part, mask_sems, in_sems, out_sems) = refs[:-5], refs[-5:]
    ranks = len(out_refs)
    planes, rows, cols = plane_ref.shape
    levels, block, _ = mask_ref.shape
    held = planes // levels
    me = lax.axis_index("comp")
    copies = []
    order = [*range(1, ranks), 0]

    def start(source, target, sem):
        copies.append(pltpu.make_async_copy(source, target, sem))
        copies[-1].start()

    for q in order:
        at = jnp.bitwise_xor(me, pair(q, ranks)) * (levels // ranks) + layer
        for index in range(held):
            spot = pl.ds(index * rows, rows)
            start(plane_ref.at[index * levels + at], part_ref.at[q, spot], in_sems.at[len(copies)])
        start(mask_ref.at[at], mask_part.at[q], mask_sems.at[q])
    arrivals = list(copies)
    copies.clear()
    if layer:
        lane_at = lax.broadcasted_iota(jnp.int32, (rows, LANES), 1)
        low_side, high_side = by_side(low_ref, high_ref)
        sides = jnp.where(lane_at < planes, high_side, low_side)
        for group, row, lane in band_spots(rows, cols):
            row += held * rows + block
            for q in order:
                part_ref[q, row : row + TILE, lane : lane + LANES] = sides[
                    group * TILE : (group + 1) * TILE
                ]
    for position, q in enumerate(order):
        for copy in arrivals[position * (held + 1) : (position + 1) * (held + 1)]:
            copy.wait()
        part_ref[q, held * rows : held * rows + block, :] = mask_part[q].astype(jnp.float32)
        start(part_ref.at[q], out_refs[q], out_sems.at[q])
    for copy in copies:
        copy.wait()


def pack(concentration, stiff_mask, layer, ranks, sides):
    planes, rows, cols = concentration.shape
    held = planes // NZ
    block = stiff_mask.shape[1]
    size = held * rows + block + (bands(rows, cols) if layer else 0)
    results = pl.pallas_call(
        functools.partial(pack_kernel, layer),
        out_shape=[jax.ShapeDtypeStruct((size, cols), jnp.float32)] * ranks,
        in_specs=[hbm_spec()] * 2 + [whole_spec()] * len(sides),
        out_specs=[any_spec()] * ranks,
        scratch_shapes=[
            pltpu.VMEM((ranks, size, cols), jnp.float32),
            pltpu.VMEM((ranks, block, cols), jnp.int32),
            pltpu.SemaphoreType.DMA((ranks,)),
            pltpu.SemaphoreType.DMA((ranks * (held + 1),)),
            pltpu.SemaphoreType.DMA((ranks,)),
        ],
        compiler_params=pltpu.CompilerParams(vmem_limit_bytes=VMEM_LIMIT if layer else MOST_VMEM),
        cost_estimate=pl.CostEstimate(flops=0, bytes_accessed=0, transcendentals=0),
        name="pack",
    )(concentration, stiff_mask, *sides)
    return list(results)


def plane_edges_kernel(first_ref, last_ref, rate_ref, flag_ref, *refs):
    planes, rows, _ = first_ref.shape
    weight_plus, weight_minus = face_weights(rate_ref[1], flag_ref[1])
    columns = [first_ref[plane][:, :1] for plane in range(planes)]
    columns += [last_ref[plane][:, LANES - 1 :] for plane in range(planes)]
    columns += [weight_plus[:, LANES - 1 :], weight_minus[:, LANES - 1 :]]
    refs[-1][...] = gather_columns(columns, rows)


def plane_edges(concentration, face_rate, face_flag, after):
    planes, rows, cols = concentration.shape
    last = cols // LANES - 1
    face = pl.BlockSpec((2, rows, LANES), lambda i: (0, 0, last))
    return pl.pallas_call(
        plane_edges_kernel,
        grid=(1,),
        out_shape=jax.ShapeDtypeStruct((rows, LANES), jnp.float32),
        in_specs=[
            pl.BlockSpec((planes, rows, LANES), lambda i: (0, 0, 0)),
            pl.BlockSpec((planes, rows, LANES), lambda i: (0, 0, last)),
            face,
            face,
        ]
        + [any_spec()] * len(after),
        out_specs=pl.BlockSpec((rows, LANES), lambda i: (0, 0)),
        compiler_params=pltpu.CompilerParams(vmem_limit_bytes=VMEM_LIMIT),
        cost_estimate=pl.CostEstimate(flops=0, bytes_accessed=0, transcendentals=0),
        name="plane_edges",
    )(concentration, concentration, face_rate, face_flag, *after)


def edges_kernel(held, *refs):
    half = (len(refs) - 4) // 2
    low_refs, high_refs, (rate_ref, flag_ref, _, out_ref) = refs[:half], refs[half:-4], refs[-4:]
    rows = rate_ref.shape[1]
    weight_plus, weight_minus = face_weights(rate_ref[1], flag_ref[1])
    spots = [slice(index * rows, (index + 1) * rows) for index in range(held)]
    columns = [ref[spot, :][:, :1] for ref in low_refs for spot in spots]
    columns += [ref[spot, :][:, LANES - 1 :] for ref in high_refs for spot in spots]
    columns += [weight_plus[:, LANES - 1 :], weight_minus[:, LANES - 1 :]]
    out_ref[...] = gather_columns(columns, rows)


def edges_of(values, face_rate, face_flag, after):
    rows, cols = face_rate.shape[1:]
    last = cols // LANES - 1
    size = values[0].shape[0]
    low = pl.BlockSpec((size, LANES), lambda i: (0, 0))
    high = pl.BlockSpec((size, LANES), lambda i: (0, last))
    face = pl.BlockSpec((2, rows, LANES), lambda i: (0, 0, last))
    return pl.pallas_call(
        functools.partial(edges_kernel, size // rows),
        grid=(1,),
        out_shape=jax.ShapeDtypeStruct((rows, LANES), jnp.float32),
        in_specs=[low] * len(values) + [high] * len(values) + [face, face, hbm_spec()],
        out_specs=pl.BlockSpec((rows, LANES), lambda i: (0, 0)),
        compiler_params=pltpu.CompilerParams(vmem_limit_bytes=VMEM_LIMIT),
        cost_estimate=pl.CostEstimate(flops=0, bytes_accessed=0, transcendentals=0),
        name="edges",
    )(*values, *values, face_rate, face_flag, after)


def spread_kernel(ranks, mixing_ref, inverse_ref, affinity_ref, mineral_ref, *refs):
    _, first_ref, both_ref, ratio_ref = refs
    components = mixing_ref.shape[0]
    stacked = components * TILE
    held = components // ranks
    me = lax.axis_index("comp")

    def dot(left, right):
        return jnp.dot(left, right, precision=highest, preferred_element_type=jnp.float32)

    def pick(shape, stacked_dim):
        at = lax.broadcasted_iota(jnp.int32, shape, stacked_dim) // TILE
        component = jnp.bitwise_xor(me, pair(at // held, ranks)) * held + lax.rem(at, held)
        held_at = lax.broadcasted_iota(jnp.int32, shape, 1 - stacked_dim)
        return jnp.where(component == held_at, 1.0, 0.0)

    rows = pick((stacked, components), 0)
    cols = pick((components, stacked), 1)
    inner = (stacked, stacked)
    same = lax.rem(lax.broadcasted_iota(jnp.int32, inner, 0), TILE) == lax.rem(
        lax.broadcasted_iota(jnp.int32, inner, 1), TILE
    )

    def spread(matrix):
        return jnp.where(same, dot(dot(rows, matrix), cols), 0.0)

    inverse = inverse_ref[...]
    square = (components, components)
    unit = jnp.where(
        lax.broadcasted_iota(jnp.int32, square, 0) == lax.broadcasted_iota(jnp.int32, square, 1),
        1.0,
        0.0,
    )
    blend = unit - dot(inverse, mixing_ref[...])
    high, low = split(spread(inverse))
    first_ref[...] = jnp.concatenate([high, low, high], axis=1)
    high, low = split(
        jnp.concatenate([spread(blend), spread(-inverse * affinity_ref[...])], axis=1)
    )
    both_ref[...] = jnp.concatenate([high, low, high], axis=1)
    ratio = jnp.sum(rows * (mineral_ref[...] / affinity_ref[...]), axis=1, keepdims=True)
    ratio_ref[...] = jnp.broadcast_to(ratio, (stacked, LANES))


def spread_parameters(ranks, mixing, mixing_inverse, affinity, mineral, after):
    components = mixing.shape[0]
    stacked = components * TILE
    return pl.pallas_call(
        functools.partial(spread_kernel, ranks),
        out_shape=[
            jax.ShapeDtypeStruct((stacked, 3 * stacked), jnp.bfloat16),
            jax.ShapeDtypeStruct((stacked, 6 * stacked), jnp.bfloat16),
            jax.ShapeDtypeStruct((stacked, LANES), jnp.float32),
        ],
        in_specs=[whole_spec()] * 4 + [any_spec()],
        out_specs=[whole_spec()] * 3,
        compiler_params=pltpu.CompilerParams(vmem_limit_bytes=VMEM_LIMIT),
        cost_estimate=pl.CostEstimate(flops=0, bytes_accessed=0, transcendentals=0),
        name="spread_parameters",
    )(mixing, mixing_inverse, affinity.reshape(1, -1), mineral.reshape(1, -1), after)


def step_kernel(pieces, layer, is_first, with_rim, spread_ref, retard_ref, *refs):
    value_refs, refs = refs[:pieces], refs[pieces:]
    (low_ref, high_ref, rate_ref, flag_ref, ratio_ref, first_ref, both_ref), refs = (
        refs[:7],
        refs[7:],
    )
    if not is_first:
        stiff_ref, refs = refs[0], refs[1:]
    out_refs, refs = refs[:pieces], refs[pieces:]
    if with_rim:
        rim_ref, refs = refs[0], refs[1:]
    if is_first:
        stiff_ref, refs = refs[0], refs[1:]
    offset_ref, species_ref, plain_ref = refs
    groups, stacked, cols = species_ref.shape
    rows = groups * TILE
    components = stacked // TILE
    held = components // pieces
    me = lax.axis_index("comp")
    ranks = [jnp.bitwise_xor(me, pair(q, pieces)) for q in range(pieces)]
    row_at = lax.broadcasted_iota(jnp.int32, (rows, cols), 0)
    col_at = lax.broadcasted_iota(jnp.int32, (rows, cols), 1)

    def product(weights, parts):
        highs, lows = zip(*[split(part) for part in parts])
        operand = jnp.concatenate(highs + highs + lows, axis=0)
        return jnp.dot(weights[...], operand, preferred_element_type=jnp.float32)

    weight_plus, weight_minus = face_weights(rate_ref[...], flag_ref[...])

    def column(side, at):
        return jnp.broadcast_to(side[:, at : at + 1], (rows, cols))

    def from_lower_row(value):
        return jnp.where(row_at == 0, 0.0, pltpu.roll(value, 1, 0))

    def from_upper_row(value):
        return jnp.where(row_at == rows - 1, 0.0, pltpu.roll(value, rows - 1, 0))

    def from_lower_col(value, edge):
        return jnp.where(col_at == 0, edge, pltpu.roll(value, 1, 1))

    def from_upper_col(value, edge):
        return jnp.where(col_at == cols - 1, edge, pltpu.roll(value, cols - 1, 1))

    block = rows // pieces
    if is_first and layer:
        sides, rim_at = [], 2 * held * NZ
        turn = LANES - (me * (NZ // pieces) + layer)
        for value_ref in value_refs:
            start = held * rows + block
            side = jnp.concatenate(
                [
                    value_ref[start + row : start + row + TILE, lane : lane + LANES]
                    for _, row, lane in band_spots(rows, cols)
                ]
            )
            if not sides:
                low_side = side
            side = pltpu.roll(side, turn, 1)
            for index in range(held):
                sides.append((side, (held + index) * NZ, side, index * NZ))
    else:
        low_side, high_side = by_side(low_ref, high_ref)
        rim_at = 2 * components
        sides = [(low_side, components + at, high_side, at) for at in range(components)]
    down_plus = from_lower_row(weight_plus[0])
    down_minus = from_lower_row(weight_minus[0])
    side_plus = from_lower_col(weight_plus[1], column(low_side, rim_at))
    side_minus = from_lower_col(weight_minus[1], column(low_side, rim_at + 1))
    centre = down_minus + weight_plus[0] + side_minus + weight_plus[1]
    for at, (low_side, low_at, high_side, high_at) in enumerate(sides):
        q, index = divmod(at, held)
        value = value_refs[q][index * rows : (index + 1) * rows, :]
        component = ranks[q] * held + index
        spread = spread_ref[component]
        retard = 1.0 / jnp.full((rows, LANES), retard_ref[component], jnp.float32)
        retard = jnp.concatenate([retard] * (cols // LANES), axis=1)
        change = (
            (down_plus + spread) * from_lower_row(value)
            + (weight_minus[0] + spread) * from_upper_row(value)
            + (side_plus + spread) * from_lower_col(value, column(low_side, low_at))
            + (weight_minus[1] + spread) * from_upper_col(value, column(high_side, high_at))
            - (centre + 4.0 * spread) * value
        )
        value = value + change * retard
        for group in range(groups):
            offset_ref[group, at * TILE : (at + 1) * TILE, :] = value[
                group * TILE : (group + 1) * TILE
            ]

    for group in range(groups):
        offset = product(first_ref, [offset_ref[group]])
        offset_ref[group] = offset
        species_ref[group] = offset

    def plain_step(_, carry):
        for group in range(groups):
            species = species_ref[group]
            species_ref[group] = offset_ref[group] + product(both_ref, [species, jnp.tanh(species)])
        return carry

    lax.fori_loop(0, NEWT - 1, plain_step, 0, unroll=True)
    plain_ref[...] = species_ref[...]
    ratio = jnp.concatenate([ratio_ref[...]] * (cols // LANES), axis=1)

    def stiff_step(_, carry):
        for group in range(groups):
            species = species_ref[group]
            reaction = jnp.tanh(species) + ratio * jnp.tanh(species + species)
            species_ref[group] = offset_ref[group] + product(both_ref, [species, reaction])
        return carry

    lax.fori_loop(0, STIFF, stiff_step, 0, unroll=True)
    if is_first:
        for rank, value_ref in zip(ranks, value_refs):
            spot = pl.ds(pl.multiple_of(rank * block, TILE), block)
            stiff_ref[spot, :] = value_ref[held * rows : held * rows + block, :]
    for group in range(groups):
        spot = slice(group * TILE, (group + 1) * TILE)
        stiff = stiff_ref[spot, :] > 0.0
        for at in range(components):
            lane = slice(at * TILE, (at + 1) * TILE)
            start = at % held * rows + group * TILE
            out_refs[at // held][start : start + TILE, :] = jnp.where(
                stiff, species_ref[group, lane, :], plain_ref[group, lane, :]
            )
    if with_rim:
        edges = [ref[i * rows : (i + 1) * rows, :] for ref in out_refs for i in range(held)]
        columns = [value[:, :1] for value in edges] + [value[:, cols - 1 :] for value in edges]
        columns += [weight_plus[1][:, cols - 1 :], weight_minus[1][:, cols - 1 :]]
        rim_ref[...] = gather_columns(columns, rows)


def layer_step(values, stiff, low, high, shared, layer, with_rim):
    dispersion, retardation, face_rate, face_flag, ratio, first, both = shared
    pieces = len(values)
    rows, cols = face_rate.shape[1:]
    groups = rows // TILE
    stacked = ratio.shape[0]
    components = stacked // TILE
    scalar = pl.BlockSpec(memory_space=pltpu.SMEM)
    plane = jax.ShapeDtypeStruct((components // pieces * rows, cols), jnp.float32)
    out_shape = [plane] * pieces
    if with_rim:
        out_shape.append(jax.ShapeDtypeStruct((rows, LANES), jnp.float32))
    if stiff is None:
        out_shape.append(jax.ShapeDtypeStruct((rows, cols), jnp.float32))
    field = pltpu.VMEM((groups, stacked, cols), jnp.float32)
    cells = rows * cols
    operands = [dispersion, retardation, *values, low, high, face_rate, face_flag]
    operands += [ratio, first, both]
    if stiff is not None:
        operands.append(stiff)
    results = pl.pallas_call(
        functools.partial(step_kernel, pieces, layer, stiff is None, with_rim),
        out_shape=out_shape,
        in_specs=[scalar, scalar] + [whole_spec()] * (len(operands) - 2),
        out_specs=[whole_spec()] * len(out_shape),
        scratch_shapes=[field, field, field],
        compiler_params=pltpu.CompilerParams(vmem_limit_bytes=VMEM_LIMIT),
        cost_estimate=pl.CostEstimate(flops=0, bytes_accessed=0, transcendentals=0),
        name="layer_step",
    )(*operands)
    values, results = results[:pieces], results[pieces:]
    rims = results[0] if with_rim else None
    return values, (results[-1] if stiff is None else stiff), rims


def by_layers(
    concentration,
    face_rate,
    face_flag,
    retardation,
    dispersion,
    mixing,
    mixing_inverse,
    affinity,
    mineral,
    stiff_mask,
):
    ranks = lax.axis_size("comp")
    me = lax.axis_index("comp")
    planes, rows, cols = concentration.shape
    held = planes // NZ
    layers = NZ // ranks

    def send(value, by):
        return lax.ppermute(value, "comp", [(i, i ^ by) for i in range(ranks)]) if by else value

    def send_all(parts):
        return [send(part, pair(q, ranks)) for q, part in enumerate(parts)]

    messages = pack(concentration, stiff_mask, 0, ranks, ())
    arrived = [send_all(messages)]
    if layers > 1:
        edges = plane_edges(concentration, face_rate, face_flag, messages[:1])
        sides = (paired(edges, 0), paired(edges, 1))
    for layer in range(1, layers):
        messages = pack(concentration, stiff_mask, layer, ranks, sides)
        messages, arrived[-1] = lax.optimization_barrier((messages, arrived[-1]))
        arrived.append(send_all(messages))

    first, both, ratio = spread_parameters(ranks, mixing, mixing_inverse, affinity, mineral, messages[0]
    )
    shared = (dispersion, retardation, face_rate, face_flag, ratio, first, both)

    result = jnp.zeros((held, NZ, rows, cols), jnp.float32)
    for layer in range(layers):
        values, stiff = arrived[layer], None
        rims = None if layer else edges_of(values, face_rate, face_flag, messages[0])
        for step in range(STEPS):
            if rims is None:
                low, high = sides
            else:
                low, high = paired(rims, 0), paired(rims, 1)
            values, stiff, rims = layer_step(
                values, stiff, low, high, shared, layer, step < STEPS - 1
            )
        for q, piece in enumerate(send_all(values)):
            result = lax.dynamic_update_slice(
                result,
                piece.reshape(held, 1, rows, cols),
                (0, (me ^ pair(q, ranks)) * layers + layer, 0, 0),
            )
    return result.reshape(planes, rows, cols)


def shards(concentration, face_rate, face_flag, *parameters):
    ranks = lax.axis_size("comp")
    planes, rows, cols = concentration.shape
    whole = NZ % ranks == 0 and planes % NZ == 0 and ranks & (ranks - 1) == 0
    narrow = 2 * max(NC, planes) + 2 <= LANES
    even = rows % (ranks * TILE) == 0 and cols % LANES == 0
    plan = by_layers if whole and narrow and even else by_rows
    return plan(concentration, face_rate, face_flag, *parameters)


def solution(mesh):
    in_specs = (
        P(("real", "comp"), None, "space"),
        P(None, "real", "space"),
        P(None, "real", "space"),
        P(),
        P(),
        P(),
        P(),
        P(),
        P(),
        P(None, ("real", "comp"), "space"),
    )
    out_specs = P(("real", "comp"), None, "space")
    return jax.shard_map(shards, mesh=mesh, in_specs=in_specs, out_specs=out_specs, check_vma=False)
```

```python
import functools

import jax
import jax.numpy as jnp
from jax import lax
from jax.experimental import pallas as pl
from jax.experimental.pallas import tpu as pltpu
from jax.sharding import PartitionSpec as P

NC = 16
NZ = 8
STEPS = 2
NEWT = 4
STIFF = 4


highest = lax.Precision.HIGHEST


def shifted(shard, axis, by):
    devices = lax.axis_size(axis)
    pairs = [(i, i + by) for i in range(devices) if 0 <= i + by < devices]
    return lax.ppermute(shard, axis, pairs)


def extended(block, sides, width):
    for axis, dim in sides:
        count = lax.axis_size(axis)
        forward = [(i, i + 1) for i in range(count - 1)]
        backward = [(target, source) for source, target in forward]
        low = lax.ppermute(
            lax.slice_in_dim(block, block.shape[dim] - width, None, axis=dim), axis, forward
        )
        high = lax.ppermute(lax.slice_in_dim(block, 0, width, axis=dim), axis, backward)
        block = jnp.concatenate([low, block, high], axis=dim)
    return block


def shift_down(values, axis_index):
    size_along = values.shape[axis_index]
    zero_row = jnp.zeros_like(lax.slice_in_dim(values, 0, 1, axis=axis_index))
    kept = lax.slice_in_dim(values, 0, size_along - 1, axis=axis_index)
    return jnp.concatenate([zero_row, kept], axis=axis_index)


def face_weights(face_rate, face_flag):
    flag_values = face_flag.astype(jnp.float32)
    weight_plus = face_rate * flag_values
    weight_minus = face_rate * (1.0 - flag_values)
    return (weight_plus, weight_minus)


def advance(
    values, lower_row, upper_row, lower_col, upper_col, coefficients, retard_planes, spread_planes
):
    divergence = (
        coefficients[0] * lower_row
        + coefficients[1] * upper_row
        + coefficients[2] * lower_col
        + coefficients[3] * upper_col
        - coefficients[4] * values
    )
    laplace = lower_row + upper_row + lower_col + upper_col - 4.0 * values
    return values + (divergence + spread_planes * laplace) / retard_planes


def residual_of(species, target, mixing, affinity, mineral, stiff):
    total = jnp.dot(
        mixing, species, precision=highest, preferred_element_type=jnp.float32
    ) + affinity[:, None] * jnp.tanh(species)
    if stiff:
        total = total + mineral[:, None] * jnp.tanh(2.0 * species)
    return total - target


def newton_steps(species, target, repeats, stiff, mixing, mixing_inverse, affinity, mineral):
    for iteration in range(repeats):
        update = residual_of(species, target, mixing, affinity, mineral, stiff)
        species = species - jnp.dot(
            mixing_inverse, update, precision=highest, preferred_element_type=jnp.float32
        )
    return species


def speciate(cell_block, stiff_mask, mixing, mixing_inverse, affinity, mineral):
    target = cell_block.reshape(NC, -1)
    flat_mask = stiff_mask.reshape(-1) > 0
    species = jnp.zeros_like(target)
    species = newton_steps(species, target, NEWT, False, mixing, mixing_inverse, affinity, mineral)
    stiffer = newton_steps(species, target, STIFF, True, mixing, mixing_inverse, affinity, mineral)
    species = jnp.where(flat_mask[None, :], stiffer, species)
    return species.reshape(cell_block.shape)


def by_rows(
    concentration,
    face_rate,
    face_flag,
    retardation,
    dispersion,
    mixing,
    mixing_inverse,
    affinity,
    mineral,
    stiff_mask,
):
    weight_plus, weight_minus = face_weights(face_rate, face_flag)
    rim_weights = jnp.stack([weight_plus[1, :, -1], weight_minus[1, :, -1]])
    left_rims = shifted(rim_weights, "space", 1)
    side_plus = jnp.concatenate([left_rims[0][:, None], weight_plus[1, :, :-1]], axis=1)
    side_minus = jnp.concatenate([left_rims[1][:, None], weight_minus[1, :, :-1]], axis=1)
    down_plus = shift_down(weight_plus[0], 0)
    down_minus = shift_down(weight_minus[0], 0)
    centre = down_minus + weight_plus[0] + side_minus + weight_plus[1]
    coefficients = jnp.stack([down_plus, weight_minus[0], side_plus, weight_minus[1], centre])
    retard_all = jnp.repeat(retardation, NZ)
    spread_all = jnp.repeat(dispersion, NZ)
    rows_held = stiff_mask.shape[1]
    row_start = lax.axis_index("comp") * rows_held
    cell_coefficients = lax.dynamic_slice_in_dim(coefficients, row_start, rows_held, 1)
    retard_planes = retard_all[:, None, None]
    spread_planes = spread_all[:, None, None]
    cell_block = lax.all_to_all(concentration, "comp", split_axis=1, concat_axis=0, tiled=True)
    for step_index in range(STEPS):
        padded = extended(cell_block, (("comp", 1), ("space", 2)), 1)
        cell_block = advance(
            cell_block,
            padded[:, :-2, 1:-1],
            padded[:, 2:, 1:-1],
            padded[:, 1:-1, :-2],
            padded[:, 1:-1, 2:],
            cell_coefficients,
            retard_planes,
            spread_planes,
        )
        cell_block = speciate(cell_block, stiff_mask, mixing, mixing_inverse, affinity, mineral)
    return lax.all_to_all(cell_block, "comp", split_axis=0, concat_axis=1, tiled=True)


TILE = 8
LANES = 128
VMEM_LIMIT = 24 * 1024 * 1024
MOST_VMEM = 60 * 1024 * 1024


def whole_spec():
    return pl.BlockSpec(memory_space=pltpu.VMEM)


def any_spec():
    return pl.BlockSpec(memory_space=pl.ANY)


def hbm_spec():
    return pl.BlockSpec(memory_space=pltpu.HBM)


def pair(q, ranks):
    return (ranks - q) % ranks


def paired(value, first):
    low = range(first, lax.axis_size("space") - 1, 2)
    return lax.ppermute(value, "space", [(i, i + 1) for i in low] + [(i + 1, i) for i in low])


def by_side(even_ref, odd_ref):
    upward = lax.rem(lax.axis_index("space"), 2) == 0
    even, odd = even_ref[...], odd_ref[...]
    return jnp.where(upward, odd, even), jnp.where(upward, even, odd)


def split(value):
    high = value.astype(jnp.bfloat16)
    return high, (value - high.astype(jnp.float32)).astype(jnp.bfloat16)


def gather_columns(columns, rows):
    lane_at = lax.broadcasted_iota(jnp.int32, (rows, LANES), 1)
    gathered = jnp.zeros((rows, LANES), jnp.float32)
    for lane, column in enumerate(columns):
        gathered = jnp.where(lane_at == lane, jnp.broadcast_to(column, (rows, LANES)), gathered)
    return gathered


def bands(rows, cols):
    return -(-rows * LANES // (TILE * cols)) * TILE


def band_spots(rows, cols):
    wide = cols // LANES
    return [
        (group, group // wide * TILE, group % wide * LANES) for group in range(rows // TILE)
    ]


def pack_kernel(layer, plane_ref, mask_ref, *refs):
    if layer:
        (low_ref, high_ref), refs = refs[:2], refs[2:]
    out_refs, (part_ref, mask_part, mask_sems, in_sems, out_sems) = refs[:-5], refs[-5:]
    ranks = len(out_refs)
    planes, rows, cols = plane_ref.shape
    levels, block, _ = mask_ref.shape
    held = planes // levels
    me = lax.axis_index("comp")
    copies = []
    order = [*range(1, ranks), 0]

    def start(source, target, sem):
        copies.append(pltpu.make_async_copy(source, target, sem))
        copies[-1].start()

    for q in order:
        at = jnp.bitwise_xor(me, pair(q, ranks)) * (levels // ranks) + layer
        for index in range(held):
            spot = pl.ds(index * rows, rows)
            start(plane_ref.at[index * levels + at], part_ref.at[q, spot], in_sems.at[len(copies)])
        start(mask_ref.at[at], mask_part.at[q], mask_sems.at[q])
    arrivals = list(copies)
    copies.clear()
    if layer:
        lane_at = lax.broadcasted_iota(jnp.int32, (rows, LANES), 1)
        low_side, high_side = by_side(low_ref, high_ref)
        sides = jnp.where(lane_at < planes, high_side, low_side)
        for group, row, lane in band_spots(rows, cols):
            row += held * rows + block
            for q in order:
                part_ref[q, row : row + TILE, lane : lane + LANES] = sides[
                    group * TILE : (group + 1) * TILE
                ]
    for position, q in enumerate(order):
        for copy in arrivals[position * (held + 1) : (position + 1) * (held + 1)]:
            copy.wait()
        part_ref[q, held * rows : held * rows + block, :] = mask_part[q].astype(jnp.float32)
        start(part_ref.at[q], out_refs[q], out_sems.at[q])
    for copy in copies:
        copy.wait()


def pack(concentration, stiff_mask, layer, ranks, sides):
    planes, rows, cols = concentration.shape
    held = planes // NZ
    block = stiff_mask.shape[1]
    size = held * rows + block + (bands(rows, cols) if layer else 0)
    results = pl.pallas_call(
        functools.partial(pack_kernel, layer),
        out_shape=[jax.ShapeDtypeStruct((size, cols), jnp.float32)] * ranks,
        in_specs=[hbm_spec()] * 2 + [whole_spec()] * len(sides),
        out_specs=[any_spec()] * ranks,
        scratch_shapes=[
            pltpu.VMEM((ranks, size, cols), jnp.float32),
            pltpu.VMEM((ranks, block, cols), jnp.int32),
            pltpu.SemaphoreType.DMA((ranks,)),
            pltpu.SemaphoreType.DMA((ranks * (held + 1),)),
            pltpu.SemaphoreType.DMA((ranks,)),
        ],
        compiler_params=pltpu.CompilerParams(vmem_limit_bytes=VMEM_LIMIT if layer else MOST_VMEM),
        cost_estimate=pl.CostEstimate(flops=0, bytes_accessed=0, transcendentals=0),
        name="pack",
    )(concentration, stiff_mask, *sides)
    return list(results)


def plane_edges_kernel(first_ref, last_ref, rate_ref, flag_ref, *refs):
    planes, rows, _ = first_ref.shape
    weight_plus, weight_minus = face_weights(rate_ref[1], flag_ref[1])
    columns = [first_ref[plane][:, :1] for plane in range(planes)]
    columns += [last_ref[plane][:, LANES - 1 :] for plane in range(planes)]
    columns += [weight_plus[:, LANES - 1 :], weight_minus[:, LANES - 1 :]]
    refs[-1][...] = gather_columns(columns, rows)


def plane_edges(concentration, face_rate, face_flag, after):
    planes, rows, cols = concentration.shape
    last = cols // LANES - 1
    face = pl.BlockSpec((2, rows, LANES), lambda i: (0, 0, last))
    return pl.pallas_call(
        plane_edges_kernel,
        grid=(1,),
        out_shape=jax.ShapeDtypeStruct((rows, LANES), jnp.float32),
        in_specs=[
            pl.BlockSpec((planes, rows, LANES), lambda i: (0, 0, 0)),
            pl.BlockSpec((planes, rows, LANES), lambda i: (0, 0, last)),
            face,
            face,
        ]
        + [any_spec()] * len(after),
        out_specs=pl.BlockSpec((rows, LANES), lambda i: (0, 0)),
        compiler_params=pltpu.CompilerParams(vmem_limit_bytes=VMEM_LIMIT),
        cost_estimate=pl.CostEstimate(flops=0, bytes_accessed=0, transcendentals=0),
        name="plane_edges",
    )(concentration, concentration, face_rate, face_flag, *after)


def edges_kernel(held, *refs):
    half = (len(refs) - 4) // 2
    low_refs, high_refs, (rate_ref, flag_ref, _, out_ref) = refs[:half], refs[half:-4], refs[-4:]
    rows = rate_ref.shape[1]
    weight_plus, weight_minus = face_weights(rate_ref[1], flag_ref[1])
    spots = [slice(index * rows, (index + 1) * rows) for index in range(held)]
    columns = [ref[spot, :][:, :1] for ref in low_refs for spot in spots]
    columns += [ref[spot, :][:, LANES - 1 :] for ref in high_refs for spot in spots]
    columns += [weight_plus[:, LANES - 1 :], weight_minus[:, LANES - 1 :]]
    out_ref[...] = gather_columns(columns, rows)


def edges_of(values, face_rate, face_flag, after):
    rows, cols = face_rate.shape[1:]
    last = cols // LANES - 1
    size = values[0].shape[0]
    low = pl.BlockSpec((size, LANES), lambda i: (0, 0))
    high = pl.BlockSpec((size, LANES), lambda i: (0, last))
    face = pl.BlockSpec((2, rows, LANES), lambda i: (0, 0, last))
    return pl.pallas_call(
        functools.partial(edges_kernel, size // rows),
        grid=(1,),
        out_shape=jax.ShapeDtypeStruct((rows, LANES), jnp.float32),
        in_specs=[low] * len(values) + [high] * len(values) + [face, face, hbm_spec()],
        out_specs=pl.BlockSpec((rows, LANES), lambda i: (0, 0)),
        compiler_params=pltpu.CompilerParams(vmem_limit_bytes=VMEM_LIMIT),
        cost_estimate=pl.CostEstimate(flops=0, bytes_accessed=0, transcendentals=0),
        name="edges",
    )(*values, *values, face_rate, face_flag, after)


def spread_kernel(ranks, mixing_ref, inverse_ref, affinity_ref, mineral_ref, *refs):
    _, first_ref, both_ref, ratio_ref = refs
    components = mixing_ref.shape[0]
    stacked = components * TILE
    held = components // ranks
    me = lax.axis_index("comp")

    def dot(left, right):
        return jnp.dot(left, right, precision=highest, preferred_element_type=jnp.float32)

    def pick(shape, stacked_dim):
        at = lax.broadcasted_iota(jnp.int32, shape, stacked_dim) // TILE
        component = jnp.bitwise_xor(me, pair(at // held, ranks)) * held + lax.rem(at, held)
        held_at = lax.broadcasted_iota(jnp.int32, shape, 1 - stacked_dim)
        return jnp.where(component == held_at, 1.0, 0.0)

    rows = pick((stacked, components), 0)
    cols = pick((components, stacked), 1)
    inner = (stacked, stacked)
    same = lax.rem(lax.broadcasted_iota(jnp.int32, inner, 0), TILE) == lax.rem(
        lax.broadcasted_iota(jnp.int32, inner, 1), TILE
    )

    def spread(matrix):
        return jnp.where(same, dot(dot(rows, matrix), cols), 0.0)

    inverse = inverse_ref[...]
    square = (components, components)
    unit = jnp.where(
        lax.broadcasted_iota(jnp.int32, square, 0) == lax.broadcasted_iota(jnp.int32, square, 1),
        1.0,
        0.0,
    )
    blend = unit - dot(inverse, mixing_ref[...])
    high, low = split(spread(inverse))
    first_ref[...] = jnp.concatenate([high, low, high], axis=1)
    high, low = split(
        jnp.concatenate([spread(blend), spread(-inverse * affinity_ref[...])], axis=1)
    )
    both_ref[...] = jnp.concatenate([high, low, high], axis=1)
    ratio = jnp.sum(rows * (mineral_ref[...] / affinity_ref[...]), axis=1, keepdims=True)
    ratio_ref[...] = jnp.broadcast_to(ratio, (stacked, LANES))


def spread_parameters(ranks, mixing, mixing_inverse, affinity, mineral, after):
    components = mixing.shape[0]
    stacked = components * TILE
    return pl.pallas_call(
        functools.partial(spread_kernel, ranks),
        out_shape=[
            jax.ShapeDtypeStruct((stacked, 3 * stacked), jnp.bfloat16),
            jax.ShapeDtypeStruct((stacked, 6 * stacked), jnp.bfloat16),
            jax.ShapeDtypeStruct((stacked, LANES), jnp.float32),
        ],
        in_specs=[whole_spec()] * 4 + [any_spec()],
        out_specs=[whole_spec()] * 3,
        compiler_params=pltpu.CompilerParams(vmem_limit_bytes=VMEM_LIMIT),
        cost_estimate=pl.CostEstimate(flops=0, bytes_accessed=0, transcendentals=0),
        name="spread_parameters",
    )(mixing, mixing_inverse, affinity.reshape(1, -1), mineral.reshape(1, -1), after)


def step_kernel(pieces, layer, is_first, with_rim, spread_ref, retard_ref, *refs):
    value_refs, refs = refs[:pieces], refs[pieces:]
    (low_ref, high_ref, rate_ref, flag_ref, ratio_ref, first_ref, both_ref), refs = (
        refs[:7],
        refs[7:],
    )
    if not is_first:
        stiff_ref, refs = refs[0], refs[1:]
    out_refs, refs = refs[:pieces], refs[pieces:]
    if with_rim:
        rim_ref, refs = refs[0], refs[1:]
    if is_first:
        stiff_ref, refs = refs[0], refs[1:]
    offset_ref, species_ref, plain_ref = refs
    groups, stacked, cols = species_ref.shape
    rows = groups * TILE
    components = stacked // TILE
    held = components // pieces
    me = lax.axis_index("comp")
    ranks = [jnp.bitwise_xor(me, pair(q, pieces)) for q in range(pieces)]
    row_at = lax.broadcasted_iota(jnp.int32, (rows, cols), 0)
    col_at = lax.broadcasted_iota(jnp.int32, (rows, cols), 1)

    def product(weights, parts):
        highs, lows = zip(*[split(part) for part in parts])
        operand = jnp.concatenate(highs + highs + lows, axis=0)
        return jnp.dot(weights[...], operand, preferred_element_type=jnp.float32)

    weight_plus, weight_minus = face_weights(rate_ref[...], flag_ref[...])

    def column(side, at):
        return jnp.broadcast_to(side[:, at : at + 1], (rows, cols))

    def from_lower_row(value):
        return jnp.where(row_at == 0, 0.0, pltpu.roll(value, 1, 0))

    def from_upper_row(value):
        return jnp.where(row_at == rows - 1, 0.0, pltpu.roll(value, rows - 1, 0))

    def from_lower_col(value, edge):
        return jnp.where(col_at == 0, edge, pltpu.roll(value, 1, 1))

    def from_upper_col(value, edge):
        return jnp.where(col_at == cols - 1, edge, pltpu.roll(value, cols - 1, 1))

    block = rows // pieces
    if is_first and layer:
        sides, rim_at = [], 2 * held * NZ
        turn = LANES - (me * (NZ // pieces) + layer)
        for value_ref in value_refs:
            start = held * rows + block
            side = jnp.concatenate(
                [
                    value_ref[start + row : start + row + TILE, lane : lane + LANES]
                    for _, row, lane in band_spots(rows, cols)
                ]
            )
            if not sides:
                low_side = side
            side = pltpu.roll(side, turn, 1)
            for index in range(held):
                sides.append((side, (held + index) * NZ, side, index * NZ))
    else:
        low_side, high_side = by_side(low_ref, high_ref)
        rim_at = 2 * components
        sides = [(low_side, components + at, high_side, at) for at in range(components)]
    down_plus = from_lower_row(weight_plus[0])
    down_minus = from_lower_row(weight_minus[0])
    side_plus = from_lower_col(weight_plus[1], column(low_side, rim_at))
    side_minus = from_lower_col(weight_minus[1], column(low_side, rim_at + 1))
    centre = down_minus + weight_plus[0] + side_minus + weight_plus[1]
    for at, (low_side, low_at, high_side, high_at) in enumerate(sides):
        q, index = divmod(at, held)
        value = value_refs[q][index * rows : (index + 1) * rows, :]
        component = ranks[q] * held + index
        spread = spread_ref[component]
        retard = 1.0 / jnp.full((rows, LANES), retard_ref[component], jnp.float32)
        retard = jnp.concatenate([retard] * (cols // LANES), axis=1)
        change = (
            (down_plus + spread) * from_lower_row(value)
            + (weight_minus[0] + spread) * from_upper_row(value)
            + (side_plus + spread) * from_lower_col(value, column(low_side, low_at))
            + (weight_minus[1] + spread) * from_upper_col(value, column(high_side, high_at))
            - (centre + 4.0 * spread) * value
        )
        value = value + change * retard
        for group in range(groups):
            offset_ref[group, at * TILE : (at + 1) * TILE, :] = value[
                group * TILE : (group + 1) * TILE
            ]

    for group in range(groups):
        offset = product(first_ref, [offset_ref[group]])
        offset_ref[group] = offset
        species_ref[group] = offset

    def plain_step(_, carry):
        for group in range(groups):
            species = species_ref[group]
            species_ref[group] = offset_ref[group] + product(both_ref, [species, jnp.tanh(species)])
        return carry

    lax.fori_loop(0, NEWT - 1, plain_step, 0, unroll=True)
    plain_ref[...] = species_ref[...]
    ratio = jnp.concatenate([ratio_ref[...]] * (cols // LANES), axis=1)

    def stiff_step(_, carry):
        for group in range(groups):
            species = species_ref[group]
            reaction = jnp.tanh(species) + ratio * jnp.tanh(species + species)
            species_ref[group] = offset_ref[group] + product(both_ref, [species, reaction])
        return carry

    lax.fori_loop(0, STIFF, stiff_step, 0, unroll=True)
    if is_first:
        for rank, value_ref in zip(ranks, value_refs):
            spot = pl.ds(pl.multiple_of(rank * block, TILE), block)
            stiff_ref[spot, :] = value_ref[held * rows : held * rows + block, :]
    for group in range(groups):
        spot = slice(group * TILE, (group + 1) * TILE)
        stiff = stiff_ref[spot, :] > 0.0
        for at in range(components):
            lane = slice(at * TILE, (at + 1) * TILE)
            start = at % held * rows + group * TILE
            out_refs[at // held][start : start + TILE, :] = jnp.where(
                stiff, species_ref[group, lane, :], plain_ref[group, lane, :]
            )
    if with_rim:
        edges = [ref[i * rows : (i + 1) * rows, :] for ref in out_refs for i in range(held)]
        columns = [value[:, :1] for value in edges] + [value[:, cols - 1 :] for value in edges]
        columns += [weight_plus[1][:, cols - 1 :], weight_minus[1][:, cols - 1 :]]
        rim_ref[...] = gather_columns(columns, rows)


def layer_step(values, stiff, low, high, shared, layer, with_rim):
    dispersion, retardation, face_rate, face_flag, ratio, first, both = shared
    pieces = len(values)
    rows, cols = face_rate.shape[1:]
    groups = rows // TILE
    stacked = ratio.shape[0]
    components = stacked // TILE
    scalar = pl.BlockSpec(memory_space=pltpu.SMEM)
    plane = jax.ShapeDtypeStruct((components // pieces * rows, cols), jnp.float32)
    out_shape = [plane] * pieces
    if with_rim:
        out_shape.append(jax.ShapeDtypeStruct((rows, LANES), jnp.float32))
    if stiff is None:
        out_shape.append(jax.ShapeDtypeStruct((rows, cols), jnp.float32))
    field = pltpu.VMEM((groups, stacked, cols), jnp.float32)
    cells = rows * cols
    operands = [dispersion, retardation, *values, low, high, face_rate, face_flag]
    operands += [ratio, first, both]
    if stiff is not None:
        operands.append(stiff)
    results = pl.pallas_call(
        functools.partial(step_kernel, pieces, layer, stiff is None, with_rim),
        out_shape=out_shape,
        in_specs=[scalar, scalar] + [whole_spec()] * (len(operands) - 2),
        out_specs=[whole_spec()] * len(out_shape),
        scratch_shapes=[field, field, field],
        compiler_params=pltpu.CompilerParams(vmem_limit_bytes=VMEM_LIMIT),
        cost_estimate=pl.CostEstimate(flops=0, bytes_accessed=0, transcendentals=0),
        name="layer_step",
    )(*operands)
    values, results = results[:pieces], results[pieces:]
    rims = results[0] if with_rim else None
    return values, (results[-1] if stiff is None else stiff), rims


def by_layers(
    concentration,
    face_rate,
    face_flag,
    retardation,
    dispersion,
    mixing,
    mixing_inverse,
    affinity,
    mineral,
    stiff_mask,
):
    ranks = lax.axis_size("comp")
    me = lax.axis_index("comp")
    planes, rows, cols = concentration.shape
    held = planes // NZ
    layers = NZ // ranks

    def send(value, by):
        return lax.ppermute(value, "comp", [(i, i ^ by) for i in range(ranks)]) if by else value

    def send_all(parts):
        return [send(part, pair(q, ranks)) for q, part in enumerate(parts)]

    messages = pack(concentration, stiff_mask, 0, ranks, ())
    arrived = [send_all(messages)]
    if layers > 1:
        edges = plane_edges(concentration, face_rate, face_flag, messages[:1])
        sides = (paired(edges, 0), paired(edges, 1))
    for layer in range(1, layers):
        messages = pack(concentration, stiff_mask, layer, ranks, sides)
        messages, arrived[-1] = lax.optimization_barrier((messages, arrived[-1]))
        arrived.append(send_all(messages))

    first, both, ratio = spread_parameters(ranks, mixing, mixing_inverse, affinity, mineral, messages[0]
    )
    shared = (dispersion, retardation, face_rate, face_flag, ratio, first, both)

    result = jnp.zeros((held, NZ, rows, cols), jnp.float32)
    for layer in range(layers):
        values, stiff = arrived[layer], None
        rims = None if layer else edges_of(values, face_rate, face_flag, messages[0])
        for step in range(STEPS):
            if rims is None:
                low, high = sides
            else:
                low, high = paired(rims, 0), paired(rims, 1)
            values, stiff, rims = layer_step(
                values, stiff, low, high, shared, layer, step < STEPS - 1
            )
        for q, piece in reversed(list(enumerate(send_all(values)))):
            result = lax.dynamic_update_slice(
                result,
                piece.reshape(held, 1, rows, cols),
                (0, (me ^ pair(q, ranks)) * layers + layer, 0, 0),
            )
    return result.reshape(planes, rows, cols)


def shards(concentration, face_rate, face_flag, *parameters):
    ranks = lax.axis_size("comp")
    planes, rows, cols = concentration.shape
    whole = NZ % ranks == 0 and planes % NZ == 0 and ranks & (ranks - 1) == 0
    narrow = 2 * max(NC, planes) + 2 <= LANES
    even = rows % (ranks * TILE) == 0 and cols % LANES == 0
    plan = by_layers if whole and narrow and even else by_rows
    return plan(concentration, face_rate, face_flag, *parameters)


def solution(mesh):
    in_specs = (
        P(("real", "comp"), None, "space"),
        P(None, "real", "space"),
        P(None, "real", "space"),
        P(),
        P(),
        P(),
        P(),
        P(),
        P(),
        P(None, ("real", "comp"), "space"),
    )
    out_specs = P(("real", "comp"), None, "space")
    return jax.shard_map(shards, mesh=mesh, in_specs=in_specs, out_specs=out_specs, check_vma=False)
```

```python
import functools

import jax
import jax.numpy as jnp
from jax import lax
from jax.experimental import pallas as pl
from jax.experimental.pallas import tpu as pltpu
from jax.sharding import PartitionSpec as P

NC = 16
NZ = 8
STEPS = 2
NEWT = 4
STIFF = 4


highest = lax.Precision.HIGHEST


def shifted(shard, axis, by):
    devices = lax.axis_size(axis)
    pairs = [(i, i + by) for i in range(devices) if 0 <= i + by < devices]
    return lax.ppermute(shard, axis, pairs)


def extended(block, sides, width):
    for axis, dim in sides:
        count = lax.axis_size(axis)
        forward = [(i, i + 1) for i in range(count - 1)]
        backward = [(target, source) for source, target in forward]
        low = lax.ppermute(
            lax.slice_in_dim(block, block.shape[dim] - width, None, axis=dim), axis, forward
        )
        high = lax.ppermute(lax.slice_in_dim(block, 0, width, axis=dim), axis, backward)
        block = jnp.concatenate([low, block, high], axis=dim)
    return block


def shift_down(values, axis_index):
    size_along = values.shape[axis_index]
    zero_row = jnp.zeros_like(lax.slice_in_dim(values, 0, 1, axis=axis_index))
    kept = lax.slice_in_dim(values, 0, size_along - 1, axis=axis_index)
    return jnp.concatenate([zero_row, kept], axis=axis_index)


def face_weights(face_rate, face_flag):
    flag_values = face_flag.astype(jnp.float32)
    weight_plus = face_rate * flag_values
    weight_minus = face_rate * (1.0 - flag_values)
    return (weight_plus, weight_minus)


def advance(
    values, lower_row, upper_row, lower_col, upper_col, coefficients, retard_planes, spread_planes
):
    divergence = (
        coefficients[0] * lower_row
        + coefficients[1] * upper_row
        + coefficients[2] * lower_col
        + coefficients[3] * upper_col
        - coefficients[4] * values
    )
    laplace = lower_row + upper_row + lower_col + upper_col - 4.0 * values
    return values + (divergence + spread_planes * laplace) / retard_planes


def residual_of(species, target, mixing, affinity, mineral, stiff):
    total = jnp.dot(
        mixing, species, precision=highest, preferred_element_type=jnp.float32
    ) + affinity[:, None] * jnp.tanh(species)
    if stiff:
        total = total + mineral[:, None] * jnp.tanh(2.0 * species)
    return total - target


def newton_steps(species, target, repeats, stiff, mixing, mixing_inverse, affinity, mineral):
    for iteration in range(repeats):
        update = residual_of(species, target, mixing, affinity, mineral, stiff)
        species = species - jnp.dot(
            mixing_inverse, update, precision=highest, preferred_element_type=jnp.float32
        )
    return species


def speciate(cell_block, stiff_mask, mixing, mixing_inverse, affinity, mineral):
    target = cell_block.reshape(NC, -1)
    flat_mask = stiff_mask.reshape(-1) > 0
    species = jnp.zeros_like(target)
    species = newton_steps(species, target, NEWT, False, mixing, mixing_inverse, affinity, mineral)
    stiffer = newton_steps(species, target, STIFF, True, mixing, mixing_inverse, affinity, mineral)
    species = jnp.where(flat_mask[None, :], stiffer, species)
    return species.reshape(cell_block.shape)


def by_rows(
    concentration,
    face_rate,
    face_flag,
    retardation,
    dispersion,
    mixing,
    mixing_inverse,
    affinity,
    mineral,
    stiff_mask,
):
    weight_plus, weight_minus = face_weights(face_rate, face_flag)
    rim_weights = jnp.stack([weight_plus[1, :, -1], weight_minus[1, :, -1]])
    left_rims = shifted(rim_weights, "space", 1)
    side_plus = jnp.concatenate([left_rims[0][:, None], weight_plus[1, :, :-1]], axis=1)
    side_minus = jnp.concatenate([left_rims[1][:, None], weight_minus[1, :, :-1]], axis=1)
    down_plus = shift_down(weight_plus[0], 0)
    down_minus = shift_down(weight_minus[0], 0)
    centre = down_minus + weight_plus[0] + side_minus + weight_plus[1]
    coefficients = jnp.stack([down_plus, weight_minus[0], side_plus, weight_minus[1], centre])
    retard_all = jnp.repeat(retardation, NZ)
    spread_all = jnp.repeat(dispersion, NZ)
    rows_held = stiff_mask.shape[1]
    row_start = lax.axis_index("comp") * rows_held
    cell_coefficients = lax.dynamic_slice_in_dim(coefficients, row_start, rows_held, 1)
    retard_planes = retard_all[:, None, None]
    spread_planes = spread_all[:, None, None]
    cell_block = lax.all_to_all(concentration, "comp", split_axis=1, concat_axis=0, tiled=True)
    for step_index in range(STEPS):
        padded = extended(cell_block, (("comp", 1), ("space", 2)), 1)
        cell_block = advance(
            cell_block,
            padded[:, :-2, 1:-1],
            padded[:, 2:, 1:-1],
            padded[:, 1:-1, :-2],
            padded[:, 1:-1, 2:],
            cell_coefficients,
            retard_planes,
            spread_planes,
        )
        cell_block = speciate(cell_block, stiff_mask, mixing, mixing_inverse, affinity, mineral)
    return lax.all_to_all(cell_block, "comp", split_axis=0, concat_axis=1, tiled=True)


TILE = 8
LANES = 128
VMEM_LIMIT = 24 * 1024 * 1024
MOST_VMEM = 60 * 1024 * 1024


def whole_spec():
    return pl.BlockSpec(memory_space=pltpu.VMEM)


def any_spec():
    return pl.BlockSpec(memory_space=pl.ANY)


def hbm_spec():
    return pl.BlockSpec(memory_space=pltpu.HBM)


def pair(q, ranks):
    return (ranks - q) % ranks


def paired(value, first):
    low = range(first, lax.axis_size("space") - 1, 2)
    return lax.ppermute(value, "space", [(i, i + 1) for i in low] + [(i + 1, i) for i in low])


def by_side(even_ref, odd_ref):
    upward = lax.rem(lax.axis_index("space"), 2) == 0
    even, odd = even_ref[...], odd_ref[...]
    return jnp.where(upward, odd, even), jnp.where(upward, even, odd)


def split(value):
    high = value.astype(jnp.bfloat16)
    return high, (value - high.astype(jnp.float32)).astype(jnp.bfloat16)


def gather_columns(columns, rows):
    lane_at = lax.broadcasted_iota(jnp.int32, (rows, LANES), 1)
    gathered = jnp.zeros((rows, LANES), jnp.float32)
    for lane, column in enumerate(columns):
        gathered = jnp.where(lane_at == lane, jnp.broadcast_to(column, (rows, LANES)), gathered)
    return gathered


def bands(rows, cols):
    return -(-rows * LANES // (TILE * cols)) * TILE


def band_spots(rows, cols):
    wide = cols // LANES
    return [
        (group, group // wide * TILE, group % wide * LANES) for group in range(rows // TILE)
    ]


def pack_kernel(layer, ranks, order, plane_ref, mask_ref, *refs):
    if layer:
        (low_ref, high_ref), refs = refs[:2], refs[2:]
    out_refs, (part_ref, mask_part, mask_sems, in_sems, out_sems) = refs[:-5], refs[-5:]
    planes, rows, cols = plane_ref.shape
    levels, block, _ = mask_ref.shape
    held = planes // levels
    me = lax.axis_index("comp")
    copies = []

    def start(source, target, sem):
        copies.append(pltpu.make_async_copy(source, target, sem))
        copies[-1].start()

    for place, q in enumerate(order):
        at = jnp.bitwise_xor(me, pair(q, ranks)) * (levels // ranks) + layer
        for index in range(held):
            spot = pl.ds(index * rows, rows)
            start(plane_ref.at[index * levels + at], part_ref.at[place, spot], in_sems.at[len(copies)])
        start(mask_ref.at[at], mask_part.at[place], mask_sems.at[place])
    arrivals = list(copies)
    copies.clear()
    if layer:
        lane_at = lax.broadcasted_iota(jnp.int32, (rows, LANES), 1)
        low_side, high_side = by_side(low_ref, high_ref)
        sides = jnp.where(lane_at < planes, high_side, low_side)
        for group, row, lane in band_spots(rows, cols):
            row += held * rows + block
            for place in range(len(order)):
                part_ref[place, row : row + TILE, lane : lane + LANES] = sides[
                    group * TILE : (group + 1) * TILE
                ]
    for place, out_ref in enumerate(out_refs):
        for copy in arrivals[place * (held + 1) : (place + 1) * (held + 1)]:
            copy.wait()
        part_ref[place, held * rows : held * rows + block, :] = mask_part[place].astype(jnp.float32)
        start(part_ref.at[place], out_ref, out_sems.at[place])
    for copy in copies:
        copy.wait()


def pack(concentration, stiff_mask, layer, ranks, order, sides):
    planes, rows, cols = concentration.shape
    held = planes // NZ
    block = stiff_mask.shape[1]
    size = held * rows + block + (bands(rows, cols) if layer else 0)
    results = pl.pallas_call(
        functools.partial(pack_kernel, layer, ranks, order),
        out_shape=[jax.ShapeDtypeStruct((size, cols), jnp.float32)] * len(order),
        in_specs=[hbm_spec()] * 2 + [whole_spec()] * len(sides),
        out_specs=[any_spec()] * len(order),
        scratch_shapes=[
            pltpu.VMEM((len(order), size, cols), jnp.float32),
            pltpu.VMEM((len(order), block, cols), jnp.int32),
            pltpu.SemaphoreType.DMA((len(order),)),
            pltpu.SemaphoreType.DMA((len(order) * (held + 1),)),
            pltpu.SemaphoreType.DMA((len(order),)),
        ],
        compiler_params=pltpu.CompilerParams(vmem_limit_bytes=VMEM_LIMIT if layer else MOST_VMEM),
        cost_estimate=pl.CostEstimate(flops=0, bytes_accessed=0, transcendentals=0),
        name="pack",
    )(concentration, stiff_mask, *sides)
    return list(results)


def plane_edges_kernel(first_ref, last_ref, rate_ref, flag_ref, *refs):
    planes, rows, _ = first_ref.shape
    weight_plus, weight_minus = face_weights(rate_ref[1], flag_ref[1])
    columns = [first_ref[plane][:, :1] for plane in range(planes)]
    columns += [last_ref[plane][:, LANES - 1 :] for plane in range(planes)]
    columns += [weight_plus[:, LANES - 1 :], weight_minus[:, LANES - 1 :]]
    refs[-1][...] = gather_columns(columns, rows)


def plane_edges(concentration, face_rate, face_flag, after):
    planes, rows, cols = concentration.shape
    last = cols // LANES - 1
    face = pl.BlockSpec((2, rows, LANES), lambda i: (0, 0, last))
    return pl.pallas_call(
        plane_edges_kernel,
        grid=(1,),
        out_shape=jax.ShapeDtypeStruct((rows, LANES), jnp.float32),
        in_specs=[
            pl.BlockSpec((planes, rows, LANES), lambda i: (0, 0, 0)),
            pl.BlockSpec((planes, rows, LANES), lambda i: (0, 0, last)),
            face,
            face,
        ]
        + [any_spec()] * len(after),
        out_specs=pl.BlockSpec((rows, LANES), lambda i: (0, 0)),
        compiler_params=pltpu.CompilerParams(vmem_limit_bytes=VMEM_LIMIT),
        cost_estimate=pl.CostEstimate(flops=0, bytes_accessed=0, transcendentals=0),
        name="plane_edges",
    )(concentration, concentration, face_rate, face_flag, *after)


def edges_kernel(held, *refs):
    half = (len(refs) - 4) // 2
    low_refs, high_refs, (rate_ref, flag_ref, _, out_ref) = refs[:half], refs[half:-4], refs[-4:]
    rows = rate_ref.shape[1]
    weight_plus, weight_minus = face_weights(rate_ref[1], flag_ref[1])
    spots = [slice(index * rows, (index + 1) * rows) for index in range(held)]
    columns = [ref[spot, :][:, :1] for ref in low_refs for spot in spots]
    columns += [ref[spot, :][:, LANES - 1 :] for ref in high_refs for spot in spots]
    columns += [weight_plus[:, LANES - 1 :], weight_minus[:, LANES - 1 :]]
    out_ref[...] = gather_columns(columns, rows)


def edges_of(values, face_rate, face_flag, after):
    rows, cols = face_rate.shape[1:]
    last = cols // LANES - 1
    size = values[0].shape[0]
    low = pl.BlockSpec((size, LANES), lambda i: (0, 0))
    high = pl.BlockSpec((size, LANES), lambda i: (0, last))
    face = pl.BlockSpec((2, rows, LANES), lambda i: (0, 0, last))
    return pl.pallas_call(
        functools.partial(edges_kernel, size // rows),
        grid=(1,),
        out_shape=jax.ShapeDtypeStruct((rows, LANES), jnp.float32),
        in_specs=[low] * len(values) + [high] * len(values) + [face, face, hbm_spec()],
        out_specs=pl.BlockSpec((rows, LANES), lambda i: (0, 0)),
        compiler_params=pltpu.CompilerParams(vmem_limit_bytes=VMEM_LIMIT),
        cost_estimate=pl.CostEstimate(flops=0, bytes_accessed=0, transcendentals=0),
        name="edges",
    )(*values, *values, face_rate, face_flag, after)


def spread_kernel(ranks, mixing_ref, inverse_ref, affinity_ref, mineral_ref, *refs):
    _, first_ref, both_ref, ratio_ref = refs
    components = mixing_ref.shape[0]
    stacked = components * TILE
    held = components // ranks
    me = lax.axis_index("comp")

    def dot(left, right):
        return jnp.dot(left, right, precision=highest, preferred_element_type=jnp.float32)

    def pick(shape, stacked_dim):
        at = lax.broadcasted_iota(jnp.int32, shape, stacked_dim) // TILE
        component = jnp.bitwise_xor(me, pair(at // held, ranks)) * held + lax.rem(at, held)
        held_at = lax.broadcasted_iota(jnp.int32, shape, 1 - stacked_dim)
        return jnp.where(component == held_at, 1.0, 0.0)

    rows = pick((stacked, components), 0)
    cols = pick((components, stacked), 1)
    inner = (stacked, stacked)
    same = lax.rem(lax.broadcasted_iota(jnp.int32, inner, 0), TILE) == lax.rem(
        lax.broadcasted_iota(jnp.int32, inner, 1), TILE
    )

    def spread(matrix):
        return jnp.where(same, dot(dot(rows, matrix), cols), 0.0)

    inverse = inverse_ref[...]
    square = (components, components)
    unit = jnp.where(
        lax.broadcasted_iota(jnp.int32, square, 0) == lax.broadcasted_iota(jnp.int32, square, 1),
        1.0,
        0.0,
    )
    blend = unit - dot(inverse, mixing_ref[...])
    high, low = split(spread(inverse))
    first_ref[...] = jnp.concatenate([high, low, high], axis=1)
    high, low = split(
        jnp.concatenate([spread(blend), spread(-inverse * affinity_ref[...])], axis=1)
    )
    both_ref[...] = jnp.concatenate([high, low, high], axis=1)
    ratio = jnp.sum(rows * (mineral_ref[...] / affinity_ref[...]), axis=1, keepdims=True)
    ratio_ref[...] = jnp.broadcast_to(ratio, (stacked, LANES))


def spread_parameters(ranks, mixing, mixing_inverse, affinity, mineral, after):
    components = mixing.shape[0]
    stacked = components * TILE
    return pl.pallas_call(
        functools.partial(spread_kernel, ranks),
        out_shape=[
            jax.ShapeDtypeStruct((stacked, 3 * stacked), jnp.bfloat16),
            jax.ShapeDtypeStruct((stacked, 6 * stacked), jnp.bfloat16),
            jax.ShapeDtypeStruct((stacked, LANES), jnp.float32),
        ],
        in_specs=[whole_spec()] * 4 + [any_spec()],
        out_specs=[whole_spec()] * 3,
        compiler_params=pltpu.CompilerParams(vmem_limit_bytes=VMEM_LIMIT),
        cost_estimate=pl.CostEstimate(flops=0, bytes_accessed=0, transcendentals=0),
        name="spread_parameters",
    )(mixing, mixing_inverse, affinity.reshape(1, -1), mineral.reshape(1, -1), after)


def step_kernel(pieces, layer, is_first, with_rim, spread_ref, retard_ref, *refs):
    value_refs, refs = refs[:pieces], refs[pieces:]
    (low_ref, high_ref, rate_ref, flag_ref, ratio_ref, first_ref, both_ref), refs = (
        refs[:7],
        refs[7:],
    )
    if not is_first:
        stiff_ref, refs = refs[0], refs[1:]
    out_refs, refs = refs[:pieces], refs[pieces:]
    if with_rim:
        rim_ref, refs = refs[0], refs[1:]
    if is_first:
        stiff_ref, refs = refs[0], refs[1:]
    offset_ref, species_ref, plain_ref = refs
    groups, stacked, cols = species_ref.shape
    rows = groups * TILE
    components = stacked // TILE
    held = components // pieces
    me = lax.axis_index("comp")
    ranks = [jnp.bitwise_xor(me, pair(q, pieces)) for q in range(pieces)]
    row_at = lax.broadcasted_iota(jnp.int32, (rows, cols), 0)
    col_at = lax.broadcasted_iota(jnp.int32, (rows, cols), 1)

    def product(weights, parts):
        highs, lows = zip(*[split(part) for part in parts])
        operand = jnp.concatenate(highs + highs + lows, axis=0)
        return jnp.dot(weights[...], operand, preferred_element_type=jnp.float32)

    weight_plus, weight_minus = face_weights(rate_ref[...], flag_ref[...])

    def column(side, at):
        return jnp.broadcast_to(side[:, at : at + 1], (rows, cols))

    def from_lower_row(value):
        return jnp.where(row_at == 0, 0.0, pltpu.roll(value, 1, 0))

    def from_upper_row(value):
        return jnp.where(row_at == rows - 1, 0.0, pltpu.roll(value, rows - 1, 0))

    def from_lower_col(value, edge):
        return jnp.where(col_at == 0, edge, pltpu.roll(value, 1, 1))

    def from_upper_col(value, edge):
        return jnp.where(col_at == cols - 1, edge, pltpu.roll(value, cols - 1, 1))

    block = rows // pieces
    if is_first and layer:
        sides, rim_at = [], 2 * held * NZ
        turn = LANES - (me * (NZ // pieces) + layer)
        for value_ref in value_refs:
            start = held * rows + block
            side = jnp.concatenate(
                [
                    value_ref[start + row : start + row + TILE, lane : lane + LANES]
                    for _, row, lane in band_spots(rows, cols)
                ]
            )
            if not sides:
                low_side = side
            side = pltpu.roll(side, turn, 1)
            for index in range(held):
                sides.append((side, (held + index) * NZ, side, index * NZ))
    else:
        low_side, high_side = by_side(low_ref, high_ref)
        rim_at = 2 * components
        sides = [(low_side, components + at, high_side, at) for at in range(components)]
    down_plus = from_lower_row(weight_plus[0])
    down_minus = from_lower_row(weight_minus[0])
    side_plus = from_lower_col(weight_plus[1], column(low_side, rim_at))
    side_minus = from_lower_col(weight_minus[1], column(low_side, rim_at + 1))
    centre = down_minus + weight_plus[0] + side_minus + weight_plus[1]
    for at, (low_side, low_at, high_side, high_at) in enumerate(sides):
        q, index = divmod(at, held)
        value = value_refs[q][index * rows : (index + 1) * rows, :]
        component = ranks[q] * held + index
        spread = spread_ref[component]
        retard = 1.0 / jnp.full((rows, LANES), retard_ref[component], jnp.float32)
        retard = jnp.concatenate([retard] * (cols // LANES), axis=1)
        change = (
            (down_plus + spread) * from_lower_row(value)
            + (weight_minus[0] + spread) * from_upper_row(value)
            + (side_plus + spread) * from_lower_col(value, column(low_side, low_at))
            + (weight_minus[1] + spread) * from_upper_col(value, column(high_side, high_at))
            - (centre + 4.0 * spread) * value
        )
        value = value + change * retard
        for group in range(groups):
            offset_ref[group, at * TILE : (at + 1) * TILE, :] = value[
                group * TILE : (group + 1) * TILE
            ]

    for group in range(groups):
        offset = product(first_ref, [offset_ref[group]])
        offset_ref[group] = offset
        species_ref[group] = offset

    def plain_step(_, carry):
        for group in range(groups):
            species = species_ref[group]
            species_ref[group] = offset_ref[group] + product(both_ref, [species, jnp.tanh(species)])
        return carry

    lax.fori_loop(0, NEWT - 1, plain_step, 0, unroll=True)
    plain_ref[...] = species_ref[...]
    ratio = jnp.concatenate([ratio_ref[...]] * (cols // LANES), axis=1)

    def stiff_step(_, carry):
        for group in range(groups):
            species = species_ref[group]
            reaction = jnp.tanh(species) + ratio * jnp.tanh(species + species)
            species_ref[group] = offset_ref[group] + product(both_ref, [species, reaction])
        return carry

    lax.fori_loop(0, STIFF, stiff_step, 0, unroll=True)
    if is_first:
        for rank, value_ref in zip(ranks, value_refs):
            spot = pl.ds(pl.multiple_of(rank * block, TILE), block)
            stiff_ref[spot, :] = value_ref[held * rows : held * rows + block, :]
    for group in range(groups):
        spot = slice(group * TILE, (group + 1) * TILE)
        stiff = stiff_ref[spot, :] > 0.0
        for at in range(components):
            lane = slice(at * TILE, (at + 1) * TILE)
            start = at % held * rows + group * TILE
            out_refs[at // held][start : start + TILE, :] = jnp.where(
                stiff, species_ref[group, lane, :], plain_ref[group, lane, :]
            )
    if with_rim:
        edges = [ref[i * rows : (i + 1) * rows, :] for ref in out_refs for i in range(held)]
        columns = [value[:, :1] for value in edges] + [value[:, cols - 1 :] for value in edges]
        columns += [weight_plus[1][:, cols - 1 :], weight_minus[1][:, cols - 1 :]]
        rim_ref[...] = gather_columns(columns, rows)


def layer_step(values, stiff, low, high, shared, layer, with_rim):
    dispersion, retardation, face_rate, face_flag, ratio, first, both = shared
    pieces = len(values)
    rows, cols = face_rate.shape[1:]
    groups = rows // TILE
    stacked = ratio.shape[0]
    components = stacked // TILE
    scalar = pl.BlockSpec(memory_space=pltpu.SMEM)
    plane = jax.ShapeDtypeStruct((components // pieces * rows, cols), jnp.float32)
    out_shape = [plane] * pieces
    if with_rim:
        out_shape.append(jax.ShapeDtypeStruct((rows, LANES), jnp.float32))
    if stiff is None:
        out_shape.append(jax.ShapeDtypeStruct((rows, cols), jnp.float32))
    field = pltpu.VMEM((groups, stacked, cols), jnp.float32)
    cells = rows * cols
    operands = [dispersion, retardation, *values, low, high, face_rate, face_flag]
    operands += [ratio, first, both]
    if stiff is not None:
        operands.append(stiff)
    results = pl.pallas_call(
        functools.partial(step_kernel, pieces, layer, stiff is None, with_rim),
        out_shape=out_shape,
        in_specs=[scalar, scalar] + [whole_spec()] * (len(operands) - 2),
        out_specs=[whole_spec()] * len(out_shape),
        scratch_shapes=[field, field, field],
        compiler_params=pltpu.CompilerParams(vmem_limit_bytes=VMEM_LIMIT),
        cost_estimate=pl.CostEstimate(flops=0, bytes_accessed=0, transcendentals=0),
        name="layer_step",
    )(*operands)
    values, results = results[:pieces], results[pieces:]
    rims = results[0] if with_rim else None
    return values, (results[-1] if stiff is None else stiff), rims


def by_layers(
    concentration,
    face_rate,
    face_flag,
    retardation,
    dispersion,
    mixing,
    mixing_inverse,
    affinity,
    mineral,
    stiff_mask,
):
    ranks = lax.axis_size("comp")
    me = lax.axis_index("comp")
    planes, rows, cols = concentration.shape
    held = planes // NZ
    layers = NZ // ranks

    def send(value, by):
        return lax.ppermute(value, "comp", [(i, i ^ by) for i in range(ranks)]) if by else value

    def send_all(parts):
        return [send(part, pair(q, ranks)) for q, part in enumerate(parts)]

    far, near = list(range(1, ranks - 1)), list(range(1, ranks))[-1:] + [0]
    parts = [pack(concentration, stiff_mask, 0, ranks, part, ()) for part in (far, near) if part]
    messages = [message for _, message in sorted(zip(far + near, sum(parts, [])), key=lambda x: x[0])]
    arrived = [send_all(messages)]
    if layers > 1:
        edges = plane_edges(concentration, face_rate, face_flag, messages[:1])
        sides = (paired(edges, 0), paired(edges, 1))
    for layer in range(1, layers):
        order = list(range(ranks))
        messages = pack(concentration, stiff_mask, layer, ranks, order, sides)
        messages, arrived[-1] = lax.optimization_barrier((messages, arrived[-1]))
        arrived.append(send_all(messages))

    first, both, ratio = spread_parameters(ranks, mixing, mixing_inverse, affinity, mineral, messages[0]
    )
    shared = (dispersion, retardation, face_rate, face_flag, ratio, first, both)

    result = jnp.zeros((held, NZ, rows, cols), jnp.float32)
    for layer in range(layers):
        values, stiff = arrived[layer], None
        rims = None if layer else edges_of(values, face_rate, face_flag, messages[0])
        for step in range(STEPS):
            if rims is None:
                low, high = sides
            else:
                low, high = paired(rims, 0), paired(rims, 1)
            values, stiff, rims = layer_step(
                values, stiff, low, high, shared, layer, step < STEPS - 1
            )
        for q, piece in reversed(list(enumerate(send_all(values)))):
            result = lax.dynamic_update_slice(
                result,
                piece.reshape(held, 1, rows, cols),
                (0, (me ^ pair(q, ranks)) * layers + layer, 0, 0),
            )
    return result.reshape(planes, rows, cols)


def shards(concentration, face_rate, face_flag, *parameters):
    ranks = lax.axis_size("comp")
    planes, rows, cols = concentration.shape
    whole = NZ % ranks == 0 and planes % NZ == 0 and ranks & (ranks - 1) == 0
    narrow = 2 * max(NC, planes) + 2 <= LANES
    even = rows % (ranks * TILE) == 0 and cols % LANES == 0
    plan = by_layers if whole and narrow and even else by_rows
    return plan(concentration, face_rate, face_flag, *parameters)


def solution(mesh):
    in_specs = (
        P(("real", "comp"), None, "space"),
        P(None, "real", "space"),
        P(None, "real", "space"),
        P(),
        P(),
        P(),
        P(),
        P(),
        P(),
        P(None, ("real", "comp"), "space"),
    )
    out_specs = P(("real", "comp"), None, "space")
    return jax.shard_map(shards, mesh=mesh, in_specs=in_specs, out_specs=out_specs, check_vma=False)
```
